128 devices in a mesh: section: 16 (over y_hi, x, core), ctx: 8 (over y_lo, z).
Axes of the slice: x: 4, y: 4 (y_hi: 2, y_lo: 2; y = y_hi * 2 + y_lo), z: 4, core: 2. Of those that a mesh axis runs over, the one named last changes fastest.
Arguments:
- section_input: bfloat16 [16, 2048, 5120], P('section', 'ctx'), may hold values from -60 to 60
- last_hidden: bfloat16 [2048, 5120], P('section'), may hold values from -60 to 60
- kv_gain: float32 [5120], replicated, may hold values from 0.25 to 1.75
- query_gain: float32 [16, 5120], P('section'), may hold values from 0.25 to 1.75
- w_key: bfloat16 [5120, 3072], P(None, 'ctx'), may hold values from -1 to 1
- w_value: bfloat16 [5120, 3072], P(None, 'ctx'), may hold values from -0.078125 to 0.078125
- w_query: bfloat16 [16, 5120, 3072], P('section', None, 'ctx'), may hold values from -30 to 30
- w_out: bfloat16 [16, 3072, 5120], P('section', None, 'ctx'), may hold values from -0.625 to 0.625
- segment_ids: int32 [2048], replicated, may hold values from 0 to 3, never falling along the last dimension, each value on 1 to 1024 neighbouring positions
Outputs:
- layer_output: bfloat16 [16, 2048, 5120], P('section', None, 'ctx')
The draws below stay inside these ranges and needn't reach their ends.
Inputs may be any that keep to these rules, and one draw needn't show every extreme that they name: `segment_ids`: documents are runs of equal ids that never fall; the longest holds exactly 1024 tokens.
All inputs are finite; a program needn't handle non-finite values.
Results may differ from the reference program's by a relative error of at most 0.005.
The reference program's roundings to bfloat16 on the way (of `kv_in`, `keys`, `values`, `q_in`, `queries`, `weights` and `context`) count: a program that leaves them out, or rounds other values in their place, can miss the bound.
Values may be sent and summed in bfloat16 or wider, within the bound.
No kernel may reach another device: no remote copies, remote signals or barrier semaphores. Data moves between devices by JAX's collectives and lax.ppermute only.
A program may use at most 128 MiB of HBM per device.

```python
import math
import jax
import jax.numpy as jnp
import numpy as np
from jax import lax

D = 5120
HEADS = 24
HD = 128
TOKENS = 2048
LAYERS = 16


def feature_scales(key):
    inner = jax.random.fold_in(key, 101)
    return jnp.exp(jax.random.uniform(inner, (D,), jnp.float32, math.log(0.3), math.log(3.0)))


def row_scales(key, count):
    return jnp.exp(jax.random.uniform(key, (count, 1), jnp.float32, math.log(0.3), math.log(3.0)))


def hidden_states(key):
    scales = feature_scales(key)
    first, second = jax.random.split(jax.random.fold_in(key, 103), 2)
    base = jax.random.truncated_normal(first, -6.0, 6.0, (TOKENS, D), jnp.float32)
    base = base * scales * row_scales(second, TOKENS)
    return base


def key_base(key):
    inner = jax.random.fold_in(key, 109)
    return jax.random.truncated_normal(inner, -6.0, 6.0, (D, HEADS * HD), jnp.float32) / math.sqrt(D)


def draw_last_hidden(key, part):
    return hidden_states(key).astype(jnp.bfloat16)


def draw_section_input(key, part):
    scales = feature_scales(key)
    first, second = jax.random.split(jax.random.fold_in(key, 107))
    fresh = jax.random.truncated_normal(first, -6.0, 6.0, (LAYERS, TOKENS, D), jnp.float32)
    fresh = fresh * scales * row_scales(second, LAYERS * TOKENS).reshape(LAYERS, TOKENS, 1)
    return fresh.astype(jnp.bfloat16)


def draw_w_key(key, part):
    return key_base(key).astype(jnp.bfloat16)


def draw_w_query(key, part):
    first = jax.random.fold_in(jax.random.fold_in(key, 113), 0)
    own = jax.random.truncated_normal(first, -6.0, 6.0, (LAYERS, D, HEADS * HD), jnp.float32) / math.sqrt(D)
    return own.astype(jnp.bfloat16)


def block_scale(own_key, dims, cuts, least, top_value):
    level = 1.0
    for axis_at, parts in cuts:
        draws = jax.random.uniform(jax.random.fold_in(jax.random.fold_in(own_key, 6), axis_at), (parts,), jnp.float32, least / len(cuts), top_value / len(cuts))
        level = level * jnp.repeat(jnp.exp(draws), dims[axis_at] // parts).reshape((-1,) + (1,) * (len(dims) - 1 - axis_at))
    return level


def length_profile(count, total, reach, slope):
    portions = [(1 << 20) // math.isqrt(grade ** slope) + 1 for grade in range(2, count + 1)]
    surplus, holding = total - reach - (count - 1), [1] * (count - 1)
    while surplus > 0:
        free = [i for i in range(count - 1) if holding[i] < reach]
        pool, budget = sum([portions[i] for i in free]), surplus
        for i in free:
            more = min(reach - holding[i], max(1, budget * portions[i] // pool), surplus)
            holding[i] = holding[i] + more
            surplus = surplus - more
    return np.array([reach] + holding)


def uneven_parts(rng, count, total, limit, skew):
    if count == 2:
        one = jax.random.randint(rng, (), max(1, total - limit), min(limit, total - 1) + 1)
        return jnp.stack([one, total - one])
    sizes = jnp.asarray(length_profile(count, total, limit, skew), jnp.int32)
    couples = (count - 1) // 2
    source_of, receiver = sizes[1:1 + 2 * couples:2], sizes[2:2 + 2 * couples:2]
    margin = jnp.minimum(source_of - 1, limit - receiver)
    shifted = jax.random.randint(jax.random.fold_in(rng, 1), (couples,), 0, 1 << 20) % (margin + 1)
    sizes = sizes.at[1:1 + 2 * couples:2].set(source_of - shifted).at[2:2 + 2 * couples:2].set(receiver + shifted)
    return sizes[jax.random.permutation(jax.random.fold_in(rng, 2), count)]


def scatter_about(rng, shape, deviation, most, shards=(), held_as=jnp.bfloat16):
    entries = deviation * jax.random.normal(rng, shape, jnp.float32)
    if shards:
        entries = entries * block_scale(rng, shape, shards, -0.22, 0.18)
    return jnp.clip(entries, -most, most).astype(held_as)


def setup_inputs(seed: int = 0) -> dict:
    key_list = jax.random.split(jax.random.key(seed), 10)
    section_input = draw_section_input(jax.random.fold_in(key_list[9], 71), 0)
    last_hidden = draw_last_hidden(jax.random.fold_in(key_list[9], 71), 0)
    kv_gain = jnp.clip(1.0 + 0.15 * jax.random.normal(key_list[2], (D,), jnp.float32), 0.25, 1.75)
    query_gain = jnp.clip(1.0 + 0.15 * jax.random.normal(key_list[3], (LAYERS, D), jnp.float32), 0.25, 1.75)
    w_key = draw_w_key(jax.random.fold_in(key_list[9], 71), 0)
    w_value = scatter_about(key_list[5], (D, HEADS * HD), D ** -0.5, 0.078125, ((1, 8),))
    w_query = draw_w_query(jax.random.fold_in(key_list[9], 71), 0)
    w_out = scatter_about(key_list[7], (LAYERS, HEADS * HD, D), (2.5 / (HEADS * HD) ** 0.5), 0.625, ((0, 16), (2, 8)))
    segment_ids = jnp.searchsorted(jnp.cumsum(uneven_parts(key_list[8], 4, TOKENS, TOKENS // 2, 1)), jnp.arange(TOKENS), side="right").astype(jnp.int32)
    return {"section_input": section_input, "last_hidden": last_hidden, "kv_gain": kv_gain, "query_gain": query_gain, "w_key": w_key, "w_value": w_value, "w_query": w_query, "w_out": w_out, "segment_ids": segment_ids}


def rms_rows(rows, gain):
    full = rows.astype(jnp.float32)
    scaled = full * lax.rsqrt(lax.optimization_barrier(jnp.mean(full * full, axis=-1, keepdims=True)) + 1e-05) * gain
    return scaled.astype(jnp.bfloat16)

def reference(section_input, last_hidden, kv_gain, query_gain, w_key, w_value, w_query, w_out, segment_ids):
    kv_in = rms_rows(last_hidden, kv_gain)
    keys = jnp.dot(kv_in, w_key, preferred_element_type=jnp.float32).astype(jnp.bfloat16)
    values = jnp.dot(kv_in, w_value, preferred_element_type=jnp.float32).astype(jnp.bfloat16)
    key_heads = keys.astype(jnp.float32).reshape(TOKENS, HEADS, HD)
    value_heads = values.astype(jnp.float32).reshape(TOKENS, HEADS, HD)
    places = jnp.arange(TOKENS, dtype=jnp.int32)
    visible = (places[None, :] <= places[:, None]) & (segment_ids[None, :] == segment_ids[:, None])

    def layer(operands):
        rows, gain, w_q, w_o = operands
        q_in = rms_rows(rows, gain)
        queries = jnp.dot(q_in, w_q, preferred_element_type=jnp.float32).astype(jnp.bfloat16)
        query_heads = queries.astype(jnp.float32).reshape(TOKENS, HEADS, HD)
        scores = jnp.einsum('qhd,khd->hqk', query_heads, key_heads) * HD ** (-0.5)
        scores = jnp.where(visible[None], scores, -1e+30)
        top = lax.optimization_barrier(jnp.max(scores, axis=-1, keepdims=True))
        expo = jnp.where(visible[None], jnp.exp(scores - top), 0.0)
        weights = (expo / lax.optimization_barrier(jnp.sum(expo, axis=-1, keepdims=True))).astype(jnp.bfloat16)
        context = jnp.einsum('hqk,khd->qhd', weights.astype(jnp.float32), value_heads)
        context = context.reshape(TOKENS, HEADS * HD).astype(jnp.bfloat16)
        mixed = jnp.dot(context, w_o, preferred_element_type=jnp.float32)
        return (rows.astype(jnp.float32) + mixed).astype(jnp.bfloat16)
    return lax.map(layer, (section_input, query_gain, w_query, w_out))
```

```python
import jax
import jax.numpy as jnp
import numpy as np
from jax import lax
from jax.experimental import pallas as pl
from jax.experimental.pallas import tpu as pltpu
from jax.sharding import PartitionSpec as P

HD = 128
RB = 256
BF = jnp.bfloat16
F32 = jnp.float32
AXES = ("section", "ctx")
MIB = 1 << 20

PLACE = (((0, 1, 2, 3), (4, 5, 6, 7)), ((1, 0, 4, 5), (2, 3, 7, 6)))
SPOT = tuple(
    tuple(next((h, r) for h in range(2) for r in range(4) if table[h][r] == c) for c in range(8))
    for table in PLACE
)


def moves(step):
    pairs = []
    for s in range(16):
        for c in range(8):
            core = s % 2
            half, spot = SPOT[core][c]
            yh, x, k, h, r = step(s // 8, s // 2 % 4, core, half, spot)
            if k == core:
                place = PLACE[core][h][r % 4]
            else:
                place = c
            pairs.append((s * 8 + c, (yh * 8 + x % 4 * 2 + k) * 8 + place))
    return pairs


NEXT = moves(lambda yh, x, k, h, r: (yh, x, k, h, r + 1))
PREV = moves(lambda yh, x, k, h, r: (yh, x, k, h, r - 1))
PARTNER = moves(lambda yh, x, k, h, r: (yh, x, k, 1 - h, r))
CORE = moves(lambda yh, x, k, h, r: (yh, x, 1 - k, h, r))
FAR_Y = moves(lambda yh, x, k, h, r: (1 - yh, x, k, h, r))
X_NEXT = moves(lambda yh, x, k, h, r: (yh, x + 1, k, h, r))
X_PREV = moves(lambda yh, x, k, h, r: (yh, x - 1, k, h, r))
X_FAR = moves(lambda yh, x, k, h, r: (yh, x + 2, k, h, r))


def send(value, pairs):
    return lax.ppermute(value, AXES, pairs)


def normalize(rows, gain):
    full = rows.astype(F32)
    scaled = full * lax.rsqrt(jnp.mean(full * full, axis=-1, keepdims=True) + 1e-05) * gain
    return scaled.astype(BF)


def project_kernel(pieces, slot, has_prior, meta, *refs):
    xs = refs[:pieces]
    gain, w = refs[pieces : pieces + 2]
    normed, q, res_own, res_other = refs[-4:]
    row = 0
    for x in xs:
        rows, step = x.shape[0], 32
        base = row

        def norm_rows(i, _, x=x, base=base):
            at = pl.multiple_of(i * step, step)
            full = x[pl.ds(at, step), :].astype(F32)
            mean = jnp.mean(full * full, axis=-1, keepdims=True)
            normed[0, pl.ds(base + at, step), :] = (
                full * lax.rsqrt(mean + 1e-05) * gain[...]
            ).astype(BF)
            return 0

        lax.fori_loop(0, rows // step, norm_rows, 0)
        width = res_own.shape[2]
        for k, out in ((0, res_own), (1, res_other)):
            first = pl.multiple_of(meta[k] * width, 128)
            out[0, row : row + rows, :] = x[:, pl.ds(first, width)]
        row += rows
    q[0] = jnp.dot(normed[0], w[...], preferred_element_type=F32).astype(BF)


def project(meta, xs, gain, w, slot, prior):
    d, n = w.shape
    width = 640
    shapes = [(4, RB, d), (4, RB, n), (4, RB, width), (4, RB, width)]
    whole = lambda a: pl.BlockSpec(a.shape, lambda i, m, nd=a.ndim: (0,) * nd)
    ins = list(xs) + [gain, w]
    specs = [whole(a) for a in ins]
    aliases = {}
    if prior is not None:
        for k, a in enumerate(prior):
            aliases[1 + len(ins)] = k
            ins.append(a)
            specs.append(pl.BlockSpec(memory_space=pl.ANY))

    def kernel(meta, *refs):
        project_kernel(len(xs), slot, prior is not None, meta, *refs)

    return pl.pallas_call(
        kernel,
        grid_spec=pltpu.PrefetchScalarGridSpec(
            num_scalar_prefetch=1,
            grid=(1,),
            in_specs=specs,
            out_specs=[pl.BlockSpec((1,) + s[1:], lambda i, m: (slot, 0, 0)) for s in shapes],
        ),
        out_shape=[jax.ShapeDtypeStruct(s, BF) for s in shapes],
        input_output_aliases=aliases,
        compiler_params=pltpu.CompilerParams(vmem_limit_bytes=40 * MIB),
        cost_estimate=pl.CostEstimate(
            flops=2 * RB * d * n, bytes_accessed=2 * (3 * RB * d + d * n), transcendentals=0
        ),
    )(meta, *ins)


def more_queries_kernel(n_ref, w_ref, q_ref):
    q_ref[0] = jnp.dot(n_ref[0], w_ref[...], preferred_element_type=F32).astype(BF)


def more_queries(normed, w):
    d, n = w.shape
    return pl.pallas_call(
        more_queries_kernel,
        grid=(4,),
        in_specs=[
            pl.BlockSpec((1, RB, d), lambda i: (i, 0, 0)),
            pl.BlockSpec((d, n), lambda i: (0, 0)),
        ],
        out_specs=pl.BlockSpec((1, RB, n), lambda i: (i, 0, 0)),
        out_shape=jax.ShapeDtypeStruct((4, RB, n), BF),
        compiler_params=pltpu.CompilerParams(vmem_limit_bytes=32 * MIB),
        cost_estimate=pl.CostEstimate(
            flops=8 * RB * d * n, bytes_accessed=2 * (4 * RB * d + d * n), transcendentals=0
        ),
    )(normed, w)


def attend_kernel(
    slots, blocks, firsts, where_x, q_own, q_other, kv_own, kv_other, seg_col, seg_row, out,
    scores, tops, sums,
):
    t = pl.program_id(0)
    block = blocks[t]
    first = firsts[t]
    count = block - first + 1
    x = where_x[0]
    heads = q_own.shape[2] // HD
    factor = HD ** (-0.5) * 1.4426950408889634
    pairs = [(src, i) for src in range(2) for i in range(heads)]
    qs = (q_own, q_other)
    kvs = (kv_own, kv_other)

    def place(i):
        kb = first + i
        j = lax.rem(lax.rem(kb, 4) - x + 4, 4)
        return kb, j, kb // 4

    tops[...] = jnp.full(tops.shape, -1e30, F32)
    sums[...] = jnp.zeros(sums.shape, F32)
    q_doc = seg_col[block]
    row_at = block * RB + lax.broadcasted_iota(jnp.int32, (RB, RB), 0)
    col_at = lax.broadcasted_iota(jnp.int32, (RB, RB), 1)

    def score(i, _):
        kb, j, y = place(i)
        visible = (q_doc == seg_row[kb]) & (kb * RB + col_at <= row_at)
        for n, (src, h) in enumerate(pairs):
            cols = slice(h * HD, (h + 1) * HD)
            s = lax.dot_general(
                qs[src][0, :, cols], kvs[src][j, y, :, cols], (((1,), (1,)), ((), ())),
                preferred_element_type=F32,
            )
            s = jnp.where(visible, s, -1e30)
            scores[n, i] = s
            tops[n] = jnp.maximum(tops[n], jnp.maximum(s[:, :HD], s[:, HD:]))
        return 0

    lax.fori_loop(0, count, score, 0)
    for n in range(len(pairs)):
        tops[n] = jnp.broadcast_to(jnp.max(tops[n], axis=-1, keepdims=True), (RB, HD))

    def expo(i, _):
        for n in range(len(pairs)):
            s = scores[n, i]
            top = tops[n]
            left = jnp.exp2((s[:, :HD] - top) * factor)
            right = jnp.exp2((s[:, HD:] - top) * factor)
            scores[n, i, :, :HD] = left
            scores[n, i, :, HD:] = right
            sums[n] += left + right
        return 0

    lax.fori_loop(0, count, expo, 0)
    for n in range(len(pairs)):
        total = jnp.sum(sums[n], axis=-1, keepdims=True)
        sums[n] = jnp.broadcast_to(1.0 / total, (RB, HD))
        tops[n] = jnp.zeros((RB, HD), F32)

    def mix(i, _):
        kb, j, y = place(i)
        for n, (src, h) in enumerate(pairs):
            cols = slice((heads + h) * HD, (heads + h + 1) * HD)
            e = scores[n, i]
            inv = sums[n]
            weights = jnp.concatenate([e[:, :HD] * inv, e[:, HD:] * inv], axis=1).astype(BF)
            tops[n] += jnp.dot(weights, kvs[src][j, y, :, cols], preferred_element_type=F32)
        return 0

    lax.fori_loop(0, count, mix, 0)
    for n in range(len(pairs)):
        out[:, n * HD : (n + 1) * HD] = tops[n].astype(BF)


def attend(slots, blocks, firsts, where_x, q_own, q_other, kv_own, kv_other, seg_col, seg_row):
    n = q_own.shape[2]
    heads = n // HD
    whole = lambda a: pl.BlockSpec(a.shape, lambda t, *s, nd=a.ndim: (0,) * nd)
    q_spec = pl.BlockSpec((1, RB, n), lambda t, slots, *s: (slots[t], 0, 0))
    return pl.pallas_call(
        attend_kernel,
        grid_spec=pltpu.PrefetchScalarGridSpec(
            num_scalar_prefetch=4,
            grid=(2,),
            in_specs=[
                q_spec, q_spec, whole(kv_own), whole(kv_other), whole(seg_col), whole(seg_row)
            ],
            out_specs=pl.BlockSpec((RB, 2 * n), lambda t, *s: (t, 0)),
            scratch_shapes=[
                pltpu.VMEM((2 * heads, 5, RB, RB), F32),
                pltpu.VMEM((2 * heads, RB, HD), F32),
                pltpu.VMEM((2 * heads, RB, HD), F32),
            ],
        ),
        out_shape=jax.ShapeDtypeStruct((2 * RB, 2 * n), BF),
        compiler_params=pltpu.CompilerParams(vmem_limit_bytes=40 * MIB),
        cost_estimate=pl.CostEstimate(
            flops=4 * 2 * RB * 768 * 2 * n, bytes_accessed=8 * MIB, transcendentals=2 * RB * 768 * 6
        ),
    )(slots, blocks, firsts, where_x, q_own, q_other, kv_own, kv_other, seg_col, seg_row)


def finish_kernel(rows_of, slots, targets, c0, c1, c2a, c2b, c3, w, res, *refs):
    out = refs[-1]
    t = pl.program_id(0)
    far = jnp.where(t == 0, c2a[...], c2b[...])
    n = w.shape[1]
    total = jnp.zeros((RB, w.shape[2]), F32)
    for j, c in enumerate((c0[...], c1[...], far, c3[...])):
        for k in range(2):
            total += jnp.dot(
                c[:, k * n : (k + 1) * n], w[rows_of[2 * j + k]], preferred_element_type=F32
            )
    out[0] = (res[0].astype(F32) + total).astype(BF)


def finish(rows_of, slots, targets, parts, w, res, blocks, prior=None):
    k8, n, width = w.shape
    tile = pl.BlockSpec((RB, 2 * n), lambda t, *s: (t, 0))
    fixed = pl.BlockSpec((RB, 2 * n), lambda t, *s: (0, 0))
    ins = list(parts) + [w, res]
    specs = [tile, tile, fixed, fixed, tile]
    specs.append(pl.BlockSpec(w.shape, lambda t, *s: (0, 0, 0)))
    specs.append(pl.BlockSpec((1, RB, width), lambda t, r, slots, g: (slots[t], 0, 0)))
    aliases = {}
    if prior is not None:
        aliases[3 + len(ins)] = 0
        ins.append(prior)
        specs.append(pl.BlockSpec(memory_space=pl.ANY))
    return pl.pallas_call(
        finish_kernel,
        grid_spec=pltpu.PrefetchScalarGridSpec(
            num_scalar_prefetch=3,
            grid=(2,),
            in_specs=specs,
            out_specs=pl.BlockSpec((1, RB, width), lambda t, r, s, targets: (targets[t], 0, 0)),
        ),
        out_shape=jax.ShapeDtypeStruct((blocks, RB, width), BF),
        input_output_aliases=aliases,
        compiler_params=pltpu.CompilerParams(vmem_limit_bytes=32 * MIB),
        cost_estimate=pl.CostEstimate(
            flops=4 * RB * k8 * n * width, bytes_accessed=8 * MIB, transcendentals=0
        ),
    )(rows_of, slots, targets, *ins)


def place_kernel(targets, got, prior, out):
    out[...] = got[...]


def place(targets, got, prior):
    count, rows, width = got.shape
    return pl.pallas_call(
        place_kernel,
        grid_spec=pltpu.PrefetchScalarGridSpec(
            num_scalar_prefetch=1,
            grid=(count,),
            in_specs=[
                pl.BlockSpec((1, rows, width), lambda t, g: (t, 0, 0)),
                pl.BlockSpec(memory_space=pl.ANY),
            ],
            out_specs=pl.BlockSpec((1, rows, width), lambda t, targets: (targets[t], 0, 0)),
        ),
        out_shape=jax.ShapeDtypeStruct(prior.shape, BF),
        input_output_aliases={2: 0},
    )(targets, got, prior)


def body(
    section_input, last_hidden, kv_gain, query_gain, w_key, w_value, w_query, w_out, segment_ids
):
    section = lax.axis_index("section")
    c = lax.axis_index("ctx")
    core = section % 2
    x_at = section // 2 % 4
    y_hi = section // 8
    spot = jnp.array(SPOT, jnp.int32)[core, c]
    half, r = spot[0], spot[1]
    place_of = jnp.array(PLACE, jnp.int32)[core]
    mine, theirs = place_of[half], place_of[1 - half]

    x0 = section_input[0]
    w_q = w_query[0]
    w_o = w_out[0]
    gain = query_gain

    xp = send(x0, NEXT)
    xn = send(x0, PREV)
    w_q2 = send(w_q, PARTNER)

    kv_in = normalize(last_hidden, kv_gain)
    own_k = jnp.dot(kv_in, w_key, preferred_element_type=F32).astype(BF)
    own_v = jnp.dot(kv_in, w_value, preferred_element_type=F32).astype(BF)
    kv = jnp.concatenate([own_k, own_v], axis=1)
    kv_far = send(kv, FAR_Y)
    pair = jnp.where(y_hi == 0, jnp.stack([kv, kv_far]), jnp.stack([kv_far, kv]))
    pair2 = send(pair, CORE)
    piece = jnp.where(
        core == 0, jnp.concatenate([pair, pair2], axis=1), jnp.concatenate([pair2, pair], axis=1)
    )
    piece2 = send(piece, PARTNER)

    def spread(p):
        return jnp.stack([p, send(p, X_PREV), send(p, X_FAR), send(p, X_NEXT)])

    kv_own = spread(piece)
    kv_other = spread(piece2)

    xo_a = send(xp[: RB // 2], NEXT)
    xo_b = send(xn[RB // 2 :], PREV)
    w_o2 = send(w_o, PARTNER)

    cols = jnp.stack([mine[r], theirs[r]])
    state = project(cols, [x0], gain, w_q, 0, None)
    state = project(cols, [xn], gain, w_q, 1, state)
    state = project(cols, [xp], gain, w_q, 3, state)
    normed, q_own, res_own, res_other = project(cols, [xo_a, xo_b], gain, w_q, 2, state)
    q_other = more_queries(normed, w_q2)

    ids = segment_ids.reshape(8, RB)
    starts = jnp.sum(segment_ids[None, :] < ids[:, :1], axis=1, dtype=jnp.int32) // RB
    starts = jnp.maximum(starts, jnp.arange(8, dtype=jnp.int32) - 4)
    seg_col = segment_ids.reshape(8, RB, 1)
    seg_row = segment_ids.reshape(8, 1, RB)
    xs = x_at[None]
    w_o_r = w_o.reshape(8, 384, -1)
    w_o2_r = w_o2.reshape(8, 384, -1)
    ring = (r + jnp.arange(4, dtype=jnp.int32)) % 4
    rows_of = jnp.stack([mine[ring], theirs[ring]], axis=1).reshape(8)

    order = jnp.arange(2, dtype=jnp.int32)
    result = None
    for chunk in range(2):
        spots = order + 2 * chunk
        slots = (spots - r + 4) % 4
        blocks = mine[2 * chunk : 2 * chunk + 2]
        others = theirs[2 * chunk : 2 * chunk + 2]
        own = attend(
            slots, blocks, starts[blocks], xs, q_own, q_other, kv_own, kv_other, seg_col, seg_row
        )
        cp = send(own, NEXT)
        cn = send(own, PREV)
        co_a = send(cp[:RB], NEXT)
        co_b = send(cn[RB:], PREV)
        parts = (own, cn, co_a, co_b, cp)
        sent = send(finish(rows_of, slots, order, parts, w_o2_r, res_other, 2), PARTNER)
        result = finish(rows_of, slots, blocks, parts, w_o_r, res_own, 8, result)
        result = place(others, sent, result)
    return result.reshape(1, 8 * RB, -1)


def solution(mesh):
    return jax.shard_map(
        body,
        mesh=mesh,
        in_specs=(
            P("section", "ctx", None),
            P("section", None),
            P(),
            P("section", None),
            P(None, "ctx"),
            P(None, "ctx"),
            P("section", None, "ctx"),
            P("section", None, "ctx"),
            P(),
        ),
        out_specs=P("section", None, "ctx"),
        check_vma=False,
    )
```

```python
import functools

import jax
import jax.numpy as jnp
from jax import lax
from jax.experimental import pallas as pl
from jax.experimental.pallas import tpu as pltpu
from jax.sharding import PartitionSpec as P

HD = 128
RB = 256
BF = jnp.bfloat16
F32 = jnp.float32
AXES = ("section", "ctx")
MIB = 1 << 20

PLACE = (((0, 1, 2, 3), (4, 5, 6, 7)), ((1, 0, 4, 5), (2, 3, 7, 6)))
SPOT = tuple(
    tuple(next((h, r) for h in range(2) for r in range(4) if table[h][r] == c) for c in range(8))
    for table in PLACE
)

MINE, THEIRS, SLOT, ROWS, OWN, FIRST, X_AT = 0, 4, 8, 12, 20, 22, 30


def facts_of(core, c):
    half, r = SPOT[core][c]
    mine, theirs = PLACE[core][half], PLACE[core][1 - half]
    slots = [(p - r) % 4 for p in range(4)]
    ring = [(r + j) % 4 for j in range(4)]
    rows = [place[p] for p in ring for place in (mine, theirs)]
    return [*mine, *theirs, *slots, *rows, mine[r], theirs[r]]


FACTS = [[facts_of(core, c) for c in range(8)] for core in range(2)]


def moves(step):
    pairs = []
    for s in range(16):
        for c in range(8):
            core = s % 2
            half, spot = SPOT[core][c]
            yh, x, k, h, r = step(s // 8, s // 2 % 4, core, half, spot)
            if k == core:
                place = PLACE[core][h][r % 4]
            else:
                place = c
            pairs.append((s * 8 + c, (yh * 8 + x % 4 * 2 + k) * 8 + place))
    return pairs


NEXT = moves(lambda yh, x, k, h, r: (yh, x, k, h, r + 1))
PREV = moves(lambda yh, x, k, h, r: (yh, x, k, h, r - 1))
PARTNER = moves(lambda yh, x, k, h, r: (yh, x, k, 1 - h, r))
CORE = moves(lambda yh, x, k, h, r: (yh, x, 1 - k, h, r))
FAR_Y = moves(lambda yh, x, k, h, r: (1 - yh, x, k, h, r))
X_NEXT = moves(lambda yh, x, k, h, r: (yh, x + 1, k, h, r))
X_PREV = moves(lambda yh, x, k, h, r: (yh, x - 1, k, h, r))
X_FAR = moves(lambda yh, x, k, h, r: (yh, x + 2, k, h, r))


def send(value, pairs):
    return lax.ppermute(value, AXES, pairs)


def normalize(rows, gain):
    full = rows.astype(F32)
    scaled = full * lax.rsqrt(jnp.mean(full * full, axis=-1, keepdims=True) + 1e-05) * gain
    return scaled.astype(BF)


def project_kernel(pieces, meta, *refs):
    xs = refs[:pieces]
    gain, w = refs[pieces : pieces + 2]
    normed, q, res_own, res_other = refs[-4:]
    step = 32
    base = 0
    for x in xs:
        rows = x.shape[0]

        def norm_rows(i, _, x=x, base=base):
            at = pl.multiple_of(i * step, step)
            full = x[pl.ds(at, step), :].astype(F32)
            mean = jnp.mean(full * full, axis=-1, keepdims=True)
            normed[0, pl.ds(base + at, step), :] = (
                full * lax.rsqrt(mean + 1e-05) * gain[...]
            ).astype(BF)
            return 0

        lax.fori_loop(0, rows // step, norm_rows, 0)
        width = res_own.shape[2]
        for k, out in ((0, res_own), (1, res_other)):
            first = pl.multiple_of(meta[OWN + k] * width, 128)
            out[0, base : base + rows, :] = x[:, pl.ds(first, width)]
        base += rows
    q[0] = jnp.dot(normed[0], w[...], preferred_element_type=F32).astype(BF)


def project(meta, xs, gain, w, slot, width, prior=None):
    d, n = w.shape
    shapes = [(4, RB, d), (4, RB, n), (4, RB, width), (4, RB, width)]
    whole = lambda a: pl.BlockSpec(a.shape, lambda i, m, nd=a.ndim: (0,) * nd)
    ins = list(xs) + [gain, w]
    specs = [whole(a) for a in ins]
    aliases = {}
    for k, a in enumerate(prior or ()):
        aliases[1 + len(ins)] = k
        ins.append(a)
        specs.append(pl.BlockSpec(memory_space=pl.ANY))

    def kernel(meta, *refs):
        project_kernel(len(xs), meta, *refs)

    return pl.pallas_call(
        kernel,
        grid_spec=pltpu.PrefetchScalarGridSpec(
            num_scalar_prefetch=1,
            grid=(1,),
            in_specs=specs,
            out_specs=[pl.BlockSpec((1,) + s[1:], lambda i, m: (slot, 0, 0)) for s in shapes],
        ),
        out_shape=[jax.ShapeDtypeStruct(s, BF) for s in shapes],
        input_output_aliases=aliases,
        compiler_params=pltpu.CompilerParams(vmem_limit_bytes=40 * MIB),
        cost_estimate=pl.CostEstimate(
            flops=2 * RB * d * n, bytes_accessed=2 * (3 * RB * d + d * n), transcendentals=0
        ),
    )(meta, *ins)


def more_queries_kernel(n_ref, w_ref, q_ref):
    q_ref[0] = jnp.dot(n_ref[0], w_ref[...], preferred_element_type=F32).astype(BF)


def more_queries(normed, w):
    d, n = w.shape
    return pl.pallas_call(
        more_queries_kernel,
        grid=(4,),
        in_specs=[
            pl.BlockSpec((1, RB, d), lambda i: (i, 0, 0)),
            pl.BlockSpec((d, n), lambda i: (0, 0)),
        ],
        out_specs=pl.BlockSpec((1, RB, n), lambda i: (i, 0, 0)),
        out_shape=jax.ShapeDtypeStruct((4, RB, n), BF),
        compiler_params=pltpu.CompilerParams(vmem_limit_bytes=32 * MIB),
        cost_estimate=pl.CostEstimate(
            flops=8 * RB * d * n, bytes_accessed=2 * (4 * RB * d + d * n), transcendentals=0
        ),
    )(normed, w)


def attend_kernel(
    chunk, meta, q_own, q_other, kv_own, kv_other, seg_col, seg_row, out, scores, tops, sums
):
    t = pl.program_id(0)
    block = meta[MINE + 2 * chunk + t]
    first = meta[FIRST + block]
    count = block - first + 1
    x = meta[X_AT]
    heads = q_own.shape[2] // HD
    factor = HD ** (-0.5) * 1.4426950408889634
    pairs = [(src, i) for src in range(2) for i in range(heads)]
    qs = (q_own, q_other)
    kvs = (kv_own, kv_other)

    def place(i):
        kb = first + i
        j = lax.rem(lax.rem(kb, 4) - x + 4, 4)
        return kb, j, kb // 4

    tops[...] = jnp.full(tops.shape, -1e30, F32)
    sums[...] = jnp.zeros(sums.shape, F32)
    q_doc = seg_col[block]
    row_at = block * RB + lax.broadcasted_iota(jnp.int32, (RB, RB), 0)
    col_at = lax.broadcasted_iota(jnp.int32, (RB, RB), 1)

    def score(i, _):
        kb, j, y = place(i)
        visible = (q_doc == seg_row[kb]) & (kb * RB + col_at <= row_at)
        for n, (src, h) in enumerate(pairs):
            cols = slice(h * HD, (h + 1) * HD)
            s = lax.dot_general(
                qs[src][0, :, cols], kvs[src][j, y, :, cols], (((1,), (1,)), ((), ())),
                preferred_element_type=F32,
            )
            s = jnp.where(visible, s, -1e30)
            scores[n, i] = s
            tops[n] = jnp.maximum(tops[n], jnp.maximum(s[:, :HD], s[:, HD:]))
        return 0

    lax.fori_loop(0, count, score, 0)
    for n in range(len(pairs)):
        tops[n] = jnp.broadcast_to(jnp.max(tops[n], axis=-1, keepdims=True), (RB, HD))

    def expo(i, _):
        for n in range(len(pairs)):
            s = scores[n, i]
            top = tops[n]
            left = jnp.exp2((s[:, :HD] - top) * factor)
            right = jnp.exp2((s[:, HD:] - top) * factor)
            scores[n, i, :, :HD] = left
            scores[n, i, :, HD:] = right
            sums[n] += left + right
        return 0

    lax.fori_loop(0, count, expo, 0)
    for n in range(len(pairs)):
        total = jnp.sum(sums[n], axis=-1, keepdims=True)
        sums[n] = jnp.broadcast_to(1.0 / total, (RB, HD))
        tops[n] = jnp.zeros((RB, HD), F32)

    def mix(i, _):
        kb, j, y = place(i)
        for n, (src, h) in enumerate(pairs):
            cols = slice((heads + h) * HD, (heads + h + 1) * HD)
            e = scores[n, i]
            inv = sums[n]
            weights = jnp.concatenate([e[:, :HD] * inv, e[:, HD:] * inv], axis=1).astype(BF)
            tops[n] += jnp.dot(weights, kvs[src][j, y, :, cols], preferred_element_type=F32)
        return 0

    lax.fori_loop(0, count, mix, 0)
    for n in range(len(pairs)):
        out[:, n * HD : (n + 1) * HD] = tops[n].astype(BF)


def attend(meta, chunk, q_own, q_other, kv_own, kv_other, seg_col, seg_row):
    n = q_own.shape[2]
    heads = n // HD
    whole = lambda a: pl.BlockSpec(a.shape, lambda t, m, nd=a.ndim: (0,) * nd)
    q_spec = pl.BlockSpec((1, RB, n), lambda t, m: (m[SLOT + 2 * chunk + t], 0, 0))
    return pl.pallas_call(
        functools.partial(attend_kernel, chunk),
        grid_spec=pltpu.PrefetchScalarGridSpec(
            num_scalar_prefetch=1,
            grid=(2,),
            in_specs=[
                q_spec, q_spec, whole(kv_own), whole(kv_other), whole(seg_col), whole(seg_row)
            ],
            out_specs=pl.BlockSpec((RB, 2 * n), lambda t, m: (t, 0)),
            scratch_shapes=[
                pltpu.VMEM((2 * heads, 5, RB, RB), F32),
                pltpu.VMEM((2 * heads, RB, HD), F32),
                pltpu.VMEM((2 * heads, RB, HD), F32),
            ],
        ),
        out_shape=jax.ShapeDtypeStruct((2 * RB, 2 * n), BF),
        compiler_params=pltpu.CompilerParams(vmem_limit_bytes=40 * MIB),
        cost_estimate=pl.CostEstimate(
            flops=4 * 2 * RB * 768 * 2 * n, bytes_accessed=8 * MIB, transcendentals=2 * RB * 768 * 6
        ),
    )(meta, q_own, q_other, kv_own, kv_other, seg_col, seg_row)


def finish_kernel(meta, c0, c1, c2a, c2b, c3, w, res, *refs):
    out = refs[-1]
    t = pl.program_id(0)
    far = jnp.where(t == 0, c2a[...], c2b[...])
    n = w.shape[1]
    total = jnp.zeros((RB, w.shape[2]), F32)
    for j, c in enumerate((c0[...], c1[...], far, c3[...])):
        for k in range(2):
            total += jnp.dot(
                c[:, k * n : (k + 1) * n],
                w[meta[ROWS + 2 * j + k]],
                preferred_element_type=F32,
            )
    out[0] = (res[0].astype(F32) + total).astype(BF)


def finish(meta, chunk, parts, w, res, blocks, prior=None):
    k8, n, width = w.shape
    tile = pl.BlockSpec((RB, 2 * n), lambda t, m: (t, 0))
    fixed = pl.BlockSpec((RB, 2 * n), lambda t, m: (0, 0))
    ins = list(parts) + [w, res]
    specs = [tile, tile, fixed, fixed, tile]
    specs.append(pl.BlockSpec(w.shape, lambda t, m: (0, 0, 0)))
    specs.append(pl.BlockSpec((1, RB, width), lambda t, m: (m[SLOT + 2 * chunk + t], 0, 0)))
    aliases = {}
    if prior is not None:
        aliases[1 + len(ins)] = 0
        ins.append(prior)
        specs.append(pl.BlockSpec(memory_space=pl.ANY))
    if blocks == 2:
        target = lambda t, m: (t, 0, 0)
    else:
        target = lambda t, m: (m[MINE + 2 * chunk + t], 0, 0)
    return pl.pallas_call(
        finish_kernel,
        grid_spec=pltpu.PrefetchScalarGridSpec(
            num_scalar_prefetch=1,
            grid=(2,),
            in_specs=specs,
            out_specs=pl.BlockSpec((1, RB, width), target),
        ),
        out_shape=jax.ShapeDtypeStruct((blocks, RB, width), BF),
        input_output_aliases=aliases,
        compiler_params=pltpu.CompilerParams(vmem_limit_bytes=32 * MIB),
        cost_estimate=pl.CostEstimate(
            flops=4 * RB * k8 * n * width, bytes_accessed=8 * MIB, transcendentals=0
        ),
    )(meta, *ins)


def place_kernel(meta, got, prior, out):
    out[...] = got[...]


def place(meta, chunk, got, prior):
    count, rows, width = got.shape
    target = lambda t, m: (m[THEIRS + 2 * chunk + t], 0, 0)
    return pl.pallas_call(
        place_kernel,
        grid_spec=pltpu.PrefetchScalarGridSpec(
            num_scalar_prefetch=1,
            grid=(count,),
            in_specs=[
                pl.BlockSpec((1, rows, width), lambda t, m: (t, 0, 0)),
                pl.BlockSpec(memory_space=pl.ANY),
            ],
            out_specs=pl.BlockSpec((1, rows, width), target),
        ),
        out_shape=jax.ShapeDtypeStruct(prior.shape, BF),
        input_output_aliases={2: 0},
    )(meta, got, prior)


def after(value, *done):
    return lax.optimization_barrier((value,) + done)[0]


def body(
    section_input, last_hidden, kv_gain, query_gain, w_key, w_value, w_query, w_out, segment_ids
):
    section = lax.axis_index("section")
    c = lax.axis_index("ctx")
    core = section % 2
    y_hi = section // 8
    x0 = section_input[0]
    w_q = w_query[0]
    w_o = w_out[0]
    width = w_o.shape[1]

    xp = send(x0, NEXT)
    xn = send(x0, PREV)
    w_q2 = send(w_q, PARTNER)

    ids = segment_ids.reshape(8, RB)
    starts = jnp.sum(segment_ids[None, :] < ids[:, :1], axis=1, dtype=jnp.int32) // RB
    starts = jnp.maximum(starts, jnp.arange(8, dtype=jnp.int32) - 4)
    facts = jnp.array(FACTS, jnp.int32)[core, c]
    meta = jnp.concatenate([facts, starts, (section // 2 % 4)[None]])
    seg_col = segment_ids.reshape(8, RB, 1)
    seg_row = segment_ids.reshape(8, 1, RB)

    def cache(last_hidden, w_key, w_value):
        kv_in = normalize(last_hidden, kv_gain)
        own_k = jnp.dot(kv_in, w_key, preferred_element_type=F32).astype(BF)
        own_v = jnp.dot(kv_in, w_value, preferred_element_type=F32).astype(BF)
        kv = jnp.concatenate([own_k, own_v], axis=1)
        kv_far = send(kv, FAR_Y)
        pair = jnp.where(y_hi == 0, jnp.stack([kv, kv_far]), jnp.stack([kv_far, kv]))
        pair2 = send(pair, CORE)
        piece = jnp.where(
            core == 0,
            jnp.concatenate([pair, pair2], axis=1),
            jnp.concatenate([pair2, pair], axis=1),
        )
        piece2 = send(piece, PARTNER)
        share = lax.dynamic_index_in_dim(piece, core, 0, keepdims=False)
        o1 = send(share, X_PREV)
        o3 = send(share, X_NEXT)
        o2 = send(after(share, o1, o3), X_FAR)
        return piece2, jnp.stack([share, o1, o2, o3])

    def nothing(last_hidden, w_key, w_value):
        half_rows = 2 * last_hidden.shape[0]
        cols = 2 * w_key.shape[1]
        return jnp.zeros((2, half_rows, cols), BF), jnp.zeros((4, half_rows, cols), BF)

    piece2, got = lax.cond(segment_ids[0] >= 0, cache, nothing, last_hidden, w_key, w_value)
    xp, xn, piece2, got = lax.optimization_barrier((xp, xn, piece2, got))
    xo_a = send(xp[: RB // 2], NEXT)
    xo_b = send(xn[RB // 2 :], PREV)
    t1 = send(piece2, X_PREV)
    t3 = send(piece2, X_NEXT)
    state = project(meta, [after(x0, xp, xn)], query_gain, w_q, 0, width)
    state = project(meta, [xn], query_gain, w_q, 1, width, state)
    state = project(meta, [xp], query_gain, w_q, 3, width, state)
    xo_a, xo_b, t1, t3, *state = lax.optimization_barrier((xo_a, xo_b, t1, t3, *state))
    t2 = send(after(piece2, t1, t3), X_FAR)
    got2 = send(after(got, t1, t3), CORE)
    w_q2, t2, got2 = lax.optimization_barrier((w_q2, t2, got2))
    kv_own = jnp.where(
        core == 0, jnp.stack([got, got2], axis=1), jnp.stack([got2, got], axis=1)
    )
    kv_other = jnp.stack([piece2, t1, t2, t3])
    normed, q_own, res_own, res_other = project(
        meta, [xo_a, xo_b], query_gain, w_q, 2, width, state
    )
    w_o2 = send(after(w_o, xo_a, xo_b, w_q2), PARTNER)
    q_other = more_queries(normed, w_q2)

    heads_cols = w_q.shape[1]
    w_o_r = w_o.reshape(8, heads_cols, width)
    w_o2_r = w_o2.reshape(8, heads_cols, width)

    result = None
    for chunk in range(2):
        own = attend(meta, chunk, q_own, q_other, kv_own, kv_other, seg_col, seg_row)
        cp = send(own, NEXT)
        cn = send(own, PREV)
        co_a = send(cp[:RB], NEXT)
        co_b = send(cn[RB:], PREV)
        parts = (own, cn, co_a, co_b, cp)
        sent = send(finish(meta, chunk, parts, w_o2_r, res_other, 2), PARTNER)
        result = finish(meta, chunk, parts, w_o_r, res_own, 8, result)
        result = place(meta, chunk, sent, result)
    return result.reshape(1, 8 * RB, -1)


def solution(mesh):
    return jax.shard_map(
        body,
        mesh=mesh,
        in_specs=(
            P("section", "ctx", None),
            P("section", None),
            P(),
            P("section", None),
            P(None, "ctx"),
            P(None, "ctx"),
            P("section", None, "ctx"),
            P("section", None, "ctx"),
            P(),
        ),
        out_specs=P("section", None, "ctx"),
        check_vma=False,
    )
```

```python
import functools

import jax
import jax.numpy as jnp
from jax import lax
from jax.experimental import pallas as pl
from jax.experimental.pallas import tpu as pltpu
from jax.sharding import PartitionSpec as P

HD = 128
RB = 256
BF = jnp.bfloat16
F32 = jnp.float32
AXES = ("section", "ctx")
MIB = 1 << 20

PLACE = (((0, 1, 2, 3), (4, 5, 6, 7)), ((1, 0, 4, 5), (2, 3, 7, 6)))
SPOT = tuple(
    tuple(next((h, r) for h in range(2) for r in range(4) if table[h][r] == c) for c in range(8))
    for table in PLACE
)

MINE, THEIRS, SLOT, ROWS, OWN, FIRST, X_AT = 0, 4, 8, 12, 20, 22, 30


def facts_of(core, c):
    half, r = SPOT[core][c]
    mine, theirs = PLACE[core][half], PLACE[core][1 - half]
    ring = [r, r ^ 1, (r + 2) % 4, 3 - r]
    slots = [ring.index(p) for p in range(4)]
    rows = [place[p] for p in ring for place in (mine, theirs)]
    return [*mine, *theirs, *slots, *rows, mine[r], theirs[r]]


FACTS = [[facts_of(core, c) for c in range(8)] for core in range(2)]


def moves(step):
    pairs = []
    for s in range(16):
        for c in range(8):
            core = s % 2
            half, spot = SPOT[core][c]
            yh, x, k, h, r = step(s // 8, s // 2 % 4, core, half, spot)
            if k == core:
                place = PLACE[core][h][r % 4]
            else:
                place = c
            pairs.append((s * 8 + c, (yh * 8 + x % 4 * 2 + k) * 8 + place))
    return pairs


IN = moves(lambda yh, x, k, h, r: (yh, x, k, h, r ^ 1))
OUT = moves(lambda yh, x, k, h, r: (yh, x, k, h, 3 - r))
PARTNER = moves(lambda yh, x, k, h, r: (yh, x, k, 1 - h, r))
CORE = moves(lambda yh, x, k, h, r: (yh, x, 1 - k, h, r))
FAR_Y = [
    (a, b) for a, b in moves(lambda yh, x, k, h, r: (1 - yh, x, k, h, r)) if a // 8 % 2 == 0
]
X_NEXT = moves(lambda yh, x, k, h, r: (yh, x + 1, k, h, r))
X_PREV = moves(lambda yh, x, k, h, r: (yh, x - 1, k, h, r))
X_FAR = moves(lambda yh, x, k, h, r: (yh, x + 2, k, h, r))


def send(value, pairs):
    return lax.ppermute(value, AXES, pairs)


def normalize(rows, gain):
    full = rows.astype(F32)
    scaled = full * lax.rsqrt(jnp.mean(full * full, axis=-1, keepdims=True) + 1e-05) * gain
    return scaled.astype(BF)


def project_kernel(pieces, meta, *refs):
    xs = refs[:pieces]
    gain, w = refs[pieces : pieces + 2]
    normed, q, res_own, res_other = refs[-4:]
    step = 32
    base = 0
    for x in xs:
        rows = x.shape[0]

        def norm_rows(i, _, x=x, base=base):
            at = pl.multiple_of(i * step, step)
            full = x[pl.ds(at, step), :].astype(F32)
            mean = jnp.mean(full * full, axis=-1, keepdims=True)
            normed[0, pl.ds(base + at, step), :] = (
                full * lax.rsqrt(mean + 1e-05) * gain[...]
            ).astype(BF)
            return 0

        lax.fori_loop(0, rows // step, norm_rows, 0)
        width = res_own.shape[2]
        for k, out in ((0, res_own), (1, res_other)):
            first = pl.multiple_of(meta[OWN + k] * width, 128)
            out[0, base : base + rows, :] = x[:, pl.ds(first, width)]
        base += rows
    q[0] = jnp.dot(normed[0], w[...], preferred_element_type=F32).astype(BF)


def project(meta, xs, gain, w, slot, width, prior=None):
    d, n = w.shape
    shapes = [(4, RB, d), (4, RB, n), (4, RB, width), (4, RB, width)]
    whole = lambda a: pl.BlockSpec(a.shape, lambda i, m, nd=a.ndim: (0,) * nd)
    ins = list(xs) + [gain, w]
    specs = [whole(a) for a in ins]
    aliases = {}
    for k, a in enumerate(prior or ()):
        aliases[1 + len(ins)] = k
        ins.append(a)
        specs.append(pl.BlockSpec(memory_space=pl.ANY))

    def kernel(meta, *refs):
        project_kernel(len(xs), meta, *refs)

    return pl.pallas_call(
        kernel,
        grid_spec=pltpu.PrefetchScalarGridSpec(
            num_scalar_prefetch=1,
            grid=(1,),
            in_specs=specs,
            out_specs=[pl.BlockSpec((1,) + s[1:], lambda i, m: (slot, 0, 0)) for s in shapes],
        ),
        out_shape=[jax.ShapeDtypeStruct(s, BF) for s in shapes],
        input_output_aliases=aliases,
        compiler_params=pltpu.CompilerParams(vmem_limit_bytes=40 * MIB),
        cost_estimate=pl.CostEstimate(
            flops=2 * RB * d * n, bytes_accessed=2 * (3 * RB * d + d * n), transcendentals=0
        ),
    )(meta, *ins)


def more_queries_kernel(n_ref, wa_ref, wb_ref, q_ref):
    k = wa_ref.shape[0]
    q = jnp.dot(n_ref[0, :, :k], wa_ref[...], preferred_element_type=F32)
    q += jnp.dot(n_ref[0, :, k:], wb_ref[...], preferred_element_type=F32)
    q_ref[0] = q.astype(BF)


def more_queries(normed, wa, wb):
    d, n = normed.shape[2], wa.shape[1]
    return pl.pallas_call(
        more_queries_kernel,
        grid=(4,),
        in_specs=[
            pl.BlockSpec((1, RB, d), lambda i: (i, 0, 0)),
            pl.BlockSpec(wa.shape, lambda i: (0, 0)),
            pl.BlockSpec(wb.shape, lambda i: (0, 0)),
        ],
        out_specs=pl.BlockSpec((1, RB, n), lambda i: (i, 0, 0)),
        out_shape=jax.ShapeDtypeStruct((4, RB, n), BF),
        compiler_params=pltpu.CompilerParams(vmem_limit_bytes=32 * MIB),
        cost_estimate=pl.CostEstimate(
            flops=8 * RB * d * n, bytes_accessed=2 * (4 * RB * d + d * n), transcendentals=0
        ),
    )(normed, wa, wb)


def attend_kernel(
    chunk, meta, q_own, q_other, kv_own, kv_other, seg_col, seg_row, out, scores, tops, sums
):
    t = pl.program_id(0)
    block = meta[MINE + 2 * chunk + t]
    first = meta[FIRST + block]
    count = block - first + 1
    x = meta[X_AT]
    heads = q_own.shape[2] // HD
    factor = HD ** (-0.5) * 1.4426950408889634
    pairs = [(src, i) for src in range(2) for i in range(heads)]
    qs = (q_own, q_other)
    kvs = (kv_own, kv_other)

    def place(i):
        kb = first + i
        j = lax.rem(lax.rem(kb, 4) - x + 4, 4)
        return kb, j, kb // 4

    tops[...] = jnp.full(tops.shape, -1e30, F32)
    sums[...] = jnp.zeros(sums.shape, F32)
    q_doc = seg_col[block]
    row_at = block * RB + lax.broadcasted_iota(jnp.int32, (RB, RB), 0)
    col_at = lax.broadcasted_iota(jnp.int32, (RB, RB), 1)

    def score(i, _):
        kb, j, y = place(i)
        visible = (q_doc == seg_row[kb]) & (kb * RB + col_at <= row_at)
        for n, (src, h) in enumerate(pairs):
            cols = slice(h * HD, (h + 1) * HD)
            s = lax.dot_general(
                qs[src][0, :, cols], kvs[src][j, y, :, cols], (((1,), (1,)), ((), ())),
                preferred_element_type=F32,
            )
            s = jnp.where(visible, s, -1e30)
            scores[n, i] = s
            tops[n] = jnp.maximum(tops[n], jnp.maximum(s[:, :HD], s[:, HD:]))
        return 0

    lax.fori_loop(0, count, score, 0)
    for n in range(len(pairs)):
        tops[n] = jnp.broadcast_to(jnp.max(tops[n], axis=-1, keepdims=True), (RB, HD))

    def expo(i, _):
        for n in range(len(pairs)):
            s = scores[n, i]
            top = tops[n]
            left = jnp.exp2((s[:, :HD] - top) * factor)
            right = jnp.exp2((s[:, HD:] - top) * factor)
            scores[n, i, :, :HD] = left
            scores[n, i, :, HD:] = right
            sums[n] += left + right
        return 0

    lax.fori_loop(0, count, expo, 0)
    for n in range(len(pairs)):
        total = jnp.sum(sums[n], axis=-1, keepdims=True)
        sums[n] = jnp.broadcast_to(1.0 / total, (RB, HD))
        tops[n] = jnp.zeros((RB, HD), F32)

    def mix(i, _):
        kb, j, y = place(i)
        for n, (src, h) in enumerate(pairs):
            cols = slice((heads + h) * HD, (heads + h + 1) * HD)
            e = scores[n, i]
            inv = sums[n]
            weights = jnp.concatenate([e[:, :HD] * inv, e[:, HD:] * inv], axis=1).astype(BF)
            tops[n] += jnp.dot(weights, kvs[src][j, y, :, cols], preferred_element_type=F32)
        return 0

    lax.fori_loop(0, count, mix, 0)
    for n in range(len(pairs)):
        out[:, n * HD : (n + 1) * HD] = tops[n].astype(BF)


def attend(meta, chunk, q_own, q_other, kv_own, kv_other, seg_col, seg_row):
    n = q_own.shape[2]
    heads = n // HD
    whole = lambda a: pl.BlockSpec(a.shape, lambda t, m, nd=a.ndim: (0,) * nd)
    q_spec = pl.BlockSpec((1, RB, n), lambda t, m: (m[SLOT + 2 * chunk + t], 0, 0))
    return pl.pallas_call(
        functools.partial(attend_kernel, chunk),
        grid_spec=pltpu.PrefetchScalarGridSpec(
            num_scalar_prefetch=1,
            grid=(2,),
            in_specs=[
                q_spec, q_spec, whole(kv_own), whole(kv_other), whole(seg_col), whole(seg_row)
            ],
            out_specs=pl.BlockSpec((RB, 2 * n), lambda t, m: (t, 0)),
            scratch_shapes=[
                pltpu.VMEM((2 * heads, 5, RB, RB), F32),
                pltpu.VMEM((2 * heads, RB, HD), F32),
                pltpu.VMEM((2 * heads, RB, HD), F32),
            ],
        ),
        out_shape=jax.ShapeDtypeStruct((2 * RB, 2 * n), BF),
        compiler_params=pltpu.CompilerParams(vmem_limit_bytes=40 * MIB),
        cost_estimate=pl.CostEstimate(
            flops=4 * 2 * RB * 768 * 2 * n, bytes_accessed=8 * MIB, transcendentals=2 * RB * 768 * 6
        ),
    )(meta, q_own, q_other, kv_own, kv_other, seg_col, seg_row)


def reorder_kernel(meta, w, out):
    out[...] = w[...]


def reorder(meta, w, swap):
    k8, n, width = w.shape
    return pl.pallas_call(
        reorder_kernel,
        grid_spec=pltpu.PrefetchScalarGridSpec(
            num_scalar_prefetch=1,
            grid=(k8,),
            in_specs=[
                pl.BlockSpec((1, n, width), lambda k, m: (m[ROWS + (k + swap - 2 * swap * (k % 2))], 0, 0))
            ],
            out_specs=pl.BlockSpec((1, n, width), lambda k, m: (k, 0, 0)),
        ),
        out_shape=jax.ShapeDtypeStruct(w.shape, BF),
    )(meta, w).reshape(k8 * n, width)


def finish_kernel(meta, c0, c1, c2a, c2b, c3, w, res, *refs):
    out = refs[-1]
    t = pl.program_id(0)
    far = jnp.where(t == 0, c2a[...], c2b[...])
    n = far.shape[1]
    total = res[0].astype(F32)
    for j, c in enumerate((c0[...], c1[...], far, c3[...])):
        total += jnp.dot(c, w[j * n : (j + 1) * n, :], preferred_element_type=F32)
    out[0] = total.astype(BF)


def finish(meta, chunk, parts, w, res, blocks, prior=None):
    depth, width = w.shape
    n = depth // 4
    tile = pl.BlockSpec((RB, n), lambda t, m: (t, 0))
    fixed = pl.BlockSpec((RB, n), lambda t, m: (0, 0))
    ins = list(parts) + [w, res]
    specs = [tile, tile, fixed, fixed, tile]
    specs.append(pl.BlockSpec(w.shape, lambda t, m: (0, 0)))
    specs.append(pl.BlockSpec((1, RB, width), lambda t, m: (m[SLOT + 2 * chunk + t], 0, 0)))
    aliases = {}
    if prior is not None:
        aliases[1 + len(ins)] = 0
        ins.append(prior)
        specs.append(pl.BlockSpec(memory_space=pl.ANY))
    if blocks == 2:
        target = lambda t, m: (t, 0, 0)
    else:
        target = lambda t, m: (m[MINE + 2 * chunk + t], 0, 0)
    return pl.pallas_call(
        finish_kernel,
        grid_spec=pltpu.PrefetchScalarGridSpec(
            num_scalar_prefetch=1,
            grid=(2,),
            in_specs=specs,
            out_specs=pl.BlockSpec((1, RB, width), target),
        ),
        out_shape=jax.ShapeDtypeStruct((blocks, RB, width), BF),
        input_output_aliases=aliases,
        compiler_params=pltpu.CompilerParams(vmem_limit_bytes=32 * MIB),
        cost_estimate=pl.CostEstimate(
            flops=4 * RB * depth * width, bytes_accessed=8 * MIB, transcendentals=0
        ),
    )(meta, *ins)


def place_kernel(meta, got, prior, out):
    out[...] = got[...]


def place(meta, chunk, got, prior):
    count, rows, width = got.shape
    target = lambda t, m: (m[THEIRS + 2 * chunk + t], 0, 0)
    return pl.pallas_call(
        place_kernel,
        grid_spec=pltpu.PrefetchScalarGridSpec(
            num_scalar_prefetch=1,
            grid=(count,),
            in_specs=[
                pl.BlockSpec((1, rows, width), lambda t, m: (t, 0, 0)),
                pl.BlockSpec(memory_space=pl.ANY),
            ],
            out_specs=pl.BlockSpec((1, rows, width), target),
        ),
        out_shape=jax.ShapeDtypeStruct(prior.shape, BF),
        input_output_aliases={2: 0},
    )(meta, got, prior)


def after(value, *done):
    return lax.optimization_barrier((value,) + done)[0]


def body(
    section_input, last_hidden, kv_gain, query_gain, w_key, w_value, w_query, w_out, segment_ids
):
    section = lax.axis_index("section")
    c = lax.axis_index("ctx")
    core = section % 2
    y_hi = section // 8
    x0 = section_input[0]
    w_q = w_query[0]
    w_o = w_out[0]
    width = w_o.shape[1]

    x_in = send(x0, IN)
    x_out = send(x0, OUT)
    cut = w_q.shape[0] * 2 // 5

    ids = segment_ids.reshape(8, RB)
    starts = jnp.sum(segment_ids[None, :] < ids[:, :1], axis=1, dtype=jnp.int32) // RB
    starts = jnp.maximum(starts, jnp.arange(8, dtype=jnp.int32) - 4)
    facts = jnp.array(FACTS, jnp.int32)[core, c]
    meta = jnp.concatenate([facts, starts, (section // 2 % 4)[None]])
    seg_col = segment_ids.reshape(8, RB, 1)
    seg_row = segment_ids.reshape(8, 1, RB)

    def cache(last_hidden, w_key, w_value, w_query):
        kv_in = normalize(last_hidden, kv_gain)
        own_k = jnp.dot(kv_in, w_key, preferred_element_type=F32).astype(BF)
        own_v = jnp.dot(kv_in, w_value, preferred_element_type=F32).astype(BF)
        kv = jnp.concatenate([own_k, own_v], axis=1)
        kv2 = send(kv, CORE)
        pair = jnp.where(core == 0, jnp.stack([kv, kv2]), jnp.stack([kv2, kv]))
        far = send(pair, FAR_Y)
        far = jnp.where(core == 0, far, send(far, CORE))
        piece = jnp.where(y_hi == 0, jnp.stack([pair, far]), jnp.stack([far, pair]))
        piece = piece.reshape(2, 2 * kv.shape[0], kv.shape[1])
        piece2 = send(piece, PARTNER)
        share = lax.dynamic_index_in_dim(piece, core, 0, keepdims=False)
        o2 = send(share, X_FAR)
        piece2, o2, w_first = lax.optimization_barrier((piece2, o2, w_query[:cut]))
        t2 = send(piece2, X_FAR)
        w_first = send(w_first, PARTNER)
        return share, o2, piece2, t2, w_first, w_query[cut:]

    def nothing(last_hidden, w_key, w_value, w_query):
        rows = 2 * last_hidden.shape[0]
        cols = 2 * w_key.shape[1]
        few = jnp.zeros((rows, cols), BF)
        more = jnp.zeros((2, rows, cols), BF)
        first, rest = w_query[:cut], w_query[cut:]
        return few, few, more, more, jnp.zeros_like(first), jnp.zeros_like(rest)

    share, o2, piece2, t2, w_q2a, w_rest = lax.cond(
        segment_ids[0] >= 0, cache, nothing, last_hidden, w_key, w_value, w_q
    )
    w_q2b = send(w_rest, PARTNER)
    x_in, x_out, share, piece2 = lax.optimization_barrier((x_in, x_out, share, piece2))
    xo_a = send(x_out[: RB // 2], IN)
    xo_b = send(x_in[RB // 2 :], OUT)
    both = jnp.concatenate([share[None], piece2])
    s1 = send(both, X_PREV)
    s3 = send(both, X_NEXT)
    heads_cols = w_q.shape[1]
    w_o_r = after(w_o, x_in, x_out).reshape(8, heads_cols, width)
    w_o_mine, w_o_theirs = reorder(meta, w_o_r, 0), reorder(meta, w_o_r, 1)
    state = project(meta, [after(x0, x_in, x_out)], query_gain, w_q, 0, width)
    state = project(meta, [x_in], query_gain, w_q, 1, width, state)
    state = project(meta, [x_out], query_gain, w_q, 3, width, state)
    xo_a, xo_b, s1, s3, w_o_mine, w_o_theirs, *state = lax.optimization_barrier(
        (xo_a, xo_b, s1, s3, w_o_mine, w_o_theirs, *state)
    )
    got = jnp.stack([share, s1[0], o2, s3[0]])
    got2 = send(got, CORE)
    kv_own = jnp.where(
        core == 0, jnp.stack([got, got2], axis=1), jnp.stack([got2, got], axis=1)
    )
    kv_other = jnp.stack([piece2, s1[1:], t2, s3[1:]])
    normed, q_own, res_own, res_other = project(
        meta, [xo_a, xo_b], query_gain, w_q, 2, width, state
    )
    (w_q2b, kv_own, kv_other, normed, q_own, seg_col, seg_row, w_o_theirs) = (
        lax.optimization_barrier(
            (w_q2b, kv_own, kv_other, normed, q_own, seg_col, seg_row, w_o_theirs)
        )
    )
    w_o2 = send(w_o_theirs, PARTNER)
    q_other = more_queries(normed, w_q2a, w_q2b)

    result = None
    for chunk in range(2):
        own = attend(meta, chunk, q_own, q_other, kv_own, kv_other, seg_col, seg_row)
        c_in = send(own, IN)
        c_out = send(own, OUT)
        co_a = send(c_out[:RB], IN)
        co_b = send(c_in[RB:], OUT)
        parts = (own, c_in, co_a, co_b, c_out)
        sent = send(finish(meta, chunk, parts, w_o2, res_other, 2), PARTNER)
        result = finish(meta, chunk, parts, w_o_mine, res_own, 8, result)
        result = place(meta, chunk, sent, result)
    return result.reshape(1, 8 * RB, -1)


def solution(mesh):
    return jax.shard_map(
        body,
        mesh=mesh,
        in_specs=(
            P("section", "ctx", None),
            P("section", None),
            P(),
            P("section", None),
            P(None, "ctx"),
            P(None, "ctx"),
            P("section", None, "ctx"),
            P("section", None, "ctx"),
            P(),
        ),
        out_specs=P("section", None, "ctx"),
        check_vma=False,
    )
```

```python
import functools

import jax
import jax.numpy as jnp
from jax import lax
from jax.experimental import pallas as pl
from jax.experimental.pallas import tpu as pltpu
from jax.sharding import PartitionSpec as P

HD = 128
RB = 256
BF = jnp.bfloat16
F32 = jnp.float32
AXES = ("section", "ctx")
MIB = 1 << 20

PLACE = (((0, 1, 2, 3), (4, 5, 6, 7)), ((1, 0, 4, 5), (2, 3, 7, 6)))
SPOT = tuple(
    tuple(next((h, r) for h in range(2) for r in range(4) if table[h][r] == c) for c in range(8))
    for table in PLACE
)

MINE, THEIRS, SLOT, ROWS, OWN, CORE_AT, FIRST, X_AT = 0, 4, 8, 12, 20, 22, 23, 31


def facts_of(core, c):
    half, r = SPOT[core][c]
    mine, theirs = PLACE[core][half], PLACE[core][1 - half]
    ring = [r, r ^ 1, (r + 2) % 4, 3 - r]
    slots = [ring.index(p) for p in range(4)]
    rows = [place[p] for p in ring for place in (mine, theirs)]
    return [*mine, *theirs, *slots, *rows, mine[r], theirs[r], core]


FACTS = [[facts_of(core, c) for c in range(8)] for core in range(2)]


def moves(step):
    pairs = []
    for s in range(16):
        for c in range(8):
            core = s % 2
            half, spot = SPOT[core][c]
            yh, x, k, h, r = step(s // 8, s // 2 % 4, core, half, spot)
            if k == core:
                place = PLACE[core][h][r % 4]
            else:
                place = c
            pairs.append((s * 8 + c, (yh * 8 + x % 4 * 2 + k) * 8 + place))
    return pairs


IN = moves(lambda yh, x, k, h, r: (yh, x, k, h, r ^ 1))
OUT = moves(lambda yh, x, k, h, r: (yh, x, k, h, 3 - r))
PARTNER = moves(lambda yh, x, k, h, r: (yh, x, k, 1 - h, r))
CORE = moves(lambda yh, x, k, h, r: (yh, x, 1 - k, h, r))
FAR_Y = [
    (a, b) for a, b in moves(lambda yh, x, k, h, r: (1 - yh, x, k, h, r)) if a // 8 % 2 == 0
]
X_NEXT = moves(lambda yh, x, k, h, r: (yh, x + 1, k, h, r))
X_PREV = moves(lambda yh, x, k, h, r: (yh, x - 1, k, h, r))
X_FAR = moves(lambda yh, x, k, h, r: (yh, x + 2, k, h, r))


def send(value, pairs):
    return lax.ppermute(value, AXES, pairs)


def normalize(rows, gain):
    full = rows.astype(F32)
    scaled = full * lax.rsqrt(jnp.mean(full * full, axis=-1, keepdims=True) + 1e-05) * gain
    return scaled.astype(BF)


def project_kernel(pieces, meta, *refs):
    xs = refs[:pieces]
    gain, w = refs[pieces : pieces + 2]
    normed, q, res_own, res_other = refs[-4:]
    step = 32
    base = 0
    for x in xs:
        rows = x.shape[0]

        def norm_rows(i, _, x=x, base=base):
            at = pl.multiple_of(i * step, step)
            full = x[pl.ds(at, step), :].astype(F32)
            mean = jnp.mean(full * full, axis=-1, keepdims=True)
            normed[0, pl.ds(base + at, step), :] = (
                full * lax.rsqrt(mean + 1e-05) * gain[...]
            ).astype(BF)
            return 0

        lax.fori_loop(0, rows // step, norm_rows, 0)
        width = res_own.shape[2]
        for k, out in ((0, res_own), (1, res_other)):
            first = pl.multiple_of(meta[OWN + k] * width, 128)
            out[0, base : base + rows, :] = x[:, pl.ds(first, width)]
        base += rows
    q[0] = jnp.dot(normed[0], w[...], preferred_element_type=F32).astype(BF)


def project(meta, xs, gain, w, slot, width, prior=None):
    d, n = w.shape
    shapes = [(4, RB, d), (4, RB, n), (4, RB, width), (4, RB, width)]
    whole = lambda a: pl.BlockSpec(a.shape, lambda i, m, nd=a.ndim: (0,) * nd)
    ins = list(xs) + [gain, w]
    specs = [whole(a) for a in ins]
    aliases = {}
    for k, a in enumerate(prior or ()):
        aliases[1 + len(ins)] = k
        ins.append(a)
        specs.append(pl.BlockSpec(memory_space=pl.ANY))

    def kernel(meta, *refs):
        project_kernel(len(xs), meta, *refs)

    return pl.pallas_call(
        kernel,
        grid_spec=pltpu.PrefetchScalarGridSpec(
            num_scalar_prefetch=1,
            grid=(1,),
            in_specs=specs,
            out_specs=[pl.BlockSpec((1,) + s[1:], lambda i, m: (slot, 0, 0)) for s in shapes],
        ),
        out_shape=[jax.ShapeDtypeStruct(s, BF) for s in shapes],
        input_output_aliases=aliases,
        compiler_params=pltpu.CompilerParams(vmem_limit_bytes=56 * MIB),
        cost_estimate=pl.CostEstimate(
            flops=2 * RB * d * n, bytes_accessed=2 * (3 * RB * d + d * n), transcendentals=0
        ),
    )(meta, *ins)


def more_queries_kernel(n_ref, wa_ref, wb_ref, q_ref):
    k = wa_ref.shape[0]
    q = jnp.dot(n_ref[:, :k], wa_ref[...], preferred_element_type=F32)
    q += jnp.dot(n_ref[:, k:], wb_ref[...], preferred_element_type=F32)
    q_ref[...] = q.astype(BF)


def more_queries(normed, wa, wb):
    d, n = normed.shape[2], wa.shape[1]
    rows = 2 * RB
    return pl.pallas_call(
        more_queries_kernel,
        grid=(2,),
        in_specs=[
            pl.BlockSpec((rows, d), lambda i: (i, 0)),
            pl.BlockSpec(wa.shape, lambda i: (0, 0)),
            pl.BlockSpec(wb.shape, lambda i: (0, 0)),
        ],
        out_specs=pl.BlockSpec((rows, n), lambda i: (i, 0)),
        out_shape=jax.ShapeDtypeStruct((4 * RB, n), BF),
        compiler_params=pltpu.CompilerParams(vmem_limit_bytes=56 * MIB),
        cost_estimate=pl.CostEstimate(
            flops=8 * RB * d * n, bytes_accessed=2 * (4 * RB * d + d * n), transcendentals=0
        ),
    )(normed.reshape(4 * RB, d), wa, wb).reshape(4, RB, n)


def attend_kernel(
    chunk, meta, q_own, q_other, seg_col, seg_row, own0, o2, o2b, s1, s1b, s3, s3b, other0, t2,
    out, kv, scores, tops, sums, sems,
):
    t = pl.program_id(0)
    core = meta[CORE_AT]
    copies = [
        pltpu.make_async_copy(src, dst, sems.at[i])
        for i, (src, dst) in enumerate((
            (own0, kv.at[0, 0]),
            (s1.at[0], kv.at[0, 1, core]),
            (s1b.at[0], kv.at[0, 1, 1 - core]),
            (o2, kv.at[0, 2, core]),
            (o2b, kv.at[0, 2, 1 - core]),
            (s3.at[0], kv.at[0, 3, core]),
            (s3b.at[0], kv.at[0, 3, 1 - core]),
            (other0, kv.at[1, 0]),
            (s1.at[1:3], kv.at[1, 1]),
            (t2, kv.at[1, 2]),
            (s3.at[1:3], kv.at[1, 3]),
        ))
    ]

    @pl.when(t == 0)
    def _():
        for copy in copies:
            copy.start()
        for copy in copies:
            copy.wait()

    block = meta[MINE + 2 * chunk + t]
    first = meta[FIRST + block]
    count = block - first + 1
    x = meta[X_AT]
    heads = q_own.shape[2] // HD
    factor = HD ** (-0.5) * 1.4426950408889634
    pairs = [(src, i) for src in range(2) for i in range(heads)]
    qs = (q_own, q_other)

    def place(i):
        kb = first + i
        j = lax.rem(lax.rem(kb, 4) - x + 4, 4)
        return kb, j, kb // 4

    tops[...] = jnp.full(tops.shape, -1e30, F32)
    sums[...] = jnp.zeros(sums.shape, F32)
    q_doc = seg_col[block]
    row_at = block * RB + lax.broadcasted_iota(jnp.int32, (RB, RB), 0)
    col_at = lax.broadcasted_iota(jnp.int32, (RB, RB), 1)

    def score(i, _):
        kb, j, y = place(i)
        visible = (q_doc == seg_row[kb]) & (kb * RB + col_at <= row_at)
        for n, (src, h) in enumerate(pairs):
            cols = slice(h * HD, (h + 1) * HD)
            s = lax.dot_general(
                qs[src][0, :, cols], kv[src, j, y, :, cols], (((1,), (1,)), ((), ())),
                preferred_element_type=F32,
            )
            s = jnp.where(visible, s, -1e30)
            scores[n, i] = s
            tops[n] = jnp.maximum(tops[n], jnp.maximum(s[:, :HD], s[:, HD:]))
        return 0

    lax.fori_loop(0, count, score, 0)
    for n in range(len(pairs)):
        tops[n] = jnp.broadcast_to(jnp.max(tops[n], axis=-1, keepdims=True), (RB, HD))

    def expo(i, _):
        for n in range(len(pairs)):
            s = scores[n, i]
            top = tops[n]
            left = jnp.exp2((s[:, :HD] - top) * factor)
            right = jnp.exp2((s[:, HD:] - top) * factor)
            scores[n, i, :, :HD] = left
            scores[n, i, :, HD:] = right
            sums[n] += left + right
        return 0

    lax.fori_loop(0, count, expo, 0)
    for n in range(len(pairs)):
        total = jnp.sum(sums[n], axis=-1, keepdims=True)
        sums[n] = jnp.broadcast_to(1.0 / total, (RB, HD))
        tops[n] = jnp.zeros((RB, HD), F32)

    def mix(i, _):
        kb, j, y = place(i)
        for n, (src, h) in enumerate(pairs):
            cols = slice((heads + h) * HD, (heads + h + 1) * HD)
            e = scores[n, i]
            inv = sums[n]
            weights = jnp.concatenate([e[:, :HD] * inv, e[:, HD:] * inv], axis=1).astype(BF)
            tops[n] += jnp.dot(weights, kv[src, j, y, :, cols], preferred_element_type=F32)
        return 0

    lax.fori_loop(0, count, mix, 0)
    for n in range(len(pairs)):
        out[:, n * HD : (n + 1) * HD] = tops[n].astype(BF)


def attend(meta, chunk, q_own, q_other, seg_col, seg_row, pieces):
    n = q_own.shape[2]
    heads = n // HD
    whole = lambda a: pl.BlockSpec(a.shape, lambda t, m, nd=a.ndim: (0,) * nd)
    q_spec = pl.BlockSpec((1, RB, n), lambda t, m: (m[SLOT + 2 * chunk + t], 0, 0))
    in_place = pl.BlockSpec(memory_space=pl.ANY)
    return pl.pallas_call(
        functools.partial(attend_kernel, chunk),
        grid_spec=pltpu.PrefetchScalarGridSpec(
            num_scalar_prefetch=1,
            grid=(2,),
            in_specs=[q_spec, q_spec, whole(seg_col), whole(seg_row)] + [in_place] * len(pieces),
            out_specs=pl.BlockSpec((RB, 2 * n), lambda t, m: (t, 0)),
            scratch_shapes=[
                pltpu.VMEM((2, 4, 2, RB, 2 * n), BF),
                pltpu.VMEM((2 * heads, 5, RB, RB), F32),
                pltpu.VMEM((2 * heads, RB, HD), F32),
                pltpu.VMEM((2 * heads, RB, HD), F32),
                pltpu.SemaphoreType.DMA((11,)),
            ],
        ),
        out_shape=jax.ShapeDtypeStruct((2 * RB, 2 * n), BF),
        compiler_params=pltpu.CompilerParams(vmem_limit_bytes=56 * MIB),
        cost_estimate=pl.CostEstimate(
            flops=4 * 2 * RB * 768 * 2 * n, bytes_accessed=8 * MIB, transcendentals=2 * RB * 768 * 6
        ),
    )(meta, q_own, q_other, seg_col, seg_row, *pieces)


def reorder_kernel(meta, w, out):
    out[...] = w[...]


def reorder(meta, w, swap):
    k8, n, width = w.shape
    return pl.pallas_call(
        reorder_kernel,
        grid_spec=pltpu.PrefetchScalarGridSpec(
            num_scalar_prefetch=1,
            grid=(k8,),
            in_specs=[
                pl.BlockSpec((1, n, width), lambda k, m: (m[ROWS + (k + swap - 2 * swap * (k % 2))], 0, 0))
            ],
            out_specs=pl.BlockSpec((1, n, width), lambda k, m: (k, 0, 0)),
        ),
        out_shape=jax.ShapeDtypeStruct(w.shape, BF),
    )(meta, w).reshape(k8 * n, width)


def finish_kernel(chunk, blocks, meta, c0, c1, c2a, c2b, c3, w, res, *refs):
    out, cs, ws, rs, outs, c_sems, w_sems, r_sems, out_sems = refs[-9:]
    n = cs.shape[2]
    copy = pltpu.make_async_copy
    c_copies = [
        [copy(c0, cs.at[0], c_sems.at[0])],
        [copy(c1, cs.at[1], c_sems.at[1])],
        [copy(c3, cs.at[2], c_sems.at[2])],
        [
            copy(c2a, cs.at[3, 0:RB], c_sems.at[3]),
            copy(c2b, cs.at[3, RB : 2 * RB], c_sems.at[4]),
        ],
    ]
    at = (0, 1, 3, 2)
    w_copies = [
        copy(w.at[at[j] * n : (at[j] + 1) * n], ws.at[j], w_sems.at[j]) for j in range(4)
    ]
    r_copies = [
        copy(res.at[meta[SLOT + 2 * chunk + t]], rs.at[t * RB : (t + 1) * RB], r_sems.at[t])
        for t in range(2)
    ]
    for j in range(4):
        for one in (*c_copies[j], w_copies[j]):
            one.start()
    for one in r_copies:
        one.start()
    total = None
    for j in range(4):
        for one in (*c_copies[j], w_copies[j]):
            one.wait()
        part = jnp.dot(cs[j], ws[j], preferred_element_type=F32)
        total = part if total is None else total + part
    for one in r_copies:
        one.wait()
    outs[...] = (rs[...].astype(F32) + total).astype(BF)
    targets = [t if blocks == 2 else meta[MINE + 2 * chunk + t] for t in range(2)]
    out_copies = [
        copy(outs.at[t * RB : (t + 1) * RB], out.at[targets[t]], out_sems.at[t]) for t in range(2)
    ]
    for one in out_copies:
        one.start()
    for one in out_copies:
        one.wait()


def finish(meta, chunk, parts, w, res, blocks, prior=None):
    depth, width = w.shape
    n = depth // 4
    ins = list(parts) + [w, res]
    aliases = {}
    if prior is not None:
        aliases[1 + len(ins)] = 0
        ins.append(prior)
    in_place = pl.BlockSpec(memory_space=pl.ANY)
    return pl.pallas_call(
        functools.partial(finish_kernel, chunk, blocks),
        grid_spec=pltpu.PrefetchScalarGridSpec(
            num_scalar_prefetch=1,
            grid=(1,),
            in_specs=[in_place] * len(ins),
            out_specs=in_place,
            scratch_shapes=[
                pltpu.VMEM((4, 2 * RB, n), BF),
                pltpu.VMEM((4, n, width), BF),
                pltpu.VMEM((2 * RB, width), BF),
                pltpu.VMEM((2 * RB, width), BF),
                pltpu.SemaphoreType.DMA((5,)),
                pltpu.SemaphoreType.DMA((4,)),
                pltpu.SemaphoreType.DMA((2,)),
                pltpu.SemaphoreType.DMA((2,)),
            ],
        ),
        out_shape=jax.ShapeDtypeStruct((blocks, RB, width), BF),
        input_output_aliases=aliases,
        compiler_params=pltpu.CompilerParams(vmem_limit_bytes=56 * MIB),
        cost_estimate=pl.CostEstimate(
            flops=4 * RB * depth * width, bytes_accessed=8 * MIB, transcendentals=0
        ),
    )(meta, *ins)


def place_kernel(chunk, meta, got, prior, out, sems):
    copies = [
        pltpu.make_async_copy(got.at[t], out.at[meta[THEIRS + 2 * chunk + t]], sems.at[t])
        for t in range(2)
    ]
    for copy in copies:
        copy.start()
    for copy in copies:
        copy.wait()


def place(meta, chunk, got, prior):
    in_place = pl.BlockSpec(memory_space=pl.ANY)
    return pl.pallas_call(
        functools.partial(place_kernel, chunk),
        grid_spec=pltpu.PrefetchScalarGridSpec(
            num_scalar_prefetch=1,
            grid=(1,),
            in_specs=[in_place, in_place],
            out_specs=in_place,
            scratch_shapes=[pltpu.SemaphoreType.DMA((2,))],
        ),
        out_shape=jax.ShapeDtypeStruct(prior.shape, BF),
        input_output_aliases={2: 0},
        compiler_params=pltpu.CompilerParams(vmem_limit_bytes=56 * MIB),
    )(meta, got, prior)


def after(value, *done):
    return lax.optimization_barrier((value,) + done)[0]


def body(
    section_input, last_hidden, kv_gain, query_gain, w_key, w_value, w_query, w_out, segment_ids
):
    section = lax.axis_index("section")
    c = lax.axis_index("ctx")
    core = section % 2
    y_hi = section // 8
    x0 = section_input[0]
    w_q = w_query[0]
    w_o = w_out[0]
    width = w_o.shape[1]

    x_in = send(x0, IN)
    x_out = send(x0, OUT)
    cut = w_q.shape[0] * 2 // 5

    ids = segment_ids.reshape(8, RB)
    starts = jnp.sum(segment_ids[None, :] < ids[:, :1], axis=1, dtype=jnp.int32) // RB
    starts = jnp.maximum(starts, jnp.arange(8, dtype=jnp.int32) - 4)
    facts = jnp.array(FACTS, jnp.int32)[core, c]
    meta = jnp.concatenate([facts, starts, (section // 2 % 4)[None]])
    seg_col = segment_ids.reshape(8, RB, 1)
    seg_row = segment_ids.reshape(8, 1, RB)

    def cache(last_hidden, w_key, w_value, w_query, w_out):
        kv_in = normalize(last_hidden, kv_gain)
        own_k = jnp.dot(kv_in, w_key, preferred_element_type=F32).astype(BF)
        own_v = jnp.dot(kv_in, w_value, preferred_element_type=F32).astype(BF)
        kv = jnp.concatenate([own_k, own_v], axis=1)
        kv2 = send(kv, CORE)
        pair = jnp.where(core == 0, jnp.stack([kv, kv2]), jnp.stack([kv2, kv]))
        far = send(pair, FAR_Y)
        far = jnp.where(core == 0, far, send(far, CORE))
        piece = jnp.where(y_hi == 0, jnp.stack([pair, far]), jnp.stack([far, pair]))
        piece = piece.reshape(2, 2 * kv.shape[0], kv.shape[1])
        w_mine = reorder(meta, w_out, 0)
        piece2 = send(piece, PARTNER)
        share = lax.dynamic_index_in_dim(piece, core, 0, keepdims=False)
        o2 = send(share, X_FAR)
        piece2, o2, w_first, w_mine = lax.optimization_barrier(
            (piece2, o2, w_query[:cut], w_mine)
        )
        t2 = send(piece2, X_FAR)
        w_first = send(w_first, PARTNER)
        o2b = send(o2, CORE)
        both = jnp.concatenate([share[None], piece2])
        w_theirs = reorder(meta, w_out, 1)
        return piece, o2, o2b, piece2, t2, both, w_first, w_query[cut:], w_mine, w_theirs

    def nothing(last_hidden, w_key, w_value, w_query, w_out):
        rows = 2 * last_hidden.shape[0]
        cols = 2 * w_key.shape[1]
        one, two, three = (jnp.zeros((k, rows, cols), BF) for k in (1, 2, 3))
        first, rest = w_query[:cut], w_query[cut:]
        w_none = jnp.zeros((w_out.shape[0] * w_out.shape[1], w_out.shape[2]), BF)
        return (
            two, one[0], one[0], two, two, three, jnp.zeros_like(first), jnp.zeros_like(rest),
            w_none, w_none,
        )

    w_o_r = w_o.reshape(8, w_q.shape[1], width)
    piece, o2, o2b, piece2, t2, both, w_q2a, w_rest, w_o_mine, w_o_theirs = lax.cond(
        segment_ids[0] >= 0, cache, nothing, last_hidden, w_key, w_value, w_q, w_o_r
    )
    w_q2b = send(w_rest, PARTNER)
    x_in, x_out, both = lax.optimization_barrier((x_in, x_out, both))
    xo_a = send(x_out[: RB // 2], IN)
    xo_b = send(x_in[RB // 2 :], OUT)
    s1 = send(both, X_PREV)
    s3 = send(both, X_NEXT)
    state = project(meta, [after(x0, x_in, x_out)], query_gain, w_q, 0, width)
    state = project(meta, [x_in], query_gain, w_q, 1, width, state)
    state = project(meta, [x_out], query_gain, w_q, 3, width, state)
    xo_a, xo_b, s1, s3, *state = lax.optimization_barrier((xo_a, xo_b, s1, s3, *state))
    s1b = send(s1, CORE)
    s3b = send(s3, CORE)
    normed, q_own, res_own, res_other = project(
        meta, [xo_a, xo_b], query_gain, w_q, 2, width, state
    )
    w_q2b, s1b, s3b, normed, q_own, seg_col, seg_row, w_o_theirs = lax.optimization_barrier(
        (w_q2b, s1b, s3b, normed, q_own, seg_col, seg_row, w_o_theirs)
    )
    w_o2 = send(w_o_theirs, PARTNER)
    q_other = more_queries(normed, w_q2a, w_q2b)
    pieces = (piece, o2, o2b, s1, s1b, s3, s3b, piece2, t2)

    result = None
    for chunk in range(2):
        own = attend(meta, chunk, q_own, q_other, seg_col, seg_row, pieces)
        c_in = send(own, IN)
        c_out = send(own, OUT)
        co_a = send(c_out[:RB], IN)
        co_b = send(c_in[RB:], OUT)
        parts = (own, c_in, co_a, co_b, c_out)
        sent = send(finish(meta, chunk, parts, w_o2, res_other, 2), PARTNER)
        result = finish(meta, chunk, parts, w_o_mine, res_own, 8, result)
        result = place(meta, chunk, sent, result)
    return result.reshape(1, 8 * RB, -1)


def solution(mesh):
    return jax.shard_map(
        body,
        mesh=mesh,
        in_specs=(
            P("section", "ctx", None),
            P("section", None),
            P(),
            P("section", None),
            P(None, "ctx"),
            P(None, "ctx"),
            P("section", None, "ctx"),
            P("section", None, "ctx"),
            P(),
        ),
        out_specs=P("section", None, "ctx"),
        check_vma=False,
    )
```

```python
import functools

import jax
import jax.numpy as jnp
from jax import lax
from jax.experimental import pallas as pl
from jax.experimental.pallas import tpu as pltpu
from jax.sharding import PartitionSpec as P

HD = 128
RB = 256
BF = jnp.bfloat16
F32 = jnp.float32
AXES = ("section", "ctx")
MIB = 1 << 20

PLACE = (((0, 1, 2, 3), (4, 5, 6, 7)), ((1, 0, 4, 5), (2, 3, 7, 6)))
SPOT = tuple(
    tuple(next((h, r) for h in range(2) for r in range(4) if table[h][r] == c) for c in range(8))
    for table in PLACE
)

MINE, THEIRS, SLOT, ROWS, OWN, CORE_AT, FIRST, X_AT = 0, 4, 8, 12, 20, 22, 23, 31


def facts_of(core, c):
    half, r = SPOT[core][c]
    mine, theirs = PLACE[core][half], PLACE[core][1 - half]
    ring = [r, r ^ 1, (r + 2) % 4, 3 - r]
    slots = [ring.index(p) for p in range(4)]
    rows = [place[p] for p in ring for place in (mine, theirs)]
    return [*mine, *theirs, *slots, *rows, mine[r], theirs[r], core]


FACTS = [[facts_of(core, c) for c in range(8)] for core in range(2)]


def moves(step):
    pairs = []
    for s in range(16):
        for c in range(8):
            core = s % 2
            half, spot = SPOT[core][c]
            yh, x, k, h, r = step(s // 8, s // 2 % 4, core, half, spot)
            if k == core:
                place = PLACE[core][h][r % 4]
            else:
                place = c
            pairs.append((s * 8 + c, (yh * 8 + x % 4 * 2 + k) * 8 + place))
    return pairs


IN = moves(lambda yh, x, k, h, r: (yh, x, k, h, r ^ 1))
OUT = moves(lambda yh, x, k, h, r: (yh, x, k, h, 3 - r))
PARTNER = moves(lambda yh, x, k, h, r: (yh, x, k, 1 - h, r))
CORE = moves(lambda yh, x, k, h, r: (yh, x, 1 - k, h, r))
FAR_Y = [
    (a, b) for a, b in moves(lambda yh, x, k, h, r: (1 - yh, x, k, h, r)) if a // 8 % 2 == 0
]
X_NEXT = moves(lambda yh, x, k, h, r: (yh, x + 1, k, h, r))
X_PREV = moves(lambda yh, x, k, h, r: (yh, x - 1, k, h, r))
X_FAR = moves(lambda yh, x, k, h, r: (yh, x + 2, k, h, r))


def send(value, pairs):
    return lax.ppermute(value, AXES, pairs)


def normalize(rows, gain):
    full = rows.astype(F32)
    scaled = full * lax.rsqrt(jnp.mean(full * full, axis=-1, keepdims=True) + 1e-05) * gain
    return scaled.astype(BF)


def project_kernel(pieces, meta, *refs):
    xs = refs[:pieces]
    gain, w = refs[pieces : pieces + 2]
    normed, q, res_own, res_other = refs[-4:]
    step = 32
    base = 0
    for x in xs:
        rows = x.shape[0]

        def norm_rows(i, _, x=x, base=base):
            at = pl.multiple_of(i * step, step)
            full = x[pl.ds(at, step), :].astype(F32)
            mean = jnp.mean(full * full, axis=-1, keepdims=True)
            normed[0, pl.ds(base + at, step), :] = (
                full * lax.rsqrt(mean + 1e-05) * gain[...]
            ).astype(BF)
            return 0

        lax.fori_loop(0, rows // step, norm_rows, 0)
        width = res_own.shape[2]
        for k, out in ((0, res_own), (1, res_other)):
            first = pl.multiple_of(meta[OWN + k] * width, 128)
            out[0, base : base + rows, :] = x[:, pl.ds(first, width)]
        base += rows
    q[0] = jnp.dot(normed[0], w[...], preferred_element_type=F32).astype(BF)


def project(meta, xs, gain, w, slot, width, prior=None):
    d, n = w.shape
    shapes = [(4, RB, d), (4, RB, n), (4, RB, width), (4, RB, width)]
    whole = lambda a: pl.BlockSpec(
        a.shape, lambda i, m, nd=a.ndim: (0,) * nd, pipeline_mode=pl.Buffered(1)
    )
    ins = list(xs) + [gain, w]
    specs = [whole(a) for a in ins]
    aliases = {}
    for k, a in enumerate(prior or ()):
        aliases[1 + len(ins)] = k
        ins.append(a)
        specs.append(pl.BlockSpec(memory_space=pl.ANY))

    def kernel(meta, *refs):
        project_kernel(len(xs), meta, *refs)

    return pl.pallas_call(
        kernel,
        grid_spec=pltpu.PrefetchScalarGridSpec(
            num_scalar_prefetch=1,
            grid=(1,),
            in_specs=specs,
            out_specs=[pl.BlockSpec((1,) + s[1:], lambda i, m: (slot, 0, 0)) for s in shapes],
        ),
        out_shape=[jax.ShapeDtypeStruct(s, BF) for s in shapes],
        input_output_aliases=aliases,
        compiler_params=pltpu.CompilerParams(vmem_limit_bytes=20 * MIB),
        cost_estimate=pl.CostEstimate(
            flops=2 * RB * d * n, bytes_accessed=2 * (3 * RB * d + d * n), transcendentals=0
        ),
    )(meta, *ins)


def more_queries_kernel(n_ref, wa_ref, wb_ref, q_ref):
    k = wa_ref.shape[0]
    q = jnp.dot(n_ref[:, :k], wa_ref[...], preferred_element_type=F32)
    q += jnp.dot(n_ref[:, k:], wb_ref[...], preferred_element_type=F32)
    q_ref[...] = q.astype(BF)


def more_queries(normed, wa, wb):
    d, n = normed.shape[2], wa.shape[1]
    rows = 2 * RB
    return pl.pallas_call(
        more_queries_kernel,
        grid=(2,),
        in_specs=[
            pl.BlockSpec((rows, d), lambda i: (i, 0)),
            pl.BlockSpec(wa.shape, lambda i: (0, 0), pipeline_mode=pl.Buffered(1)),
            pl.BlockSpec(wb.shape, lambda i: (0, 0), pipeline_mode=pl.Buffered(1)),
        ],
        out_specs=pl.BlockSpec((rows, n), lambda i: (i, 0)),
        out_shape=jax.ShapeDtypeStruct((4 * RB, n), BF),
        compiler_params=pltpu.CompilerParams(vmem_limit_bytes=20 * MIB),
        cost_estimate=pl.CostEstimate(
            flops=8 * RB * d * n, bytes_accessed=2 * (4 * RB * d + d * n), transcendentals=0
        ),
    )(normed.reshape(4 * RB, d), wa, wb).reshape(4, RB, n)


def attend_kernel(
    chunk, meta, q_own, q_other, seg_row, own0, o2, o2b, s1, s1b, s3, s3b, other0, t2,
    out, kv, scores, tops, sums,
):
    t = pl.program_id(0)
    core = meta[CORE_AT]

    @pl.when(t == 0)
    def _():
        kv[0, 0] = own0[...]
        kv[0, 1, core] = s1[0]
        kv[0, 1, 1 - core] = s1b[0]
        kv[0, 2, core] = o2[...]
        kv[0, 2, 1 - core] = o2b[...]
        kv[0, 3, core] = s3[0]
        kv[0, 3, 1 - core] = s3b[0]
        kv[1, 0] = other0[...]
        kv[1, 1] = s1[1:3]
        kv[1, 2] = t2[...]
        kv[1, 3] = s3[1:3]

    block = meta[MINE + 2 * chunk + t]
    first = meta[FIRST + block]
    count = block - first + 1
    x = meta[X_AT]
    heads = q_own.shape[2] // HD
    factor = HD ** (-0.5) * 1.4426950408889634
    pairs = [(src, i) for src in range(2) for i in range(heads)]
    qs = (q_own, q_other)

    def place(i):
        kb = first + i
        j = lax.rem(lax.rem(kb, 4) - x + 4, 4)
        return kb, j, kb // 4

    tops[...] = jnp.full(tops.shape, -1e30, F32)
    sums[...] = jnp.zeros(sums.shape, F32)
    q_doc = jnp.transpose(jnp.broadcast_to(seg_row[block], (RB, RB)))
    row_at = block * RB + lax.broadcasted_iota(jnp.int32, (RB, RB), 0)
    col_at = lax.broadcasted_iota(jnp.int32, (RB, RB), 1)

    def score(i, _):
        kb, j, y = place(i)
        visible = (q_doc == seg_row[kb]) & (kb * RB + col_at <= row_at)
        for n, (src, h) in enumerate(pairs):
            cols = slice(h * HD, (h + 1) * HD)
            s = lax.dot_general(
                qs[src][0, :, cols], kv[src, j, y, :, cols], (((1,), (1,)), ((), ())),
                preferred_element_type=F32,
            )
            s = jnp.where(visible, s, -1e30)
            scores[n, i] = s
            tops[n] = jnp.maximum(tops[n], jnp.maximum(s[:, :HD], s[:, HD:]))
        return 0

    lax.fori_loop(0, count, score, 0)
    for n in range(len(pairs)):
        tops[n] = jnp.broadcast_to(jnp.max(tops[n], axis=-1, keepdims=True), (RB, HD))

    def expo(i, _):
        for n in range(len(pairs)):
            s = scores[n, i]
            top = tops[n]
            left = jnp.exp2((s[:, :HD] - top) * factor)
            right = jnp.exp2((s[:, HD:] - top) * factor)
            scores[n, i, :, :HD] = left
            scores[n, i, :, HD:] = right
            sums[n] += left + right
        return 0

    lax.fori_loop(0, count, expo, 0)
    for n in range(len(pairs)):
        total = jnp.sum(sums[n], axis=-1, keepdims=True)
        sums[n] = jnp.broadcast_to(1.0 / total, (RB, HD))
        tops[n] = jnp.zeros((RB, HD), F32)

    def mix(i, _):
        kb, j, y = place(i)
        for n, (src, h) in enumerate(pairs):
            cols = slice((heads + h) * HD, (heads + h + 1) * HD)
            e = scores[n, i]
            inv = sums[n]
            weights = jnp.concatenate([e[:, :HD] * inv, e[:, HD:] * inv], axis=1).astype(BF)
            tops[n] += jnp.dot(weights, kv[src, j, y, :, cols], preferred_element_type=F32)
        return 0

    lax.fori_loop(0, count, mix, 0)
    for n in range(len(pairs)):
        out[:, n * HD : (n + 1) * HD] = tops[n].astype(BF)


def attend(meta, chunk, q_own, q_other, seg_row, pieces):
    n = q_own.shape[2]
    heads = n // HD
    whole = lambda a: pl.BlockSpec(a.shape, lambda t, m, nd=a.ndim: (0,) * nd)
    q_spec = pl.BlockSpec((1, RB, n), lambda t, m: (m[SLOT + 2 * chunk + t], 0, 0))
    once = lambda a, size: pl.BlockSpec(
        (size,) + a.shape[1:], lambda t, m, nd=a.ndim: (0,) * nd, pipeline_mode=pl.Buffered(1)
    )
    sizes = [a.shape[0] for a in pieces]
    sizes[4] = sizes[6] = 1
    return pl.pallas_call(
        functools.partial(attend_kernel, chunk),
        grid_spec=pltpu.PrefetchScalarGridSpec(
            num_scalar_prefetch=1,
            grid=(2,),
            in_specs=[q_spec, q_spec, whole(seg_row)] + list(map(once, pieces, sizes)),
            out_specs=pl.BlockSpec((RB, 2 * n), lambda t, m: (t, 0)),
            scratch_shapes=[
                pltpu.VMEM((2, 4, 2, RB, 2 * n), BF),
                pltpu.VMEM((2 * heads, 5, RB, RB), F32),
                pltpu.VMEM((2 * heads, RB, HD), F32),
                pltpu.VMEM((2 * heads, RB, HD), F32),
            ],
        ),
        out_shape=jax.ShapeDtypeStruct((2 * RB, 2 * n), BF),
        compiler_params=pltpu.CompilerParams(vmem_limit_bytes=32 * MIB),
        cost_estimate=pl.CostEstimate(
            flops=4 * 2 * RB * 768 * 2 * n, bytes_accessed=8 * MIB, transcendentals=2 * RB * 768 * 6
        ),
    )(meta, q_own, q_other, seg_row, *pieces)


def reorder_kernel(meta, w, out):
    out[...] = w[...]


def reorder(meta, w, swap):
    k8, n, width = w.shape
    return pl.pallas_call(
        reorder_kernel,
        grid_spec=pltpu.PrefetchScalarGridSpec(
            num_scalar_prefetch=1,
            grid=(k8,),
            in_specs=[
                pl.BlockSpec((1, n, width), lambda k, m: (m[ROWS + (k + swap - 2 * swap * (k % 2))], 0, 0))
            ],
            out_specs=pl.BlockSpec((1, n, width), lambda k, m: (k, 0, 0)),
        ),
        out_shape=jax.ShapeDtypeStruct(w.shape, BF),
    )(meta, w).reshape(k8 * n, width)


def finish_kernel(meta, c0, c1, c2a, c2b, c3, w, res, *refs):
    out = refs[-1]
    t = pl.program_id(0)
    far = jnp.where(t == 0, c2a[...], c2b[...])
    n = far.shape[1]
    total = res[0].astype(F32)
    for j, c in enumerate((c0[...], c1[...], far, c3[...])):
        total += jnp.dot(c, w[j * n : (j + 1) * n, :], preferred_element_type=F32)
    out[0] = total.astype(BF)


def finish(meta, chunk, parts, w, res, blocks, prior=None):
    depth, width = w.shape
    n = depth // 4
    tile = pl.BlockSpec((RB, n), lambda t, m: (t, 0))
    fixed = pl.BlockSpec((RB, n), lambda t, m: (0, 0))
    ins = list(parts) + [w, res]
    specs = [tile, tile, fixed, fixed, tile]
    specs.append(pl.BlockSpec(w.shape, lambda t, m: (0, 0), pipeline_mode=pl.Buffered(1)))
    specs.append(pl.BlockSpec((1, RB, width), lambda t, m: (m[SLOT + 2 * chunk + t], 0, 0)))
    aliases = {}
    if prior is not None:
        aliases[1 + len(ins)] = 0
        ins.append(prior)
        specs.append(pl.BlockSpec(memory_space=pl.ANY))
    if blocks == 2:
        target = lambda t, m: (t, 0, 0)
    else:
        target = lambda t, m: (m[MINE + 2 * chunk + t], 0, 0)
    return pl.pallas_call(
        finish_kernel,
        grid_spec=pltpu.PrefetchScalarGridSpec(
            num_scalar_prefetch=1,
            grid=(2,),
            in_specs=specs,
            out_specs=pl.BlockSpec((1, RB, width), target),
        ),
        out_shape=jax.ShapeDtypeStruct((blocks, RB, width), BF),
        input_output_aliases=aliases,
        compiler_params=pltpu.CompilerParams(vmem_limit_bytes=20 * MIB),
        cost_estimate=pl.CostEstimate(
            flops=4 * RB * depth * width, bytes_accessed=8 * MIB, transcendentals=0
        ),
    )(meta, *ins)


def place_kernel(chunk, meta, got, prior, out, sems):
    copies = [
        pltpu.make_async_copy(got.at[t], out.at[meta[THEIRS + 2 * chunk + t]], sems.at[t])
        for t in range(2)
    ]
    for copy in copies:
        copy.start()
    for copy in copies:
        copy.wait()


def place(meta, chunk, got, prior):
    in_place = pl.BlockSpec(memory_space=pl.ANY)
    return pl.pallas_call(
        functools.partial(place_kernel, chunk),
        grid_spec=pltpu.PrefetchScalarGridSpec(
            num_scalar_prefetch=1,
            grid=(1,),
            in_specs=[pl.BlockSpec(got.shape, lambda t, m: (0, 0, 0)), in_place],
            out_specs=in_place,
            scratch_shapes=[pltpu.SemaphoreType.DMA((2,))],
        ),
        out_shape=jax.ShapeDtypeStruct(prior.shape, BF),
        input_output_aliases={2: 0},
        compiler_params=pltpu.CompilerParams(vmem_limit_bytes=4 * MIB),
    )(meta, got, prior)


def after(value, *done):
    return lax.optimization_barrier((value,) + done)[0]


def body(
    section_input, last_hidden, kv_gain, query_gain, w_key, w_value, w_query, w_out, segment_ids
):
    section = lax.axis_index("section")
    c = lax.axis_index("ctx")
    core = section % 2
    y_hi = section // 8
    x0 = section_input[0]
    w_q = w_query[0]
    w_o = w_out[0]
    width = w_o.shape[1]

    x_in = send(x0, IN)
    x_out = send(x0, OUT)
    cut = w_q.shape[0] * 2 // 5

    ids = segment_ids.reshape(8, RB)
    starts = jnp.sum(segment_ids[None, :] < ids[:, :1], axis=1, dtype=jnp.int32) // RB
    starts = jnp.maximum(starts, jnp.arange(8, dtype=jnp.int32) - 4)
    facts = jnp.array(FACTS, jnp.int32)[core, c]
    meta = jnp.concatenate([facts, starts, (section // 2 % 4)[None]])
    seg_row = segment_ids.reshape(8, 1, RB)

    def cache(last_hidden, w_key, w_value, w_query, w_out):
        kv_in = normalize(last_hidden, kv_gain)
        own_k = jnp.dot(kv_in, w_key, preferred_element_type=F32).astype(BF)
        own_v = jnp.dot(kv_in, w_value, preferred_element_type=F32).astype(BF)
        kv = jnp.concatenate([own_k, own_v], axis=1)
        kv2 = send(kv, CORE)
        pair = jnp.where(core == 0, jnp.stack([kv, kv2]), jnp.stack([kv2, kv]))
        far = send(pair, FAR_Y)
        far = jnp.where(core == 0, far, send(far, CORE))
        piece = jnp.where(y_hi == 0, jnp.stack([pair, far]), jnp.stack([far, pair]))
        piece = piece.reshape(2, 2 * kv.shape[0], kv.shape[1])
        w_mine = reorder(meta, w_out, 0)
        piece2 = send(piece, PARTNER)
        share = lax.dynamic_index_in_dim(piece, core, 0, keepdims=False)
        o2 = send(share, X_FAR)
        piece2, o2, w_first, w_mine = lax.optimization_barrier(
            (piece2, o2, w_query[:cut], w_mine)
        )
        t2 = send(piece2, X_FAR)
        w_first = send(w_first, PARTNER)
        o2b = send(o2, CORE)
        both = jnp.concatenate([share[None], piece2])
        w_theirs = reorder(meta, w_out, 1)
        return piece, o2, o2b, piece2, t2, both, w_first, w_query[cut:], w_mine, w_theirs

    def nothing(last_hidden, w_key, w_value, w_query, w_out):
        rows = 2 * last_hidden.shape[0]
        cols = 2 * w_key.shape[1]
        one, two, three = (jnp.zeros((k, rows, cols), BF) for k in (1, 2, 3))
        first, rest = w_query[:cut], w_query[cut:]
        w_none = jnp.zeros((w_out.shape[0] * w_out.shape[1], w_out.shape[2]), BF)
        return (
            two, one[0], one[0], two, two, three, jnp.zeros_like(first), jnp.zeros_like(rest),
            w_none, w_none,
        )

    w_o_r = w_o.reshape(8, w_q.shape[1], width)
    piece, o2, o2b, piece2, t2, both, w_q2a, w_rest, w_o_mine, w_o_theirs = lax.cond(
        segment_ids[0] >= 0, cache, nothing, last_hidden, w_key, w_value, w_q, w_o_r
    )
    w_q2b = send(w_rest, PARTNER)
    x_in, x_out, both = lax.optimization_barrier((x_in, x_out, both))
    xo_a = send(x_out[: RB // 2], IN)
    xo_b = send(x_in[RB // 2 :], OUT)
    s1 = send(both, X_PREV)
    s3 = send(both, X_NEXT)
    state = project(meta, [after(x0, x_in, x_out)], query_gain, w_q, 0, width)
    state = project(meta, [x_in], query_gain, w_q, 1, width, state)
    state = project(meta, [x_out], query_gain, w_q, 3, width, state)
    xo_a, xo_b, s1, s3, *state = lax.optimization_barrier((xo_a, xo_b, s1, s3, *state))
    s1b = send(s1, CORE)
    s3b = send(s3, CORE)
    normed, q_own, res_own, res_other = project(
        meta, [xo_a, xo_b], query_gain, w_q, 2, width, state
    )
    w_q2b, s1b, s3b, normed, q_own, w_o_theirs = lax.optimization_barrier(
        (w_q2b, s1b, s3b, normed, q_own, w_o_theirs)
    )
    w_o2 = send(w_o_theirs, PARTNER)
    q_other = more_queries(normed, w_q2a, w_q2b)
    pieces = (piece, o2, o2b, s1, s1b, s3, s3b, piece2, t2)

    result = None
    for chunk in range(2):
        own = attend(meta, chunk, q_own, q_other, seg_row, pieces)
        c_in = send(own, IN)
        c_out = send(own, OUT)
        co_a = send(c_out[:RB], IN)
        co_b = send(c_in[RB:], OUT)
        parts = (own, c_in, co_a, co_b, c_out)
        sent = send(finish(meta, chunk, parts, w_o2, res_other, 2), PARTNER)
        result = finish(meta, chunk, parts, w_o_mine, res_own, 8, result)
        result = place(meta, chunk, sent, result)
    return result.reshape(1, 8 * RB, -1)


def solution(mesh):
    return jax.shard_map(
        body,
        mesh=mesh,
        in_specs=(
            P("section", "ctx", None),
            P("section", None),
            P(),
            P("section", None),
            P(None, "ctx"),
            P(None, "ctx"),
            P("section", None, "ctx"),
            P("section", None, "ctx"),
            P(),
        ),
        out_specs=P("section", None, "ctx"),
        check_vma=False,
    )
```

```python
import functools

import jax
import jax.numpy as jnp
from jax import lax
from jax.experimental import pallas as pl
from jax.experimental.pallas import tpu as pltpu
from jax.sharding import PartitionSpec as P

HD = 128
RB = 256
BF = jnp.bfloat16
F32 = jnp.float32
AXES = ("section", "ctx")
MIB = 1 << 20

PLACE = (((0, 1, 2, 3), (4, 5, 6, 7)), ((1, 0, 4, 5), (2, 3, 7, 6)))
SPOT = tuple(
    tuple(next((h, r) for h in range(2) for r in range(4) if table[h][r] == c) for c in range(8))
    for table in PLACE
)

MINE, THEIRS, SLOT, ROWS, OWN, CORE_AT, FIRST, X_AT = 0, 4, 8, 12, 20, 22, 23, 31


def facts_of(core, c):
    half, r = SPOT[core][c]
    mine, theirs = PLACE[core][half], PLACE[core][1 - half]
    ring = [r, r ^ 1, (r + 2) % 4, 3 - r]
    slots = [ring.index(p) for p in range(4)]
    rows = [place[p] for p in ring for place in (mine, theirs)]
    return [*mine, *theirs, *slots, *rows, mine[r], theirs[r], core]


FACTS = [[facts_of(core, c) for c in range(8)] for core in range(2)]


def moves(step):
    pairs = []
    for s in range(16):
        for c in range(8):
            core = s % 2
            half, spot = SPOT[core][c]
            yh, x, k, h, r = step(s // 8, s // 2 % 4, core, half, spot)
            if k == core:
                place = PLACE[core][h][r % 4]
            else:
                place = c
            pairs.append((s * 8 + c, (yh * 8 + x % 4 * 2 + k) * 8 + place))
    return pairs


IN = moves(lambda yh, x, k, h, r: (yh, x, k, h, r ^ 1))
OUT = moves(lambda yh, x, k, h, r: (yh, x, k, h, 3 - r))
PARTNER = moves(lambda yh, x, k, h, r: (yh, x, k, 1 - h, r))
CORE = moves(lambda yh, x, k, h, r: (yh, x, 1 - k, h, r))
FAR_Y = [
    (a, b) for a, b in moves(lambda yh, x, k, h, r: (1 - yh, x, k, h, r)) if a // 8 % 2 == 0
]
X_NEXT = moves(lambda yh, x, k, h, r: (yh, x + 1, k, h, r))
X_PREV = moves(lambda yh, x, k, h, r: (yh, x - 1, k, h, r))
X_FAR = moves(lambda yh, x, k, h, r: (yh, x + 2, k, h, r))


def send(value, pairs):
    return lax.ppermute(value, AXES, pairs)


def normalize(rows, gain):
    full = rows.astype(F32)
    scaled = full * lax.rsqrt(jnp.mean(full * full, axis=-1, keepdims=True) + 1e-05) * gain
    return scaled.astype(BF)


def project_kernel(pieces, meta, *refs):
    xs = refs[:pieces]
    gain, w = refs[pieces : pieces + 2]
    normed, q, res_own, res_other = refs[-4:]
    step = 32
    base = 0
    for x in xs:
        rows = x.shape[0]

        def norm_rows(i, _, x=x, base=base):
            at = pl.multiple_of(i * step, step)
            full = x[pl.ds(at, step), :].astype(F32)
            mean = jnp.mean(full * full, axis=-1, keepdims=True)
            normed[0, pl.ds(base + at, step), :] = (
                full * lax.rsqrt(mean + 1e-05) * gain[...]
            ).astype(BF)
            return 0

        lax.fori_loop(0, rows // step, norm_rows, 0)
        width = res_own.shape[2]
        for k, out in ((0, res_own), (1, res_other)):
            first = pl.multiple_of(meta[OWN + k] * width, 128)
            out[0, base : base + rows, :] = x[:, pl.ds(first, width)]
        base += rows
    q[0] = jnp.dot(normed[0], w[...], preferred_element_type=F32).astype(BF)


def project(meta, xs, gain, w, slot, width, prior=None):
    d, n = w.shape
    shapes = [(4, RB, d), (4, RB, n), (4, RB, width), (4, RB, width)]
    whole = lambda a: pl.BlockSpec(
        a.shape, lambda i, m, nd=a.ndim: (0,) * nd, pipeline_mode=pl.Buffered(1)
    )
    ins = list(xs) + [gain, w]
    specs = [whole(a) for a in ins]
    aliases = {}
    for k, a in enumerate(prior or ()):
        aliases[1 + len(ins)] = k
        ins.append(a)
        specs.append(pl.BlockSpec(memory_space=pl.ANY))

    def kernel(meta, *refs):
        project_kernel(len(xs), meta, *refs)

    return pl.pallas_call(
        kernel,
        grid_spec=pltpu.PrefetchScalarGridSpec(
            num_scalar_prefetch=1,
            grid=(1,),
            in_specs=specs,
            out_specs=[pl.BlockSpec((1,) + s[1:], lambda i, m: (slot, 0, 0)) for s in shapes],
        ),
        out_shape=[jax.ShapeDtypeStruct(s, BF) for s in shapes],
        input_output_aliases=aliases,
        compiler_params=pltpu.CompilerParams(vmem_limit_bytes=20 * MIB),
        cost_estimate=pl.CostEstimate(
            flops=2 * RB * d * n, bytes_accessed=2 * (3 * RB * d + d * n), transcendentals=0
        ),
    )(meta, *ins)


def more_queries_kernel(n_ref, w_ref, q_ref):
    q_ref[...] = jnp.dot(n_ref[...], w_ref[...], preferred_element_type=F32).astype(BF)


def more_queries(normed, w):
    d, n = w.shape
    rows = 2 * RB
    return pl.pallas_call(
        more_queries_kernel,
        grid=(2,),
        in_specs=[
            pl.BlockSpec((rows, d), lambda i: (i, 0)),
            pl.BlockSpec(w.shape, lambda i: (0, 0), pipeline_mode=pl.Buffered(1)),
        ],
        out_specs=pl.BlockSpec((rows, n), lambda i: (i, 0)),
        out_shape=jax.ShapeDtypeStruct((4 * RB, n), BF),
        compiler_params=pltpu.CompilerParams(vmem_limit_bytes=20 * MIB),
        cost_estimate=pl.CostEstimate(
            flops=8 * RB * d * n, bytes_accessed=2 * (4 * RB * d + d * n), transcendentals=0
        ),
    )(normed.reshape(4 * RB, d), w).reshape(4, RB, n)


def attend_kernel(
    chunk, meta, q_own, q_other, seg_row, own0, o1, o1b, o2, o2b, o3, o3b,
    other0, t1, t2, t3,
    out, kv, scores, tops, sums,
):
    t = pl.program_id(0)
    core = meta[CORE_AT]

    @pl.when(t == 0)
    def _():
        kv[0, 0] = own0[...]
        kv[0, 1, core] = o1[...]
        kv[0, 1, 1 - core] = o1b[...]
        kv[0, 2, core] = o2[...]
        kv[0, 2, 1 - core] = o2b[...]
        kv[0, 3, core] = o3[...]
        kv[0, 3, 1 - core] = o3b[...]
        kv[1, 0] = other0[...]
        kv[1, 1] = t1[...]
        kv[1, 2] = t2[...]
        kv[1, 3] = t3[...]

    block = meta[MINE + 2 * chunk + t]
    first = meta[FIRST + block]
    count = block - first + 1
    x = meta[X_AT]
    heads = q_own.shape[2] // HD
    factor = HD ** (-0.5) * 1.4426950408889634
    pairs = [(src, i) for src in range(2) for i in range(heads)]
    qs = (q_own, q_other)

    def place(i):
        kb = first + i
        j = lax.rem(lax.rem(kb, 4) - x + 4, 4)
        return kb, j, kb // 4

    tops[...] = jnp.full(tops.shape, -1e30, F32)
    sums[...] = jnp.zeros(sums.shape, F32)
    q_doc = jnp.transpose(jnp.broadcast_to(seg_row[block], (RB, RB)))
    row_at = block * RB + lax.broadcasted_iota(jnp.int32, (RB, RB), 0)
    col_at = lax.broadcasted_iota(jnp.int32, (RB, RB), 1)

    def score(i, _):
        kb, j, y = place(i)
        visible = (q_doc == seg_row[kb]) & (kb * RB + col_at <= row_at)
        for n, (src, h) in enumerate(pairs):
            cols = slice(h * HD, (h + 1) * HD)
            s = lax.dot_general(
                qs[src][0, :, cols], kv[src, j, y, :, cols], (((1,), (1,)), ((), ())),
                preferred_element_type=F32,
            )
            s = jnp.where(visible, s, -1e30)
            scores[n, i] = s
            tops[n] = jnp.maximum(tops[n], jnp.maximum(s[:, :HD], s[:, HD:]))
        return 0

    lax.fori_loop(0, count, score, 0)
    for n in range(len(pairs)):
        tops[n] = jnp.broadcast_to(jnp.max(tops[n], axis=-1, keepdims=True), (RB, HD))

    def expo(i, _):
        for n in range(len(pairs)):
            s = scores[n, i]
            top = tops[n]
            left = jnp.exp2((s[:, :HD] - top) * factor)
            right = jnp.exp2((s[:, HD:] - top) * factor)
            scores[n, i, :, :HD] = left
            scores[n, i, :, HD:] = right
            sums[n] += left + right
        return 0

    lax.fori_loop(0, count, expo, 0)
    for n in range(len(pairs)):
        total = jnp.sum(sums[n], axis=-1, keepdims=True)
        sums[n] = jnp.broadcast_to(1.0 / total, (RB, HD))
        tops[n] = jnp.zeros((RB, HD), F32)

    def mix(i, _):
        kb, j, y = place(i)
        for n, (src, h) in enumerate(pairs):
            cols = slice((heads + h) * HD, (heads + h + 1) * HD)
            e = scores[n, i]
            inv = sums[n]
            weights = jnp.concatenate([e[:, :HD] * inv, e[:, HD:] * inv], axis=1).astype(BF)
            tops[n] += jnp.dot(weights, kv[src, j, y, :, cols], preferred_element_type=F32)
        return 0

    lax.fori_loop(0, count, mix, 0)
    for n in range(len(pairs)):
        out[:, n * HD : (n + 1) * HD] = tops[n].astype(BF)


def attend(meta, chunk, q_own, q_other, seg_row, pieces):
    n = q_own.shape[2]
    heads = n // HD
    whole = lambda a: pl.BlockSpec(a.shape, lambda t, m, nd=a.ndim: (0,) * nd)
    q_spec = pl.BlockSpec((1, RB, n), lambda t, m: (m[SLOT + 2 * chunk + t], 0, 0))
    once = lambda a: pl.BlockSpec(
        a.shape, lambda t, m, nd=a.ndim: (0,) * nd, pipeline_mode=pl.Buffered(1)
    )
    return pl.pallas_call(
        functools.partial(attend_kernel, chunk),
        grid_spec=pltpu.PrefetchScalarGridSpec(
            num_scalar_prefetch=1,
            grid=(2,),
            in_specs=[q_spec, q_spec, whole(seg_row)] + list(map(once, pieces)),
            out_specs=pl.BlockSpec((RB, 2 * n), lambda t, m: (t, 0)),
            scratch_shapes=[
                pltpu.VMEM((2, 4, 2, RB, 2 * n), BF),
                pltpu.VMEM((2 * heads, 5, RB, RB), F32),
                pltpu.VMEM((2 * heads, RB, HD), F32),
                pltpu.VMEM((2 * heads, RB, HD), F32),
            ],
        ),
        out_shape=jax.ShapeDtypeStruct((2 * RB, 2 * n), BF),
        compiler_params=pltpu.CompilerParams(vmem_limit_bytes=32 * MIB),
        cost_estimate=pl.CostEstimate(
            flops=4 * 2 * RB * 768 * 2 * n, bytes_accessed=8 * MIB, transcendentals=2 * RB * 768 * 6
        ),
    )(meta, q_own, q_other, seg_row, *pieces)


def reorder_kernel(meta, w, out):
    out[...] = w[...]


def reorder(meta, w, swap):
    k8, n, width = w.shape
    return pl.pallas_call(
        reorder_kernel,
        grid_spec=pltpu.PrefetchScalarGridSpec(
            num_scalar_prefetch=1,
            grid=(k8,),
            in_specs=[
                pl.BlockSpec((1, n, width), lambda k, m: (m[ROWS + (k + swap - 2 * swap * (k % 2))], 0, 0))
            ],
            out_specs=pl.BlockSpec((1, n, width), lambda k, m: (k, 0, 0)),
        ),
        out_shape=jax.ShapeDtypeStruct(w.shape, BF),
    )(meta, w).reshape(k8 * n, width)


def finish_kernel(meta, c0, c1, c2a, c2b, c3, w, res, *refs):
    out = refs[-1]
    t = pl.program_id(0)
    far = jnp.where(t == 0, c2a[...], c2b[...])
    n = far.shape[1]
    total = res[0].astype(F32)
    for j, c in enumerate((c0[...], c1[...], far, c3[...])):
        total += jnp.dot(c, w[j * n : (j + 1) * n, :], preferred_element_type=F32)
    out[0] = total.astype(BF)


def finish(meta, chunk, parts, w, res, blocks, prior=None):
    depth, width = w.shape
    n = depth // 4
    tile = pl.BlockSpec((RB, n), lambda t, m: (t, 0))
    fixed = pl.BlockSpec((RB, n), lambda t, m: (0, 0))
    ins = list(parts) + [w, res]
    specs = [tile, tile, fixed, fixed, tile]
    specs.append(pl.BlockSpec(w.shape, lambda t, m: (0, 0), pipeline_mode=pl.Buffered(1)))
    specs.append(pl.BlockSpec((1, RB, width), lambda t, m: (m[SLOT + 2 * chunk + t], 0, 0)))
    aliases = {}
    if prior is not None:
        aliases[1 + len(ins)] = 0
        ins.append(prior)
        specs.append(pl.BlockSpec(memory_space=pl.ANY))
    if blocks == 2:
        target = lambda t, m: (t, 0, 0)
    else:
        target = lambda t, m: (m[MINE + 2 * chunk + t], 0, 0)
    return pl.pallas_call(
        finish_kernel,
        grid_spec=pltpu.PrefetchScalarGridSpec(
            num_scalar_prefetch=1,
            grid=(2,),
            in_specs=specs,
            out_specs=pl.BlockSpec((1, RB, width), target),
        ),
        out_shape=jax.ShapeDtypeStruct((blocks, RB, width), BF),
        input_output_aliases=aliases,
        compiler_params=pltpu.CompilerParams(vmem_limit_bytes=20 * MIB),
        cost_estimate=pl.CostEstimate(
            flops=4 * RB * depth * width, bytes_accessed=8 * MIB, transcendentals=0
        ),
    )(meta, *ins)


def place_kernel(chunk, meta, got, prior, out, sems):
    copies = [
        pltpu.make_async_copy(got.at[t], out.at[meta[THEIRS + 2 * chunk + t]], sems.at[t])
        for t in range(2)
    ]
    for copy in copies:
        copy.start()
    for copy in copies:
        copy.wait()


def place(meta, chunk, got, prior):
    in_place = pl.BlockSpec(memory_space=pl.ANY)
    return pl.pallas_call(
        functools.partial(place_kernel, chunk),
        grid_spec=pltpu.PrefetchScalarGridSpec(
            num_scalar_prefetch=1,
            grid=(1,),
            in_specs=[pl.BlockSpec(got.shape, lambda t, m: (0, 0, 0)), in_place],
            out_specs=in_place,
            scratch_shapes=[pltpu.SemaphoreType.DMA((2,))],
        ),
        out_shape=jax.ShapeDtypeStruct(prior.shape, BF),
        input_output_aliases={2: 0},
        compiler_params=pltpu.CompilerParams(vmem_limit_bytes=4 * MIB),
    )(meta, got, prior)


def after(value, *done):
    return lax.optimization_barrier((value,) + done)[0]


def body(
    section_input, last_hidden, kv_gain, query_gain, w_key, w_value, w_query, w_out, segment_ids
):
    section = lax.axis_index("section")
    c = lax.axis_index("ctx")
    core = section % 2
    y_hi = section // 8
    x0 = section_input[0]
    w_q = w_query[0]
    w_o = w_out[0]
    width = w_o.shape[1]

    x_in = send(x0, IN)
    x_out = send(x0, OUT)

    ids = segment_ids.reshape(8, RB)
    starts = jnp.sum(segment_ids[None, :] < ids[:, :1], axis=1, dtype=jnp.int32) // RB
    starts = jnp.maximum(starts, jnp.arange(8, dtype=jnp.int32) - 4)
    facts = jnp.array(FACTS, jnp.int32)[core, c]
    meta = jnp.concatenate([facts, starts, (section // 2 % 4)[None]])
    seg_row = segment_ids.reshape(8, 1, RB)

    def cache(last_hidden, w_key, w_value, w_out):
        kv_in = normalize(last_hidden, kv_gain)
        own_k = jnp.dot(kv_in, w_key, preferred_element_type=F32).astype(BF)
        own_v = jnp.dot(kv_in, w_value, preferred_element_type=F32).astype(BF)
        kv = jnp.concatenate([own_k, own_v], axis=1)
        kv2 = send(kv, CORE)
        pair = jnp.where(core == 0, jnp.stack([kv, kv2]), jnp.stack([kv2, kv]))
        far = send(pair, FAR_Y)
        far, w_mine = lax.optimization_barrier((far, reorder(meta, w_out, 0)))
        far = jnp.where(core == 0, far, send(far, CORE))
        piece = jnp.where(y_hi == 0, jnp.stack([pair, far]), jnp.stack([far, pair]))
        piece = piece.reshape(2, 2 * kv.shape[0], kv.shape[1])
        piece2 = send(piece, PARTNER)
        share = lax.dynamic_index_in_dim(piece, core, 0, keepdims=False)
        o1 = send(share, X_PREV)
        o2 = send(share, X_FAR)
        return piece, share, o1, o2, piece2, w_mine, reorder(meta, w_out, 1)

    def nothing(last_hidden, w_key, w_value, w_out):
        two = jnp.zeros((2, 2 * last_hidden.shape[0], 2 * w_key.shape[1]), BF)
        w_none = jnp.zeros((w_out.shape[0] * w_out.shape[1], w_out.shape[2]), BF)
        return two, two[0], two[0], two[0], two, w_none, w_none

    w_o_r = w_o.reshape(8, w_q.shape[1], width)
    piece, share, o1, o2, piece2, w_o_mine, w_o_theirs = lax.cond(
        segment_ids[0] >= 0, cache, nothing, last_hidden, w_key, w_value, w_o_r
    )
    w_q2 = send(after(w_q, piece2), PARTNER)
    x_in, x_out, piece2, share = lax.optimization_barrier((x_in, x_out, piece2, share))
    most = RB * 3 // 4
    xo_a = send(x_out[:most], IN)
    xo_b = send(x_in[most:], OUT)
    t1 = send(piece2, X_PREV)
    t3 = send(piece2, X_NEXT)
    state = project(meta, [after(x0, x_in, x_out)], query_gain, w_q, 0, width)
    state = project(meta, [x_in], query_gain, w_q, 1, width, state)
    state = project(meta, [x_out], query_gain, w_q, 3, width, state)
    t1, t3, o1, o2, piece2, share, *state = lax.optimization_barrier(
        (t1, t3, o1, o2, piece2, share, *state)
    )
    o3 = send(share, X_NEXT)
    t2 = send(piece2, X_FAR)
    o1b = send(o1, CORE)
    o2b = send(o2, CORE)
    xo_a, xo_b, o1b, o2b, o3 = lax.optimization_barrier((xo_a, xo_b, o1b, o2b, o3))
    o3b = send(o3, CORE)
    normed, q_own, res_own, res_other = project(
        meta, [xo_a, xo_b], query_gain, w_q, 2, width, state
    )
    w_q2, t2, o1b, o2b, o3b, normed, q_own = lax.optimization_barrier(
        (w_q2, t2, o1b, o2b, o3b, normed, q_own)
    )
    w_o2 = send(after(w_o_theirs, w_q2), PARTNER)
    q_other = more_queries(normed, w_q2)
    pieces = (piece, o1, o1b, o2, o2b, o3, o3b, piece2, t1, t2, t3)

    result = None
    parts = []
    for chunk in range(2):
        own = attend(meta, chunk, q_own, q_other, seg_row, pieces)
        c_in = send(own, IN)
        c_out = send(own, OUT)
        co_a = send(c_out[:RB], IN)
        co_b = send(c_in[RB:], OUT)
        parts.append((own, c_in, co_a, co_b, c_out))
    for chunk in range(2):
        result = finish(meta, chunk, parts[chunk], w_o_mine, res_own, 8, result)
    w_o2, result = lax.optimization_barrier((w_o2, result))
    sent = [
        send(finish(meta, chunk, parts[chunk], w_o2, res_other, 2), PARTNER) for chunk in range(2)
    ]
    for chunk in range(2):
        result = place(meta, chunk, sent[chunk], result)
    return result.reshape(1, 8 * RB, -1)


def solution(mesh):
    return jax.shard_map(
        body,
        mesh=mesh,
        in_specs=(
            P("section", "ctx", None),
            P("section", None),
            P(),
            P("section", None),
            P(None, "ctx"),
            P(None, "ctx"),
            P("section", None, "ctx"),
            P("section", None, "ctx"),
            P(),
        ),
        out_specs=P("section", None, "ctx"),
        check_vma=False,
    )
```

```python
import functools

import jax
import jax.numpy as jnp
from jax import lax
from jax.experimental import pallas as pl
from jax.experimental.pallas import tpu as pltpu
from jax.sharding import PartitionSpec as P

HD = 128
RB = 256
BF = jnp.bfloat16
F32 = jnp.float32
AXES = ("section", "ctx")
MIB = 1 << 20

PLACE = (((0, 1, 2, 3), (4, 5, 6, 7)), ((1, 0, 4, 5), (2, 3, 7, 6)))
SPOT = tuple(
    tuple(next((h, r) for h in range(2) for r in range(4) if table[h][r] == c) for c in range(8))
    for table in PLACE
)

MINE, THEIRS, SLOT, ROWS, OWN, CORE_AT, X_AT = 0, 4, 8, 12, 20, 22, 23


def facts_of(section, c):
    core = section % 2
    half, r = SPOT[core][c]
    mine, theirs = PLACE[core][half], PLACE[core][1 - half]
    ring = [r, r ^ 1, (r + 2) % 4, 3 - r]
    slots = [ring.index(p) for p in range(4)]
    rows = [place[p] for p in ring for place in (mine, theirs)]
    return [*mine, *theirs, *slots, *rows, mine[r], theirs[r], core, section // 2 % 4]


FACTS = [[facts_of(section, c) for c in range(8)] for section in range(16)]


def moves(step):
    pairs = []
    for s in range(16):
        for c in range(8):
            core = s % 2
            half, spot = SPOT[core][c]
            yh, x, k, h, r = step(s // 8, s // 2 % 4, core, half, spot)
            if k == core:
                place = PLACE[core][h][r % 4]
            else:
                place = c
            pairs.append((s * 8 + c, (yh * 8 + x % 4 * 2 + k) * 8 + place))
    return pairs


IN = moves(lambda yh, x, k, h, r: (yh, x, k, h, r ^ 1))
OUT = moves(lambda yh, x, k, h, r: (yh, x, k, h, 3 - r))
PARTNER = moves(lambda yh, x, k, h, r: (yh, x, k, 1 - h, r))
CORE = moves(lambda yh, x, k, h, r: (yh, x, 1 - k, h, r))
FAR_Y = [
    (a, b) for a, b in moves(lambda yh, x, k, h, r: (1 - yh, x, k, h, r)) if a // 8 % 2 == 0
]
X_NEXT = moves(lambda yh, x, k, h, r: (yh, x + 1, k, h, r))
X_PREV = moves(lambda yh, x, k, h, r: (yh, x - 1, k, h, r))
X_FAR = moves(lambda yh, x, k, h, r: (yh, x + 2, k, h, r))


def send(value, pairs):
    return lax.ppermute(value, AXES, pairs)


def normalize(rows, gain):
    full = rows.astype(F32)
    scaled = full * lax.rsqrt(jnp.mean(full * full, axis=-1, keepdims=True) + 1e-05) * gain
    return scaled.astype(BF)


def project_kernel(pieces, meta, *refs):
    xs = refs[:pieces]
    gain, w = refs[pieces : pieces + 2]
    normed, q, res_own, res_other = refs[-4:]
    step = 32
    base = 0
    for x in xs:
        rows = x.shape[0]

        def norm_rows(i, _, x=x, base=base):
            at = pl.multiple_of(i * step, step)
            full = x[pl.ds(at, step), :].astype(F32)
            mean = jnp.mean(full * full, axis=-1, keepdims=True)
            normed[0, pl.ds(base + at, step), :] = (
                full * lax.rsqrt(mean + 1e-05) * gain[...]
            ).astype(BF)
            return 0

        lax.fori_loop(0, rows // step, norm_rows, 0)
        width = res_own.shape[2]
        for k, out in ((0, res_own), (1, res_other)):
            first = pl.multiple_of(meta[OWN + k] * width, 128)
            out[0, base : base + rows, :] = x[:, pl.ds(first, width)]
        base += rows
    q[0] = jnp.dot(normed[0], w[...], preferred_element_type=F32).astype(BF)


def project(meta, xs, gain, w, slot, width, prior=None):
    d, n = w.shape
    shapes = [(4, RB, d), (4, RB, n), (4, RB, width), (4, RB, width)]
    whole = lambda a: pl.BlockSpec(
        a.shape, lambda i, m, nd=a.ndim: (0,) * nd, pipeline_mode=pl.Buffered(1)
    )
    ins = list(xs) + [gain, w]
    specs = [whole(a) for a in ins]
    aliases = {}
    for k, a in enumerate(prior or ()):
        aliases[1 + len(ins)] = k
        ins.append(a)
        specs.append(pl.BlockSpec(memory_space=pl.ANY))

    def kernel(meta, *refs):
        project_kernel(len(xs), meta, *refs)

    return pl.pallas_call(
        kernel,
        grid_spec=pltpu.PrefetchScalarGridSpec(
            num_scalar_prefetch=1,
            grid=(1,),
            in_specs=specs,
            out_specs=[pl.BlockSpec((1,) + s[1:], lambda i, m: (slot, 0, 0)) for s in shapes],
        ),
        out_shape=[jax.ShapeDtypeStruct(s, BF) for s in shapes],
        input_output_aliases=aliases,
        compiler_params=pltpu.CompilerParams(vmem_limit_bytes=20 * MIB),
        cost_estimate=pl.CostEstimate(
            flops=2 * RB * d * n, bytes_accessed=2 * (3 * RB * d + d * n), transcendentals=0
        ),
    )(meta, *ins)


def more_queries_kernel(n_ref, w_ref, q_ref):
    q_ref[...] = jnp.dot(n_ref[...], w_ref[...], preferred_element_type=F32).astype(BF)


def more_queries(normed, w):
    d, n = w.shape
    rows = 2 * RB
    return pl.pallas_call(
        more_queries_kernel,
        grid=(2,),
        in_specs=[
            pl.BlockSpec((rows, d), lambda i: (i, 0)),
            pl.BlockSpec(w.shape, lambda i: (0, 0), pipeline_mode=pl.Buffered(1)),
        ],
        out_specs=pl.BlockSpec((rows, n), lambda i: (i, 0)),
        out_shape=jax.ShapeDtypeStruct((4 * RB, n), BF),
        compiler_params=pltpu.CompilerParams(vmem_limit_bytes=20 * MIB),
        cost_estimate=pl.CostEstimate(
            flops=8 * RB * d * n, bytes_accessed=2 * (4 * RB * d + d * n), transcendentals=0
        ),
    )(normed.reshape(4 * RB, d), w).reshape(4, RB, n)


def attend_kernel(
    chunk, meta, q_own, q_other, seg_row, own0, o1, o1b, o2, o2b, o3, o3b,
    other0, t1, t2, t3,
    out, kv, scores, tops, sums,
):
    t = pl.program_id(0)
    core = meta[CORE_AT]

    @pl.when(t == 0)
    def _():
        kv[0, 0] = own0[...]
        kv[0, 1, core] = o1[...]
        kv[0, 1, 1 - core] = o1b[...]
        kv[0, 2, core] = o2[...]
        kv[0, 2, 1 - core] = o2b[...]
        kv[0, 3, core] = o3[...]
        kv[0, 3, 1 - core] = o3b[...]
        kv[1, 0] = other0[...]
        kv[1, 1] = t1[...]
        kv[1, 2] = t2[...]
        kv[1, 3] = t3[...]

    block = meta[MINE + 2 * chunk + t]
    earlier = (seg_row[...] < seg_row[block, :, :1]).astype(F32)
    first = jnp.maximum(jnp.sum(earlier).astype(jnp.int32) // RB, block - 4)
    count = block - first + 1
    x = meta[X_AT]
    heads = q_own.shape[2] // HD
    factor = HD ** (-0.5) * 1.4426950408889634
    pairs = [(src, i) for src in range(2) for i in range(heads)]
    qs = (q_own, q_other)

    def place(i):
        kb = first + i
        j = lax.rem(lax.rem(kb, 4) - x + 4, 4)
        return kb, j, kb // 4

    tops[...] = jnp.full(tops.shape, -1e30, F32)
    sums[...] = jnp.zeros(sums.shape, F32)
    q_doc = jnp.transpose(jnp.broadcast_to(seg_row[block], (RB, RB)))
    row_at = block * RB + lax.broadcasted_iota(jnp.int32, (RB, RB), 0)
    col_at = lax.broadcasted_iota(jnp.int32, (RB, RB), 1)

    def score(i, _):
        kb, j, y = place(i)
        visible = (q_doc == seg_row[kb]) & (kb * RB + col_at <= row_at)
        for n, (src, h) in enumerate(pairs):
            cols = slice(h * HD, (h + 1) * HD)
            s = lax.dot_general(
                qs[src][0, :, cols], kv[src, j, y, :, cols], (((1,), (1,)), ((), ())),
                preferred_element_type=F32,
            )
            s = jnp.where(visible, s, -1e30)
            scores[n, i] = s
            tops[n] = jnp.maximum(tops[n], jnp.maximum(s[:, :HD], s[:, HD:]))
        return 0

    lax.fori_loop(0, count, score, 0)
    for n in range(len(pairs)):
        tops[n] = jnp.broadcast_to(jnp.max(tops[n], axis=-1, keepdims=True), (RB, HD))

    def expo(i, _):
        for n in range(len(pairs)):
            s = scores[n, i]
            top = tops[n]
            left = jnp.exp2((s[:, :HD] - top) * factor)
            right = jnp.exp2((s[:, HD:] - top) * factor)
            scores[n, i, :, :HD] = left
            scores[n, i, :, HD:] = right
            sums[n] += left + right
        return 0

    lax.fori_loop(0, count, expo, 0)
    for n in range(len(pairs)):
        total = jnp.sum(sums[n], axis=-1, keepdims=True)
        sums[n] = jnp.broadcast_to(1.0 / total, (RB, HD))
        tops[n] = jnp.zeros((RB, HD), F32)

    def mix(i, _):
        kb, j, y = place(i)
        for n, (src, h) in enumerate(pairs):
            cols = slice((heads + h) * HD, (heads + h + 1) * HD)
            e = scores[n, i]
            inv = sums[n]
            weights = jnp.concatenate([e[:, :HD] * inv, e[:, HD:] * inv], axis=1).astype(BF)
            tops[n] += jnp.dot(weights, kv[src, j, y, :, cols], preferred_element_type=F32)
        return 0

    lax.fori_loop(0, count, mix, 0)
    for n in range(len(pairs)):
        out[:, n * HD : (n + 1) * HD] = tops[n].astype(BF)


def attend(meta, chunk, q_own, q_other, seg_row, pieces):
    n = q_own.shape[2]
    heads = n // HD
    whole = lambda a: pl.BlockSpec(a.shape, lambda t, m, nd=a.ndim: (0,) * nd)
    q_spec = pl.BlockSpec((1, RB, n), lambda t, m: (m[SLOT + 2 * chunk + t], 0, 0))
    once = lambda a: pl.BlockSpec(
        a.shape, lambda t, m, nd=a.ndim: (0,) * nd, pipeline_mode=pl.Buffered(1)
    )
    return pl.pallas_call(
        functools.partial(attend_kernel, chunk),
        grid_spec=pltpu.PrefetchScalarGridSpec(
            num_scalar_prefetch=1,
            grid=(2,),
            in_specs=[q_spec, q_spec, whole(seg_row)] + list(map(once, pieces)),
            out_specs=pl.BlockSpec((RB, 2 * n), lambda t, m: (t, 0)),
            scratch_shapes=[
                pltpu.VMEM((2, 4, 2, RB, 2 * n), BF),
                pltpu.VMEM((2 * heads, 5, RB, RB), F32),
                pltpu.VMEM((2 * heads, RB, HD), F32),
                pltpu.VMEM((2 * heads, RB, HD), F32),
            ],
        ),
        out_shape=jax.ShapeDtypeStruct((2 * RB, 2 * n), BF),
        compiler_params=pltpu.CompilerParams(vmem_limit_bytes=32 * MIB),
        cost_estimate=pl.CostEstimate(
            flops=4 * 2 * RB * 768 * 2 * n, bytes_accessed=8 * MIB, transcendentals=2 * RB * 768 * 6
        ),
    )(meta, q_own, q_other, seg_row, *pieces)


def reorder_kernel(meta, w, out):
    out[...] = w[...]


def reorder(meta, w, swap):
    k8, n, width = w.shape
    return pl.pallas_call(
        reorder_kernel,
        grid_spec=pltpu.PrefetchScalarGridSpec(
            num_scalar_prefetch=1,
            grid=(k8,),
            in_specs=[
                pl.BlockSpec((1, n, width), lambda k, m: (m[ROWS + (k + swap - 2 * swap * (k % 2))], 0, 0))
            ],
            out_specs=pl.BlockSpec((1, n, width), lambda k, m: (k, 0, 0)),
        ),
        out_shape=jax.ShapeDtypeStruct(w.shape, BF),
    )(meta, w).reshape(k8 * n, width)


def finish_kernel(meta, c0, c1, c2a, c2b, c3, w, res, *refs):
    out = refs[-1]
    t = pl.program_id(0)
    far = jnp.where(t == 0, c2a[...], c2b[...])
    n = far.shape[1]
    total = res[0].astype(F32)
    for j, c in enumerate((c0[...], c1[...], far, c3[...])):
        total += jnp.dot(c, w[j * n : (j + 1) * n, :], preferred_element_type=F32)
    out[0] = total.astype(BF)


def finish(meta, chunk, parts, w, res, blocks, prior=None):
    depth, width = w.shape
    n = depth // 4
    tile = pl.BlockSpec((RB, n), lambda t, m: (t, 0))
    fixed = pl.BlockSpec((RB, n), lambda t, m: (0, 0))
    ins = list(parts) + [w, res]
    specs = [tile, tile, fixed, fixed, tile]
    specs.append(pl.BlockSpec(w.shape, lambda t, m: (0, 0), pipeline_mode=pl.Buffered(1)))
    specs.append(pl.BlockSpec((1, RB, width), lambda t, m: (m[SLOT + 2 * chunk + t], 0, 0)))
    aliases = {}
    if prior is not None:
        aliases[1 + len(ins)] = 0
        ins.append(prior)
        specs.append(pl.BlockSpec(memory_space=pl.ANY))
    if blocks == 2:
        target = lambda t, m: (t, 0, 0)
    else:
        target = lambda t, m: (m[MINE + 2 * chunk + t], 0, 0)
    return pl.pallas_call(
        finish_kernel,
        grid_spec=pltpu.PrefetchScalarGridSpec(
            num_scalar_prefetch=1,
            grid=(2,),
            in_specs=specs,
            out_specs=pl.BlockSpec((1, RB, width), target),
        ),
        out_shape=jax.ShapeDtypeStruct((blocks, RB, width), BF),
        input_output_aliases=aliases,
        compiler_params=pltpu.CompilerParams(vmem_limit_bytes=20 * MIB),
        cost_estimate=pl.CostEstimate(
            flops=4 * RB * depth * width, bytes_accessed=8 * MIB, transcendentals=0
        ),
    )(meta, *ins)


def place_kernel(chunk, meta, got, prior, out, sems):
    copies = [
        pltpu.make_async_copy(got.at[t], out.at[meta[THEIRS + 2 * chunk + t]], sems.at[t])
        for t in range(2)
    ]
    for copy in copies:
        copy.start()
    for copy in copies:
        copy.wait()


def place(meta, chunk, got, prior):
    in_place = pl.BlockSpec(memory_space=pl.ANY)
    return pl.pallas_call(
        functools.partial(place_kernel, chunk),
        grid_spec=pltpu.PrefetchScalarGridSpec(
            num_scalar_prefetch=1,
            grid=(1,),
            in_specs=[pl.BlockSpec(got.shape, lambda t, m: (0, 0, 0)), in_place],
            out_specs=in_place,
            scratch_shapes=[pltpu.SemaphoreType.DMA((2,))],
        ),
        out_shape=jax.ShapeDtypeStruct(prior.shape, BF),
        input_output_aliases={2: 0},
        compiler_params=pltpu.CompilerParams(vmem_limit_bytes=4 * MIB),
    )(meta, got, prior)


def after(value, *done):
    return lax.optimization_barrier((value,) + done)[0]


def body(
    section_input, last_hidden, kv_gain, query_gain, w_key, w_value, w_query, w_out, segment_ids
):
    section = lax.axis_index("section")
    c = lax.axis_index("ctx")
    core = section % 2
    y_hi = section // 8
    x0 = section_input[0]
    w_q = w_query[0]
    w_o = w_out[0]
    width = w_o.shape[1]

    x_in = send(x0, IN)
    x_out = send(x0, OUT)

    meta = jnp.array(FACTS, jnp.int32)[section, c]
    seg_row = segment_ids.reshape(8, 1, RB)

    def cache(last_hidden, w_key, w_value, w_out):
        kv_in = normalize(last_hidden, kv_gain)
        own_k = jnp.dot(kv_in, w_key, preferred_element_type=F32).astype(BF)
        own_v = jnp.dot(kv_in, w_value, preferred_element_type=F32).astype(BF)
        kv = jnp.concatenate([own_k, own_v], axis=1)
        kv2 = send(kv, CORE)
        pair = jnp.where(core == 0, jnp.stack([kv, kv2]), jnp.stack([kv2, kv]))
        far = send(pair, FAR_Y)
        far, w_mine = lax.optimization_barrier((far, reorder(meta, w_out, 0)))
        far = jnp.where(core == 0, far, send(far, CORE))
        piece = jnp.where(y_hi == 0, jnp.stack([pair, far]), jnp.stack([far, pair]))
        piece = piece.reshape(2, 2 * kv.shape[0], kv.shape[1])
        piece2 = send(piece, PARTNER)
        share = lax.dynamic_index_in_dim(piece, core, 0, keepdims=False)
        o1 = send(share, X_PREV)
        o2 = send(share, X_FAR)
        return piece, share, o1, o2, piece2, w_mine, reorder(meta, w_out, 1)

    def nothing(last_hidden, w_key, w_value, w_out):
        two = jnp.zeros((2, 2 * last_hidden.shape[0], 2 * w_key.shape[1]), BF)
        w_none = jnp.zeros((w_out.shape[0] * w_out.shape[1], w_out.shape[2]), BF)
        return two, two[0], two[0], two[0], two, w_none, w_none

    w_o_r = w_o.reshape(8, w_q.shape[1], width)
    piece, share, o1, o2, piece2, w_o_mine, w_o_theirs = lax.cond(
        segment_ids[0] >= 0, cache, nothing, last_hidden, w_key, w_value, w_o_r
    )
    w_q2 = send(after(w_q, piece2), PARTNER)
    x_in, x_out, piece2, share = lax.optimization_barrier((x_in, x_out, piece2, share))
    most = RB * 3 // 4
    xo_a = send(x_out[:most], IN)
    xo_b = send(x_in[most:], OUT)
    t1 = send(piece2, X_PREV)
    t3 = send(piece2, X_NEXT)
    state = project(meta, [after(x0, x_in, x_out)], query_gain, w_q, 0, width)
    state = project(meta, [x_in], query_gain, w_q, 1, width, state)
    state = project(meta, [x_out], query_gain, w_q, 3, width, state)
    t1, t3, o1, o2, piece2, share, *state = lax.optimization_barrier(
        (t1, t3, o1, o2, piece2, share, *state)
    )
    o3 = send(share, X_NEXT)
    t2 = send(piece2, X_FAR)
    o1b = send(o1, CORE)
    o2b = send(o2, CORE)
    xo_a, xo_b, o1b, o2b, o3 = lax.optimization_barrier((xo_a, xo_b, o1b, o2b, o3))
    o3b = send(o3, CORE)
    normed, q_own, res_own, res_other = project(
        meta, [xo_a, xo_b], query_gain, w_q, 2, width, state
    )
    w_q2, t2, o1b, o2b, o3b, normed, q_own = lax.optimization_barrier(
        (w_q2, t2, o1b, o2b, o3b, normed, q_own)
    )
    w_o2 = send(after(w_o_theirs, w_q2), PARTNER)
    q_other = more_queries(normed, w_q2)
    pieces = (piece, o1, o1b, o2, o2b, o3, o3b, piece2, t1, t2, t3)

    result = None
    parts = []
    for chunk in range(2):
        own = attend(meta, chunk, q_own, q_other, seg_row, pieces)
        c_in = send(own, IN)
        c_out = send(own, OUT)
        co_a = send(c_out[:RB], IN)
        co_b = send(c_in[RB:], OUT)
        parts.append((own, c_in, co_a, co_b, c_out))
    result = finish(meta, 0, parts[0], w_o_mine, res_own, 8)
    w_o2, result = lax.optimization_barrier((w_o2, result))
    others = [finish(meta, chunk, parts[chunk], w_o2, res_other, 2) for chunk in range(2)]
    sent = [send(other, PARTNER) for other in others]
    w_o_mine = after(w_o_mine, *others)
    result = finish(meta, 1, parts[1], w_o_mine, res_own, 8, result)
    for chunk in range(2):
        result = place(meta, chunk, sent[chunk], result)
    return result.reshape(1, 8 * RB, -1)


def solution(mesh):
    return jax.shard_map(
        body,
        mesh=mesh,
        in_specs=(
            P("section", "ctx", None),
            P("section", None),
            P(),
            P("section", None),
            P(None, "ctx"),
            P(None, "ctx"),
            P("section", None, "ctx"),
            P("section", None, "ctx"),
            P(),
        ),
        out_specs=P("section", None, "ctx"),
        check_vma=False,
    )
```

```python
import functools

import jax
import jax.numpy as jnp
from jax import lax
from jax.experimental import pallas as pl
from jax.experimental.pallas import tpu as pltpu
from jax.sharding import PartitionSpec as P

HD = 128
RB = 256
CUT = 384
BF = jnp.bfloat16
F32 = jnp.float32
AXES = ("section", "ctx")
MIB = 1 << 20

PLACE = (((0, 1, 2, 3), (4, 5, 6, 7)), ((1, 0, 4, 5), (2, 3, 7, 6)))
SPOT = tuple(
    tuple(next((h, r) for h in range(2) for r in range(4) if table[h][r] == c) for c in range(8))
    for table in PLACE
)

MINE, THEIRS, SLOT, ROWS, OWN, CORE_AT, X_AT = 0, 4, 8, 12, 20, 22, 23


def facts_of(section, c):
    core = section % 2
    half, r = SPOT[core][c]
    mine, theirs = PLACE[core][half], PLACE[core][1 - half]
    ring = [r, r ^ 1, (r + 2) % 4, 3 - r]
    slots = [ring.index(p) for p in range(4)]
    rows = [place[p] for p in ring for place in (mine, theirs)]
    return [*mine, *theirs, *slots, *rows, mine[r], theirs[r], core, section // 2 % 4]


FACTS = [[facts_of(section, c) for c in range(8)] for section in range(16)]


def moves(step):
    pairs = []
    for s in range(16):
        for c in range(8):
            core = s % 2
            half, spot = SPOT[core][c]
            yh, x, k, h, r = step(s // 8, s // 2 % 4, core, half, spot)
            if k == core:
                place = PLACE[core][h][r % 4]
            else:
                place = c
            pairs.append((s * 8 + c, (yh * 8 + x % 4 * 2 + k) * 8 + place))
    return pairs


IN = moves(lambda yh, x, k, h, r: (yh, x, k, h, r ^ 1))
OUT = moves(lambda yh, x, k, h, r: (yh, x, k, h, 3 - r))
PARTNER = moves(lambda yh, x, k, h, r: (yh, x, k, 1 - h, r))
CORE = moves(lambda yh, x, k, h, r: (yh, x, 1 - k, h, r))
FAR_Y = [
    (a, b) for a, b in moves(lambda yh, x, k, h, r: (1 - yh, x, k, h, r)) if a // 8 % 2 == 0
]
X_NEXT = moves(lambda yh, x, k, h, r: (yh, x + 1, k, h, r))
X_PREV = moves(lambda yh, x, k, h, r: (yh, x - 1, k, h, r))
X_FAR = moves(lambda yh, x, k, h, r: (yh, x + 2, k, h, r))


def send(value, pairs):
    return lax.ppermute(value, AXES, pairs)


def normalize(rows, gain):
    full = rows.astype(F32)
    scaled = full * lax.rsqrt(jnp.mean(full * full, axis=-1, keepdims=True) + 1e-05) * gain
    return scaled.astype(BF)


def project_kernel(pieces, meta, *refs):
    xs = refs[:pieces]
    gain, w = refs[pieces : pieces + 2]
    normed, q, res_own, res_other = refs[-4:]
    step = 32
    base = 0
    for x in xs:
        rows = x.shape[0]

        def norm_rows(i, _, x=x, base=base):
            at = pl.multiple_of(i * step, step)
            full = x[pl.ds(at, step), :].astype(F32)
            mean = jnp.mean(full * full, axis=-1, keepdims=True)
            normed[0, pl.ds(base + at, step), :] = (
                full * lax.rsqrt(mean + 1e-05) * gain[...]
            ).astype(BF)
            return 0

        lax.fori_loop(0, rows // step, norm_rows, 0)
        width = res_own.shape[2]
        for k, out in ((0, res_own), (1, res_other)):
            first = pl.multiple_of(meta[OWN + k] * width, 128)
            out[0, base : base + rows, :] = x[:, pl.ds(first, width)]
        base += rows
    q[0] = jnp.dot(normed[0], w[...], preferred_element_type=F32).astype(BF)


def project(meta, xs, gain, w, slot, width, prior=None):
    d, n = w.shape
    shapes = [(4, RB, d), (4, RB, n), (4, RB, width), (4, RB, width)]
    whole = lambda a: pl.BlockSpec(
        a.shape, lambda i, m, nd=a.ndim: (0,) * nd, pipeline_mode=pl.Buffered(1)
    )
    ins = list(xs) + [gain, w]
    specs = [whole(a) for a in ins]
    aliases = {}
    for k, a in enumerate(prior or ()):
        aliases[1 + len(ins)] = k
        ins.append(a)
        specs.append(pl.BlockSpec(memory_space=pl.ANY))

    def kernel(meta, *refs):
        project_kernel(len(xs), meta, *refs)

    return pl.pallas_call(
        kernel,
        grid_spec=pltpu.PrefetchScalarGridSpec(
            num_scalar_prefetch=1,
            grid=(1,),
            in_specs=specs,
            out_specs=[pl.BlockSpec((1,) + s[1:], lambda i, m: (slot, 0, 0)) for s in shapes],
        ),
        out_shape=[jax.ShapeDtypeStruct(s, BF) for s in shapes],
        input_output_aliases=aliases,
        compiler_params=pltpu.CompilerParams(vmem_limit_bytes=20 * MIB),
        cost_estimate=pl.CostEstimate(
            flops=2 * RB * d * n, bytes_accessed=2 * (3 * RB * d + d * n), transcendentals=0
        ),
    )(meta, *ins)


def more_queries_kernel(n_ref, w_ref, q_ref):
    q_ref[...] = jnp.dot(n_ref[...], w_ref[...], preferred_element_type=F32).astype(BF)


def more_queries(normed, w):
    d, n = w.shape
    rows = 2 * RB
    return pl.pallas_call(
        more_queries_kernel,
        grid=(2,),
        in_specs=[
            pl.BlockSpec((rows, d), lambda i: (i, 0)),
            pl.BlockSpec(w.shape, lambda i: (0, 0), pipeline_mode=pl.Buffered(1)),
        ],
        out_specs=pl.BlockSpec((rows, n), lambda i: (i, 0)),
        out_shape=jax.ShapeDtypeStruct((4 * RB, n), BF),
        compiler_params=pltpu.CompilerParams(vmem_limit_bytes=20 * MIB),
        cost_estimate=pl.CostEstimate(
            flops=8 * RB * d * n, bytes_accessed=2 * (4 * RB * d + d * n), transcendentals=0
        ),
    )(normed.reshape(4 * RB, d), w).reshape(4, RB, n)


def attend_kernel(
    chunk, meta, q_own, q_other, seg_row, own0, o1, o1b, o2, o2b, o3, o3b,
    other0, t1, t2, t3,
    out, kv, scores, tops, sums,
):
    t = pl.program_id(0)
    core = meta[CORE_AT]

    @pl.when(t == 0)
    def _():
        kv[0, 0] = own0[...]
        kv[0, 1, core] = o1[...]
        kv[0, 1, 1 - core] = o1b[...]
        kv[0, 2, core] = o2[...]
        kv[0, 2, 1 - core] = o2b[...]
        kv[0, 3, core] = o3[...]
        kv[0, 3, 1 - core] = o3b[...]
        kv[1, 0] = other0[...]
        kv[1, 1] = t1[...]
        kv[1, 2] = t2[...]
        kv[1, 3] = t3[...]

    block = meta[MINE + 2 * chunk + t]
    earlier = (seg_row[...] < seg_row[block, :, :1]).astype(F32)
    first = jnp.maximum(jnp.sum(earlier).astype(jnp.int32) // RB, block - 4)
    count = block - first + 1
    x = meta[X_AT]
    heads = q_own.shape[2] // HD
    factor = HD ** (-0.5) * 1.4426950408889634
    pairs = [(src, i) for src in range(2) for i in range(heads)]
    qs = (q_own, q_other)

    def place(i):
        kb = first + i
        j = lax.rem(lax.rem(kb, 4) - x + 4, 4)
        return kb, j, kb // 4

    tops[...] = jnp.full(tops.shape, -1e30, F32)
    sums[...] = jnp.zeros(sums.shape, F32)
    q_doc = jnp.transpose(jnp.broadcast_to(seg_row[block], (RB, RB)))
    row_at = block * RB + lax.broadcasted_iota(jnp.int32, (RB, RB), 0)
    col_at = lax.broadcasted_iota(jnp.int32, (RB, RB), 1)

    def score(i, _):
        kb, j, y = place(i)
        visible = (q_doc == seg_row[kb]) & (kb * RB + col_at <= row_at)
        for n, (src, h) in enumerate(pairs):
            cols = slice(h * HD, (h + 1) * HD)
            s = lax.dot_general(
                qs[src][0, :, cols], kv[src, j, y, :, cols], (((1,), (1,)), ((), ())),
                preferred_element_type=F32,
            )
            s = jnp.where(visible, s, -1e30)
            scores[n, i] = s
            tops[n] = jnp.maximum(tops[n], jnp.maximum(s[:, :HD], s[:, HD:]))
        return 0

    lax.fori_loop(0, count, score, 0)
    for n in range(len(pairs)):
        tops[n] = jnp.broadcast_to(jnp.max(tops[n], axis=-1, keepdims=True), (RB, HD))

    def expo(i, _):
        for n in range(len(pairs)):
            s = scores[n, i]
            top = tops[n]
            left = jnp.exp2((s[:, :HD] - top) * factor)
            right = jnp.exp2((s[:, HD:] - top) * factor)
            scores[n, i, :, :HD] = left
            scores[n, i, :, HD:] = right
            sums[n] += left + right
        return 0

    lax.fori_loop(0, count, expo, 0)
    for n in range(len(pairs)):
        total = jnp.sum(sums[n], axis=-1, keepdims=True)
        sums[n] = jnp.broadcast_to(1.0 / total, (RB, HD))
        tops[n] = jnp.zeros((RB, HD), F32)

    def mix(i, _):
        kb, j, y = place(i)
        for n, (src, h) in enumerate(pairs):
            cols = slice((heads + h) * HD, (heads + h + 1) * HD)
            e = scores[n, i]
            inv = sums[n]
            weights = jnp.concatenate([e[:, :HD] * inv, e[:, HD:] * inv], axis=1).astype(BF)
            tops[n] += jnp.dot(weights, kv[src, j, y, :, cols], preferred_element_type=F32)
        return 0

    lax.fori_loop(0, count, mix, 0)
    for n in range(len(pairs)):
        out[:, n * HD : (n + 1) * HD] = tops[n].astype(BF)


def attend(meta, chunk, q_own, q_other, seg_row, pieces):
    n = q_own.shape[2]
    heads = n // HD
    whole = lambda a: pl.BlockSpec(a.shape, lambda t, m, nd=a.ndim: (0,) * nd)
    q_spec = pl.BlockSpec((1, RB, n), lambda t, m: (m[SLOT + 2 * chunk + t], 0, 0))
    once = lambda a: pl.BlockSpec(
        a.shape, lambda t, m, nd=a.ndim: (0,) * nd, pipeline_mode=pl.Buffered(1)
    )
    return pl.pallas_call(
        functools.partial(attend_kernel, chunk),
        grid_spec=pltpu.PrefetchScalarGridSpec(
            num_scalar_prefetch=1,
            grid=(2,),
            in_specs=[q_spec, q_spec, whole(seg_row)] + list(map(once, pieces)),
            out_specs=pl.BlockSpec((RB, 2 * n), lambda t, m: (t, 0)),
            scratch_shapes=[
                pltpu.VMEM((2, 4, 2, RB, 2 * n), BF),
                pltpu.VMEM((2 * heads, 5, RB, RB), F32),
                pltpu.VMEM((2 * heads, RB, HD), F32),
                pltpu.VMEM((2 * heads, RB, HD), F32),
            ],
        ),
        out_shape=jax.ShapeDtypeStruct((2 * RB, 2 * n), BF),
        compiler_params=pltpu.CompilerParams(vmem_limit_bytes=32 * MIB),
        cost_estimate=pl.CostEstimate(
            flops=4 * 2 * RB * 768 * 2 * n, bytes_accessed=8 * MIB, transcendentals=2 * RB * 768 * 6
        ),
    )(meta, q_own, q_other, seg_row, *pieces)


def reorder_kernel(meta, w, out):
    out[...] = w[...]


def reorder(meta, w, swap):
    k8, n, width = w.shape
    return pl.pallas_call(
        reorder_kernel,
        grid_spec=pltpu.PrefetchScalarGridSpec(
            num_scalar_prefetch=1,
            grid=(k8,),
            in_specs=[
                pl.BlockSpec((1, n, width), lambda k, m: (m[ROWS + (k + swap - 2 * swap * (k % 2))], 0, 0))
            ],
            out_specs=pl.BlockSpec((1, n, width), lambda k, m: (k, 0, 0)),
        ),
        out_shape=jax.ShapeDtypeStruct(w.shape, BF),
    )(meta, w).reshape(k8 * n, width)


def finish_kernel(meta, c0, c1, c2a, c2b, c3, w, res, *refs):
    out = refs[-1]
    t = pl.program_id(0)
    far = jnp.where(t == 0, c2a[:RB, :], jnp.concatenate([c2a[RB:, :], c2b[...]], axis=0))
    n = far.shape[1]
    total = res[0].astype(F32)
    for j, c in enumerate((c0[...], c1[...], far, c3[...])):
        total += jnp.dot(c, w[j * n : (j + 1) * n, :], preferred_element_type=F32)
    out[0] = total.astype(BF)


def finish(meta, chunk, parts, w, res, blocks, prior=None):
    depth, width = w.shape
    n = depth // 4
    tile = pl.BlockSpec((RB, n), lambda t, m: (t, 0))
    fixed = lambda a: pl.BlockSpec(a.shape, lambda t, m: (0, 0))
    ins = list(parts) + [w, res]
    specs = [tile, tile, fixed(parts[2]), fixed(parts[3]), tile]
    specs.append(pl.BlockSpec(w.shape, lambda t, m: (0, 0), pipeline_mode=pl.Buffered(1)))
    specs.append(pl.BlockSpec((1, RB, width), lambda t, m: (m[SLOT + 2 * chunk + t], 0, 0)))
    aliases = {}
    if prior is not None:
        aliases[1 + len(ins)] = 0
        ins.append(prior)
        specs.append(pl.BlockSpec(memory_space=pl.ANY))
    if blocks == 2:
        target = lambda t, m: (t, 0, 0)
    else:
        target = lambda t, m: (m[MINE + 2 * chunk + t], 0, 0)
    return pl.pallas_call(
        finish_kernel,
        grid_spec=pltpu.PrefetchScalarGridSpec(
            num_scalar_prefetch=1,
            grid=(2,),
            in_specs=specs,
            out_specs=pl.BlockSpec((1, RB, width), target),
        ),
        out_shape=jax.ShapeDtypeStruct((blocks, RB, width), BF),
        input_output_aliases=aliases,
        compiler_params=pltpu.CompilerParams(vmem_limit_bytes=20 * MIB),
        cost_estimate=pl.CostEstimate(
            flops=4 * RB * depth * width, bytes_accessed=8 * MIB, transcendentals=0
        ),
    )(meta, *ins)


def place_kernel(chunk, meta, got, prior, out, sems):
    copies = [
        pltpu.make_async_copy(got.at[t], out.at[meta[THEIRS + 2 * chunk + t]], sems.at[t])
        for t in range(2)
    ]
    for copy in copies:
        copy.start()
    for copy in copies:
        copy.wait()


def place(meta, chunk, got, prior):
    in_place = pl.BlockSpec(memory_space=pl.ANY)
    return pl.pallas_call(
        functools.partial(place_kernel, chunk),
        grid_spec=pltpu.PrefetchScalarGridSpec(
            num_scalar_prefetch=1,
            grid=(1,),
            in_specs=[pl.BlockSpec(got.shape, lambda t, m: (0, 0, 0)), in_place],
            out_specs=in_place,
            scratch_shapes=[pltpu.SemaphoreType.DMA((2,))],
        ),
        out_shape=jax.ShapeDtypeStruct(prior.shape, BF),
        input_output_aliases={2: 0},
        compiler_params=pltpu.CompilerParams(vmem_limit_bytes=4 * MIB),
    )(meta, got, prior)


def after(value, *done):
    return lax.optimization_barrier((value,) + done)[0]


def body(
    section_input, last_hidden, kv_gain, query_gain, w_key, w_value, w_query, w_out, segment_ids
):
    section = lax.axis_index("section")
    c = lax.axis_index("ctx")
    core = section % 2
    y_hi = section // 8
    x0 = section_input[0]
    w_q = w_query[0]
    w_o = w_out[0]
    width = w_o.shape[1]

    x_in = send(x0, IN)
    x_out = send(x0, OUT)

    meta = jnp.array(FACTS, jnp.int32)[section, c]
    seg_row = segment_ids.reshape(8, 1, RB)

    def cache(last_hidden, w_key, w_value, w_out):
        kv_in = normalize(last_hidden, kv_gain)
        own_k = jnp.dot(kv_in, w_key, preferred_element_type=F32).astype(BF)
        own_v = jnp.dot(kv_in, w_value, preferred_element_type=F32).astype(BF)
        kv = jnp.concatenate([own_k, own_v], axis=1)
        kv2 = send(kv, CORE)
        pair = jnp.where(core == 0, jnp.stack([kv, kv2]), jnp.stack([kv2, kv]))
        far = send(pair, FAR_Y)
        near2 = send(pair, PARTNER)
        far, w_mine = lax.optimization_barrier((far, reorder(meta, w_out, 0)))
        far = jnp.where(core == 0, far, send(far, CORE))
        far2 = send(far, PARTNER)

        def in_order(near, far):
            both = jnp.where(y_hi == 0, jnp.stack([near, far]), jnp.stack([far, near]))
            return both.reshape(2, 2 * kv.shape[0], kv.shape[1])

        piece = in_order(pair, far)
        share = lax.dynamic_index_in_dim(piece, core, 0, keepdims=False)
        return piece, share, in_order(near2, far2), w_mine

    def nothing(last_hidden, w_key, w_value, w_out):
        two = jnp.zeros((2, 2 * last_hidden.shape[0], 2 * w_key.shape[1]), BF)
        w_none = jnp.zeros((w_out.shape[0] * w_out.shape[1], w_out.shape[2]), BF)
        return two, two[0], two, w_none

    w_o_r = w_o.reshape(8, w_q.shape[1], width)
    piece, share, piece2, w_o_mine = lax.cond(
        segment_ids[0] >= 0, cache, nothing, last_hidden, w_key, w_value, w_o_r
    )
    w_q2 = send(after(w_q, piece2), PARTNER)
    o1 = send(share, X_PREV)
    o3 = send(share, X_NEXT)
    o2 = send(after(share, o1, o3), X_FAR)
    x0, w_o_r = after(x0, share), after(w_o_r, share)
    w_o_theirs = reorder(meta, w_o_r, 1)
    state = project(meta, [x0], query_gain, w_q, 0, width)
    x_in, x_out, piece2, o1, o2, o3, w_o_theirs, *state = lax.optimization_barrier(
        (x_in, x_out, piece2, o1, o2, o3, w_o_theirs, *state)
    )
    most = RB * 5 // 8
    xo_a = send(x_out[:most], IN)
    xo_b = send(x_in[most:], OUT)
    t1 = send(piece2, X_PREV)
    t3 = send(piece2, X_NEXT)
    state = project(meta, [x_in], query_gain, w_q, 1, width, state)
    state = project(meta, [x_out], query_gain, w_q, 3, width, state)
    t1, t3, o1, o2, o3, piece2, *state = lax.optimization_barrier(
        (t1, t3, o1, o2, o3, piece2, *state)
    )
    t2 = send(piece2, X_FAR)
    o1b = send(o1, CORE)
    o2b = send(o2, CORE)
    o3b = send(o3, CORE)
    xo_a, xo_b, o1b, o2b, o3b = lax.optimization_barrier((xo_a, xo_b, o1b, o2b, o3b))
    normed, q_own, res_own, res_other = project(
        meta, [xo_a, xo_b], query_gain, w_q, 2, width, state
    )
    w_q2, t2, o1b, o2b, o3b, normed, q_own = lax.optimization_barrier(
        (w_q2, t2, o1b, o2b, o3b, normed, q_own)
    )
    w_o2 = send(after(w_o_theirs, w_q2), PARTNER)
    q_other = more_queries(normed, w_q2)
    pieces = (piece, o1, o1b, o2, o2b, o3, o3b, piece2, t1, t2, t3)

    result = None
    parts = []
    for chunk in range(2):
        own = attend(meta, chunk, q_own, q_other, seg_row, pieces)
        c_in = send(own, IN)
        c_out = send(own, OUT)
        c_in, c_out = lax.optimization_barrier((c_in, c_out))
        co_a = send(c_out[:CUT], IN)
        co_b = send(c_in[CUT:], OUT)
        parts.append((own, c_in, co_a, co_b, c_out))
    result = finish(meta, 0, parts[0], w_o_mine, res_own, 8)
    w_o2, result = lax.optimization_barrier((w_o2, result))
    others = [finish(meta, chunk, parts[chunk], w_o2, res_other, 2) for chunk in range(2)]
    sent = [send(other, PARTNER) for other in others]
    w_o_mine = after(w_o_mine, *others)
    result = finish(meta, 1, parts[1], w_o_mine, res_own, 8, result)
    for chunk in range(2):
        result = place(meta, chunk, sent[chunk], result)
    return result.reshape(1, 8 * RB, -1)


def solution(mesh):
    return jax.shard_map(
        body,
        mesh=mesh,
        in_specs=(
            P("section", "ctx", None),
            P("section", None),
            P(),
            P("section", None),
            P(None, "ctx"),
            P(None, "ctx"),
            P("section", None, "ctx"),
            P("section", None, "ctx"),
            P(),
        ),
        out_specs=P("section", None, "ctx"),
        check_vma=False,
    )
```

```python
import functools

import jax
import jax.numpy as jnp
from jax import lax
from jax.experimental import pallas as pl
from jax.experimental.pallas import tpu as pltpu
from jax.sharding import PartitionSpec as P

HD = 128
RB = 256
CUT = 384
BF = jnp.bfloat16
F32 = jnp.float32
AXES = ("section", "ctx")
MIB = 1 << 20

PLACE = (((0, 1, 2, 3), (4, 5, 6, 7)), ((1, 0, 4, 5), (2, 3, 7, 6)))
SPOT = tuple(
    tuple(next((h, r) for h in range(2) for r in range(4) if table[h][r] == c) for c in range(8))
    for table in PLACE
)

MINE, THEIRS, SLOT, ROWS, OWN, CORE_AT, X_AT = 0, 4, 8, 12, 20, 22, 23


def facts_of(section, c):
    core = section % 2
    half, r = SPOT[core][c]
    mine, theirs = PLACE[core][half], PLACE[core][1 - half]
    ring = [r, r ^ 1, (r + 2) % 4, 3 - r]
    slots = [ring.index(p) for p in range(4)]
    rows = [place[p] for p in ring for place in (mine, theirs)]
    return [*mine, *theirs, *slots, *rows, mine[r], theirs[r], core, section // 2 % 4]


FACTS = [[facts_of(section, c) for c in range(8)] for section in range(16)]


def moves(step):
    pairs = []
    for s in range(16):
        for c in range(8):
            core = s % 2
            half, spot = SPOT[core][c]
            yh, x, k, h, r = step(s // 8, s // 2 % 4, core, half, spot)
            if k == core:
                place = PLACE[core][h][r % 4]
            else:
                place = c
            pairs.append((s * 8 + c, (yh * 8 + x % 4 * 2 + k) * 8 + place))
    return pairs


IN = moves(lambda yh, x, k, h, r: (yh, x, k, h, r ^ 1))
OUT = moves(lambda yh, x, k, h, r: (yh, x, k, h, 3 - r))
PARTNER = moves(lambda yh, x, k, h, r: (yh, x, k, 1 - h, r))
CORE = moves(lambda yh, x, k, h, r: (yh, x, 1 - k, h, r))
FAR_Y = [
    (a, b) for a, b in moves(lambda yh, x, k, h, r: (1 - yh, x, k, h, r)) if a // 8 % 2 == 0
]
X_NEXT = moves(lambda yh, x, k, h, r: (yh, x + 1, k, h, r))
X_PREV = moves(lambda yh, x, k, h, r: (yh, x - 1, k, h, r))
X_FAR = moves(lambda yh, x, k, h, r: (yh, x + 2, k, h, r))


def send(value, pairs):
    return lax.ppermute(value, AXES, pairs)


def normalize(rows, gain):
    full = rows.astype(F32)
    scaled = full * lax.rsqrt(jnp.mean(full * full, axis=-1, keepdims=True) + 1e-05) * gain
    return scaled.astype(BF)


def project_kernel(pieces, meta, *refs):
    xs = refs[:pieces]
    gain, w = refs[pieces : pieces + 2]
    normed, q, res_own, res_other = refs[-4:]
    step = 32
    base = 0
    for x in xs:
        rows = x.shape[0]

        def norm_rows(i, _, x=x, base=base):
            at = pl.multiple_of(i * step, step)
            full = x[pl.ds(at, step), :].astype(F32)
            mean = jnp.mean(full * full, axis=-1, keepdims=True)
            normed[0, pl.ds(base + at, step), :] = (
                full * lax.rsqrt(mean + 1e-05) * gain[...]
            ).astype(BF)
            return 0

        lax.fori_loop(0, rows // step, norm_rows, 0)
        width = res_own.shape[2]
        for k, out in ((0, res_own), (1, res_other)):
            first = pl.multiple_of(meta[OWN + k] * width, 128)
            out[0, base : base + rows, :] = x[:, pl.ds(first, width)]
        base += rows
    q[0] = jnp.dot(normed[0], w[...], preferred_element_type=F32).astype(BF)


def project(meta, xs, gain, w, slot, width, prior=None):
    d, n = w.shape
    shapes = [(4, RB, d), (4, RB, n), (4, RB, width), (4, RB, width)]
    whole = lambda a: pl.BlockSpec(
        a.shape, lambda i, m, nd=a.ndim: (0,) * nd, pipeline_mode=pl.Buffered(1)
    )
    ins = list(xs) + [gain, w]
    specs = [whole(a) for a in ins]
    aliases = {}
    for k, a in enumerate(prior or ()):
        aliases[1 + len(ins)] = k
        ins.append(a)
        specs.append(pl.BlockSpec(memory_space=pl.ANY))

    def kernel(meta, *refs):
        project_kernel(len(xs), meta, *refs)

    return pl.pallas_call(
        kernel,
        grid_spec=pltpu.PrefetchScalarGridSpec(
            num_scalar_prefetch=1,
            grid=(1,),
            in_specs=specs,
            out_specs=[pl.BlockSpec((1,) + s[1:], lambda i, m: (slot, 0, 0)) for s in shapes],
        ),
        out_shape=[jax.ShapeDtypeStruct(s, BF) for s in shapes],
        input_output_aliases=aliases,
        compiler_params=pltpu.CompilerParams(vmem_limit_bytes=20 * MIB),
        cost_estimate=pl.CostEstimate(
            flops=2 * RB * d * n, bytes_accessed=2 * (3 * RB * d + d * n), transcendentals=0
        ),
    )(meta, *ins)


def more_queries_kernel(n_ref, w_ref, q_ref):
    q_ref[...] = jnp.dot(n_ref[...], w_ref[...], preferred_element_type=F32).astype(BF)


def more_queries(normed, w):
    d, n = w.shape
    rows = 2 * RB
    return pl.pallas_call(
        more_queries_kernel,
        grid=(2,),
        in_specs=[
            pl.BlockSpec((rows, d), lambda i: (i, 0)),
            pl.BlockSpec(w.shape, lambda i: (0, 0), pipeline_mode=pl.Buffered(1)),
        ],
        out_specs=pl.BlockSpec((rows, n), lambda i: (i, 0)),
        out_shape=jax.ShapeDtypeStruct((4 * RB, n), BF),
        compiler_params=pltpu.CompilerParams(vmem_limit_bytes=20 * MIB),
        cost_estimate=pl.CostEstimate(
            flops=8 * RB * d * n, bytes_accessed=2 * (4 * RB * d + d * n), transcendentals=0
        ),
    )(normed.reshape(4 * RB, d), w).reshape(4, RB, n)


def attend_kernel(
    chunk, meta, q_own, q_other, seg_row, own0, o1, o1b, o2, o2b, o3, o3b,
    other0, t1, t2, t3,
    out, kv, scores, tops, sums,
):
    t = pl.program_id(0)
    core = meta[CORE_AT]

    @pl.when(t == 0)
    def _():
        kv[0, 0] = own0[...]
        kv[0, 1, core] = o1[...]
        kv[0, 1, 1 - core] = o1b[...]
        kv[0, 2, core] = o2[...]
        kv[0, 2, 1 - core] = o2b[...]
        kv[0, 3, core] = o3[...]
        kv[0, 3, 1 - core] = o3b[...]
        kv[1, 0] = other0[...]
        kv[1, 1] = t1[...]
        kv[1, 2] = t2[...]
        kv[1, 3] = t3[...]

    block = meta[MINE + 2 * chunk + t]
    earlier = (seg_row[...] < seg_row[block, :, :1]).astype(F32)
    first = jnp.maximum(jnp.sum(earlier).astype(jnp.int32) // RB, block - 4)
    count = block - first + 1
    x = meta[X_AT]
    heads = q_own.shape[2] // HD
    factor = HD ** (-0.5) * 1.4426950408889634
    pairs = [(src, i) for src in range(2) for i in range(heads)]
    qs = (q_own, q_other)

    def place(i):
        kb = first + i
        j = lax.rem(lax.rem(kb, 4) - x + 4, 4)
        return kb, j, kb // 4

    tops[...] = jnp.full(tops.shape, -1e30, F32)
    sums[...] = jnp.zeros(sums.shape, F32)
    q_doc = jnp.transpose(jnp.broadcast_to(seg_row[block], (RB, RB)))
    row_at = block * RB + lax.broadcasted_iota(jnp.int32, (RB, RB), 0)
    col_at = lax.broadcasted_iota(jnp.int32, (RB, RB), 1)

    def score(i, _):
        kb, j, y = place(i)
        visible = (q_doc == seg_row[kb]) & (kb * RB + col_at <= row_at)
        for n, (src, h) in enumerate(pairs):
            cols = slice(h * HD, (h + 1) * HD)
            s = lax.dot_general(
                qs[src][0, :, cols], kv[src, j, y, :, cols], (((1,), (1,)), ((), ())),
                preferred_element_type=F32,
            )
            s = jnp.where(visible, s, -1e30)
            scores[n, i] = s
            tops[n] = jnp.maximum(tops[n], jnp.maximum(s[:, :HD], s[:, HD:]))
        return 0

    lax.fori_loop(0, count, score, 0)
    for n in range(len(pairs)):
        tops[n] = jnp.broadcast_to(jnp.max(tops[n], axis=-1, keepdims=True), (RB, HD))

    def expo(i, _):
        for n in range(len(pairs)):
            s = scores[n, i]
            top = tops[n]
            left = jnp.exp2((s[:, :HD] - top) * factor)
            right = jnp.exp2((s[:, HD:] - top) * factor)
            scores[n, i, :, :HD] = left
            scores[n, i, :, HD:] = right
            sums[n] += left + right
        return 0

    lax.fori_loop(0, count, expo, 0)
    for n in range(len(pairs)):
        total = jnp.sum(sums[n], axis=-1, keepdims=True)
        sums[n] = jnp.broadcast_to(1.0 / total, (RB, HD))
        tops[n] = jnp.zeros((RB, HD), F32)

    def mix(i, _):
        kb, j, y = place(i)
        for n, (src, h) in enumerate(pairs):
            cols = slice((heads + h) * HD, (heads + h + 1) * HD)
            e = scores[n, i]
            inv = sums[n]
            weights = jnp.concatenate([e[:, :HD] * inv, e[:, HD:] * inv], axis=1).astype(BF)
            tops[n] += jnp.dot(weights, kv[src, j, y, :, cols], preferred_element_type=F32)
        return 0

    lax.fori_loop(0, count, mix, 0)
    for n in range(len(pairs)):
        out[:, n * HD : (n + 1) * HD] = tops[n].astype(BF)


def attend(meta, chunk, q_own, q_other, seg_row, pieces):
    n = q_own.shape[2]
    heads = n // HD
    whole = lambda a: pl.BlockSpec(a.shape, lambda t, m, nd=a.ndim: (0,) * nd)
    q_spec = pl.BlockSpec((1, RB, n), lambda t, m: (m[SLOT + 2 * chunk + t], 0, 0))
    once = lambda a: pl.BlockSpec(
        a.shape, lambda t, m, nd=a.ndim: (0,) * nd, pipeline_mode=pl.Buffered(1)
    )
    return pl.pallas_call(
        functools.partial(attend_kernel, chunk),
        grid_spec=pltpu.PrefetchScalarGridSpec(
            num_scalar_prefetch=1,
            grid=(2,),
            in_specs=[q_spec, q_spec, whole(seg_row)] + list(map(once, pieces)),
            out_specs=pl.BlockSpec((RB, 2 * n), lambda t, m: (t, 0)),
            scratch_shapes=[
                pltpu.VMEM((2, 4, 2, RB, 2 * n), BF),
                pltpu.VMEM((2 * heads, 5, RB, RB), F32),
                pltpu.VMEM((2 * heads, RB, HD), F32),
                pltpu.VMEM((2 * heads, RB, HD), F32),
            ],
        ),
        out_shape=jax.ShapeDtypeStruct((2 * RB, 2 * n), BF),
        compiler_params=pltpu.CompilerParams(vmem_limit_bytes=32 * MIB),
        cost_estimate=pl.CostEstimate(
            flops=4 * 2 * RB * 768 * 2 * n, bytes_accessed=8 * MIB, transcendentals=2 * RB * 768 * 6
        ),
    )(meta, q_own, q_other, seg_row, *pieces)


def reorder_kernel(meta, w, out):
    out[...] = w[...]


def reorder(meta, w, swap):
    k8, n, width = w.shape
    return pl.pallas_call(
        reorder_kernel,
        grid_spec=pltpu.PrefetchScalarGridSpec(
            num_scalar_prefetch=1,
            grid=(k8,),
            in_specs=[
                pl.BlockSpec((1, n, width), lambda k, m: (m[ROWS + (k + swap - 2 * swap * (k % 2))], 0, 0))
            ],
            out_specs=pl.BlockSpec((1, n, width), lambda k, m: (k, 0, 0)),
        ),
        out_shape=jax.ShapeDtypeStruct(w.shape, BF),
        compiler_params=pltpu.CompilerParams(vmem_limit_bytes=4 * MIB),
    )(meta, w).reshape(k8 * n, width)


def finish_kernel(meta, c0, c1, c2a, c2b, c3, w, res, *refs):
    out = refs[-1]
    t = pl.program_id(0)
    far = jnp.where(t == 0, c2a[:RB, :], jnp.concatenate([c2a[RB:, :], c2b[...]], axis=0))
    n = far.shape[1]
    total = res[0].astype(F32)
    for j, c in enumerate((c0[...], c1[...], far, c3[...])):
        total += jnp.dot(c, w[j * n : (j + 1) * n, :], preferred_element_type=F32)
    out[0] = total.astype(BF)


def finish(meta, chunk, parts, w, res, blocks, prior=None):
    depth, width = w.shape
    n = depth // 4
    tile = pl.BlockSpec((RB, n), lambda t, m: (t, 0))
    fixed = lambda a: pl.BlockSpec(a.shape, lambda t, m: (0, 0))
    ins = list(parts) + [w, res]
    specs = [tile, tile, fixed(parts[2]), fixed(parts[3]), tile]
    specs.append(pl.BlockSpec(w.shape, lambda t, m: (0, 0), pipeline_mode=pl.Buffered(1)))
    specs.append(pl.BlockSpec((1, RB, width), lambda t, m: (m[SLOT + 2 * chunk + t], 0, 0)))
    aliases = {}
    if prior is not None:
        aliases[1 + len(ins)] = 0
        ins.append(prior)
        specs.append(pl.BlockSpec(memory_space=pl.ANY))
    if blocks == 2:
        target = lambda t, m: (t, 0, 0)
    else:
        target = lambda t, m: (m[MINE + 2 * chunk + t], 0, 0)
    return pl.pallas_call(
        finish_kernel,
        grid_spec=pltpu.PrefetchScalarGridSpec(
            num_scalar_prefetch=1,
            grid=(2,),
            in_specs=specs,
            out_specs=pl.BlockSpec((1, RB, width), target),
        ),
        out_shape=jax.ShapeDtypeStruct((blocks, RB, width), BF),
        input_output_aliases=aliases,
        compiler_params=pltpu.CompilerParams(vmem_limit_bytes=20 * MIB),
        cost_estimate=pl.CostEstimate(
            flops=4 * RB * depth * width, bytes_accessed=8 * MIB, transcendentals=0
        ),
    )(meta, *ins)


def place_kernel(chunk, meta, got, prior, out, sems):
    copies = [
        pltpu.make_async_copy(got.at[t], out.at[meta[THEIRS + 2 * chunk + t]], sems.at[t])
        for t in range(2)
    ]
    for copy in copies:
        copy.start()
    for copy in copies:
        copy.wait()


def place(meta, chunk, got, prior):
    in_place = pl.BlockSpec(memory_space=pl.ANY)
    return pl.pallas_call(
        functools.partial(place_kernel, chunk),
        grid_spec=pltpu.PrefetchScalarGridSpec(
            num_scalar_prefetch=1,
            grid=(1,),
            in_specs=[pl.BlockSpec(got.shape, lambda t, m: (0, 0, 0)), in_place],
            out_specs=in_place,
            scratch_shapes=[pltpu.SemaphoreType.DMA((2,))],
        ),
        out_shape=jax.ShapeDtypeStruct(prior.shape, BF),
        input_output_aliases={2: 0},
        compiler_params=pltpu.CompilerParams(vmem_limit_bytes=4 * MIB),
    )(meta, got, prior)


def after(value, *done):
    return lax.optimization_barrier((value,) + done)[0]


def body(
    section_input, last_hidden, kv_gain, query_gain, w_key, w_value, w_query, w_out, segment_ids
):
    section = lax.axis_index("section")
    c = lax.axis_index("ctx")
    core = section % 2
    y_hi = section // 8
    x0 = section_input[0]
    w_q = w_query[0]
    w_o = w_out[0]
    width = w_o.shape[1]

    x_in = send(x0, IN)
    x_out = send(x0, OUT)

    meta = jnp.array(FACTS, jnp.int32)[section, c]
    seg_row = segment_ids.reshape(8, 1, RB)

    def cache(last_hidden, w_key, w_value, w_out):
        kv_in = normalize(last_hidden, kv_gain)
        own_k = jnp.dot(kv_in, w_key, preferred_element_type=F32).astype(BF)
        own_v = jnp.dot(kv_in, w_value, preferred_element_type=F32).astype(BF)
        kv = jnp.concatenate([own_k, own_v], axis=1)
        kv2 = send(kv, CORE)
        pair = jnp.where(core == 0, jnp.stack([kv, kv2]), jnp.stack([kv2, kv]))
        far = send(pair, FAR_Y)
        far, w_mine = lax.optimization_barrier((far, reorder(meta, w_out, 0)))
        far = jnp.where(core == 0, far, send(far, CORE))
        piece = jnp.where(y_hi == 0, jnp.stack([pair, far]), jnp.stack([far, pair]))
        piece = piece.reshape(2, 2 * kv.shape[0], kv.shape[1])
        piece2 = send(piece, PARTNER)
        share = lax.dynamic_index_in_dim(piece, core, 0, keepdims=False)
        o2 = send(share, X_FAR)
        return piece, share, o2, piece2, w_mine, reorder(meta, w_out, 1)

    def nothing(last_hidden, w_key, w_value, w_out):
        two = jnp.zeros((2, 2 * last_hidden.shape[0], 2 * w_key.shape[1]), BF)
        w_none = jnp.zeros((w_out.shape[0] * w_out.shape[1], w_out.shape[2]), BF)
        return two, two[0], two[0], two, w_none, w_none

    w_o_r = w_o.reshape(8, w_q.shape[1], width)
    piece, share, o2, piece2, w_o_mine, w_o_theirs = lax.cond(
        segment_ids[0] >= 0, cache, nothing, last_hidden, w_key, w_value, w_o_r
    )
    w_q2 = send(after(w_q, piece2), PARTNER)
    o1 = send(share, X_PREV)
    o3 = send(share, X_NEXT)
    x_in, x_out, piece2, share, o1, o3 = lax.optimization_barrier(
        (x_in, x_out, piece2, share, o1, o3)
    )
    most = RB * 5 // 8
    xo_a = send(x_out[:most], IN)
    xo_b = send(x_in[most:], OUT)
    t1 = send(piece2, X_PREV)
    t3 = send(piece2, X_NEXT)
    state = project(meta, [after(x0, x_in, x_out)], query_gain, w_q, 0, width)
    state = project(meta, [x_in], query_gain, w_q, 1, width, state)
    state = project(meta, [x_out], query_gain, w_q, 3, width, state)
    xo_b, t1, t3, o1, o2, o3, piece2, *state = lax.optimization_barrier(
        (xo_b, t1, t3, o1, o2, o3, piece2, *state)
    )
    t2 = send(piece2, X_FAR)
    o1b = send(o1, CORE)
    o2b = send(o2, CORE)
    o3b = send(o3, CORE)
    xo_a, t2, w_q2, o1b, o2b, o3b, w_o_theirs = lax.optimization_barrier(
        (xo_a, t2, w_q2, o1b, o2b, o3b, w_o_theirs)
    )
    w_o2 = send(w_o_theirs, PARTNER)
    normed, q_own, res_own, res_other = project(
        meta, [xo_a, xo_b], query_gain, w_q, 2, width, state
    )
    q_other = more_queries(normed, w_q2)
    pieces = (piece, o1, o1b, o2, o2b, o3, o3b, piece2, t1, t2, t3)

    result = None
    parts = []
    for chunk in range(2):
        own = attend(meta, chunk, q_own, q_other, seg_row, pieces)
        c_in = send(own, IN)
        c_out = send(own, OUT)
        c_in, c_out = lax.optimization_barrier((c_in, c_out))
        co_a = send(c_out[:CUT], IN)
        co_b = send(c_in[CUT:], OUT)
        parts.append((own, c_in, co_a, co_b, c_out))
    result = finish(meta, 0, parts[0], w_o_mine, res_own, 8)
    w_o2, result = lax.optimization_barrier((w_o2, result))
    others = [finish(meta, chunk, parts[chunk], w_o2, res_other, 2) for chunk in range(2)]
    sent = [send(other, PARTNER) for other in others]
    w_o_mine = after(w_o_mine, *others)
    result = finish(meta, 1, parts[1], w_o_mine, res_own, 8, result)
    for chunk in range(2):
        result = place(meta, chunk, sent[chunk], result)
    return result.reshape(1, 8 * RB, -1)


def solution(mesh):
    return jax.shard_map(
        body,
        mesh=mesh,
        in_specs=(
            P("section", "ctx", None),
            P("section", None),
            P(),
            P("section", None),
            P(None, "ctx"),
            P(None, "ctx"),
            P("section", None, "ctx"),
            P("section", None, "ctx"),
            P(),
        ),
        out_specs=P("section", None, "ctx"),
        check_vma=False,
    )
```

```python
import functools

import jax
import jax.numpy as jnp
from jax import lax
from jax.experimental import pallas as pl
from jax.experimental.pallas import tpu as pltpu
from jax.sharding import PartitionSpec as P

HD = 128
RB = 256
CUT = 256
BF = jnp.bfloat16
F32 = jnp.float32
AXES = ("section", "ctx")
MIB = 1 << 20

PLACE = (((0, 1, 2, 3), (4, 5, 6, 7)), ((1, 0, 4, 5), (2, 3, 7, 6)))
SPOT = tuple(
    tuple(next((h, r) for h in range(2) for r in range(4) if table[h][r] == c) for c in range(8))
    for table in PLACE
)

MINE, THEIRS, SLOT, ROWS, OWN, CORE_AT, X_AT = 0, 4, 8, 12, 20, 22, 23


def facts_of(section, c):
    core = section % 2
    half, r = SPOT[core][c]
    mine, theirs = PLACE[core][half], PLACE[core][1 - half]
    ring = [r, r ^ 1, (r + 2) % 4, 3 - r]
    slots = [ring.index(p) for p in range(4)]
    rows = [place[p] for p in ring for place in (mine, theirs)]
    return [*mine, *theirs, *slots, *rows, mine[r], theirs[r], core, section // 2 % 4]


FACTS = [[facts_of(section, c) for c in range(8)] for section in range(16)]


def moves(step):
    pairs = []
    for s in range(16):
        for c in range(8):
            core = s % 2
            half, spot = SPOT[core][c]
            yh, x, k, h, r = step(s // 8, s // 2 % 4, core, half, spot)
            if k == core:
                place = PLACE[core][h][r % 4]
            else:
                place = c
            pairs.append((s * 8 + c, (yh * 8 + x % 4 * 2 + k) * 8 + place))
    return pairs


IN = moves(lambda yh, x, k, h, r: (yh, x, k, h, r ^ 1))
OUT = moves(lambda yh, x, k, h, r: (yh, x, k, h, 3 - r))
PARTNER = moves(lambda yh, x, k, h, r: (yh, x, k, 1 - h, r))
CORE = moves(lambda yh, x, k, h, r: (yh, x, 1 - k, h, r))
FAR_Y = [
    (a, b) for a, b in moves(lambda yh, x, k, h, r: (1 - yh, x, k, h, r)) if a // 8 % 2 == 0
]
X_NEXT = moves(lambda yh, x, k, h, r: (yh, x + 1, k, h, r))
X_PREV = moves(lambda yh, x, k, h, r: (yh, x - 1, k, h, r))
X_FAR = moves(lambda yh, x, k, h, r: (yh, x + 2, k, h, r))


def send(value, pairs):
    return lax.ppermute(value, AXES, pairs)


def normalize(rows, gain):
    full = rows.astype(F32)
    scaled = full * lax.rsqrt(jnp.mean(full * full, axis=-1, keepdims=True) + 1e-05) * gain
    return scaled.astype(BF)


def project_kernel(pieces, meta, *refs):
    xs = refs[:pieces]
    gain, w = refs[pieces : pieces + 2]
    normed, q, res_own, res_other = refs[-4:]
    step = 32
    base = 0
    for x in xs:
        rows = x.shape[0]

        def norm_rows(i, _, x=x, base=base):
            at = pl.multiple_of(i * step, step)
            full = x[pl.ds(at, step), :].astype(F32)
            mean = jnp.mean(full * full, axis=-1, keepdims=True)
            normed[0, pl.ds(base + at, step), :] = (
                full * lax.rsqrt(mean + 1e-05) * gain[...]
            ).astype(BF)
            return 0

        lax.fori_loop(0, rows // step, norm_rows, 0)
        width = res_own.shape[2]
        for k, out in ((0, res_own), (1, res_other)):
            first = pl.multiple_of(meta[OWN + k] * width, 128)
            out[0, base : base + rows, :] = x[:, pl.ds(first, width)]
        base += rows
    q[0] = jnp.dot(normed[0], w[...], preferred_element_type=F32).astype(BF)


def project(meta, xs, gain, w, slot, width, prior=None):
    d, n = w.shape
    shapes = [(4, RB, d), (4, RB, n), (4, RB, width), (4, RB, width)]
    whole = lambda a: pl.BlockSpec(
        a.shape, lambda i, m, nd=a.ndim: (0,) * nd, pipeline_mode=pl.Buffered(1)
    )
    ins = list(xs) + [gain, w]
    specs = [whole(a) for a in ins]
    aliases = {}
    for k, a in enumerate(prior or ()):
        aliases[1 + len(ins)] = k
        ins.append(a)
        specs.append(pl.BlockSpec(memory_space=pl.ANY))

    def kernel(meta, *refs):
        project_kernel(len(xs), meta, *refs)

    return pl.pallas_call(
        kernel,
        grid_spec=pltpu.PrefetchScalarGridSpec(
            num_scalar_prefetch=1,
            grid=(1,),
            in_specs=specs,
            out_specs=[pl.BlockSpec((1,) + s[1:], lambda i, m: (slot, 0, 0)) for s in shapes],
        ),
        out_shape=[jax.ShapeDtypeStruct(s, BF) for s in shapes],
        input_output_aliases=aliases,
        compiler_params=pltpu.CompilerParams(vmem_limit_bytes=20 * MIB),
        cost_estimate=pl.CostEstimate(
            flops=2 * RB * d * n, bytes_accessed=2 * (3 * RB * d + d * n), transcendentals=0
        ),
    )(meta, *ins)


def more_queries_kernel(n_ref, w_ref, q_ref):
    q_ref[...] = jnp.dot(n_ref[...], w_ref[...], preferred_element_type=F32).astype(BF)


def more_queries(normed, w):
    d, n = w.shape
    rows = 2 * RB
    return pl.pallas_call(
        more_queries_kernel,
        grid=(2,),
        in_specs=[
            pl.BlockSpec((rows, d), lambda i: (i, 0)),
            pl.BlockSpec(w.shape, lambda i: (0, 0), pipeline_mode=pl.Buffered(1)),
        ],
        out_specs=pl.BlockSpec((rows, n), lambda i: (i, 0)),
        out_shape=jax.ShapeDtypeStruct((4 * RB, n), BF),
        compiler_params=pltpu.CompilerParams(vmem_limit_bytes=20 * MIB),
        cost_estimate=pl.CostEstimate(
            flops=8 * RB * d * n, bytes_accessed=2 * (4 * RB * d + d * n), transcendentals=0
        ),
    )(normed.reshape(4 * RB, d), w).reshape(4, RB, n)


def attend_kernel(
    chunk, meta, q_own, q_other, seg_row, own0, o1, o1b, o2, o2b, o3, o3b,
    other0, t1, t2, t3,
    out, kv, scores, tops, sums,
):
    t = pl.program_id(0)
    core = meta[CORE_AT]

    @pl.when(t == 0)
    def _():
        kv[0, 0] = own0[...]
        kv[0, 1, core] = o1[...]
        kv[0, 1, 1 - core] = o1b[...]
        kv[0, 2, core] = o2[...]
        kv[0, 2, 1 - core] = o2b[...]
        kv[0, 3, core] = o3[...]
        kv[0, 3, 1 - core] = o3b[...]
        kv[1, 0] = other0[...]
        kv[1, 1] = t1[...]
        kv[1, 2] = t2[...]
        kv[1, 3] = t3[...]

    block = meta[MINE + 2 * chunk + t]
    earlier = (seg_row[...] < seg_row[block, :, :1]).astype(F32)
    first = jnp.maximum(jnp.sum(earlier).astype(jnp.int32) // RB, block - 4)
    count = block - first + 1
    x = meta[X_AT]
    heads = q_own.shape[2] // HD
    factor = HD ** (-0.5) * 1.4426950408889634
    pairs = [(src, i) for src in range(2) for i in range(heads)]
    qs = (q_own, q_other)

    def place(i):
        kb = first + i
        j = lax.rem(lax.rem(kb, 4) - x + 4, 4)
        return kb, j, kb // 4

    tops[...] = jnp.full(tops.shape, -1e30, F32)
    sums[...] = jnp.zeros(sums.shape, F32)
    q_doc = jnp.transpose(jnp.broadcast_to(seg_row[block], (RB, RB)))
    row_at = block * RB + lax.broadcasted_iota(jnp.int32, (RB, RB), 0)
    col_at = lax.broadcasted_iota(jnp.int32, (RB, RB), 1)

    def score(i, _):
        kb, j, y = place(i)
        visible = (q_doc == seg_row[kb]) & (kb * RB + col_at <= row_at)
        for n, (src, h) in enumerate(pairs):
            cols = slice(h * HD, (h + 1) * HD)
            s = lax.dot_general(
                qs[src][0, :, cols], kv[src, j, y, :, cols], (((1,), (1,)), ((), ())),
                preferred_element_type=F32,
            )
            s = jnp.where(visible, s, -1e30)
            scores[n, i] = s
            tops[n] = jnp.maximum(tops[n], jnp.maximum(s[:, :HD], s[:, HD:]))
        return 0

    lax.fori_loop(0, count, score, 0)
    for n in range(len(pairs)):
        tops[n] = jnp.broadcast_to(jnp.max(tops[n], axis=-1, keepdims=True), (RB, HD))

    def expo(i, _):
        for n in range(len(pairs)):
            s = scores[n, i]
            top = tops[n]
            left = jnp.exp2((s[:, :HD] - top) * factor)
            right = jnp.exp2((s[:, HD:] - top) * factor)
            scores[n, i, :, :HD] = left
            scores[n, i, :, HD:] = right
            sums[n] += left + right
        return 0

    lax.fori_loop(0, count, expo, 0)
    for n in range(len(pairs)):
        total = jnp.sum(sums[n], axis=-1, keepdims=True)
        sums[n] = jnp.broadcast_to(1.0 / total, (RB, HD))
        tops[n] = jnp.zeros((RB, HD), F32)

    def mix(i, _):
        kb, j, y = place(i)
        for n, (src, h) in enumerate(pairs):
            cols = slice((heads + h) * HD, (heads + h + 1) * HD)
            e = scores[n, i]
            inv = sums[n]
            weights = jnp.concatenate([e[:, :HD] * inv, e[:, HD:] * inv], axis=1).astype(BF)
            tops[n] += jnp.dot(weights, kv[src, j, y, :, cols], preferred_element_type=F32)
        return 0

    lax.fori_loop(0, count, mix, 0)
    for n in range(len(pairs)):
        out[:, n * HD : (n + 1) * HD] = tops[n].astype(BF)


def attend(meta, chunk, q_own, q_other, seg_row, pieces):
    n = q_own.shape[2]
    heads = n // HD
    whole = lambda a: pl.BlockSpec(a.shape, lambda t, m, nd=a.ndim: (0,) * nd)
    q_spec = pl.BlockSpec((1, RB, n), lambda t, m: (m[SLOT + 2 * chunk + t], 0, 0))
    once = lambda a: pl.BlockSpec(
        a.shape, lambda t, m, nd=a.ndim: (0,) * nd, pipeline_mode=pl.Buffered(1)
    )
    return pl.pallas_call(
        functools.partial(attend_kernel, chunk),
        grid_spec=pltpu.PrefetchScalarGridSpec(
            num_scalar_prefetch=1,
            grid=(2,),
            in_specs=[q_spec, q_spec, whole(seg_row)] + list(map(once, pieces)),
            out_specs=pl.BlockSpec((RB, 2 * n), lambda t, m: (t, 0)),
            scratch_shapes=[
                pltpu.VMEM((2, 4, 2, RB, 2 * n), BF),
                pltpu.VMEM((2 * heads, 5, RB, RB), F32),
                pltpu.VMEM((2 * heads, RB, HD), F32),
                pltpu.VMEM((2 * heads, RB, HD), F32),
            ],
        ),
        out_shape=jax.ShapeDtypeStruct((2 * RB, 2 * n), BF),
        compiler_params=pltpu.CompilerParams(vmem_limit_bytes=32 * MIB),
        cost_estimate=pl.CostEstimate(
            flops=4 * 2 * RB * 768 * 2 * n, bytes_accessed=8 * MIB, transcendentals=2 * RB * 768 * 6
        ),
    )(meta, q_own, q_other, seg_row, *pieces)


def reorder_kernel(meta, w, out):
    out[...] = w[...]


def reorder(meta, w, swap):
    k8, n, width = w.shape
    return pl.pallas_call(
        reorder_kernel,
        grid_spec=pltpu.PrefetchScalarGridSpec(
            num_scalar_prefetch=1,
            grid=(k8,),
            in_specs=[
                pl.BlockSpec((1, n, width), lambda k, m: (m[ROWS + (k + swap - 2 * swap * (k % 2))], 0, 0))
            ],
            out_specs=pl.BlockSpec((1, n, width), lambda k, m: (k, 0, 0)),
        ),
        out_shape=jax.ShapeDtypeStruct(w.shape, BF),
        compiler_params=pltpu.CompilerParams(vmem_limit_bytes=4 * MIB),
    )(meta, w).reshape(k8 * n, width)


def finish_kernel(meta, c0, c1, c2a, c2b, c3, w, res, *refs):
    out = refs[-1]
    t = pl.program_id(0)
    far = jnp.where(t == 0, c2a[...], c2b[...])
    n = far.shape[1]
    total = res[0].astype(F32)
    for j, c in enumerate((c0[...], c1[...], far, c3[...])):
        total += jnp.dot(c, w[j * n : (j + 1) * n, :], preferred_element_type=F32)
    out[0] = total.astype(BF)


def finish(meta, chunk, parts, w, res, blocks, prior=None):
    depth, width = w.shape
    n = depth // 4
    tile = pl.BlockSpec((RB, n), lambda t, m: (t, 0))
    fixed = lambda a: pl.BlockSpec(a.shape, lambda t, m: (0, 0))
    ins = list(parts) + [w, res]
    specs = [tile, tile, fixed(parts[2]), fixed(parts[3]), tile]
    specs.append(pl.BlockSpec(w.shape, lambda t, m: (0, 0), pipeline_mode=pl.Buffered(1)))
    specs.append(pl.BlockSpec((1, RB, width), lambda t, m: (m[SLOT + 2 * chunk + t], 0, 0)))
    aliases = {}
    if prior is not None:
        aliases[1 + len(ins)] = 0
        ins.append(prior)
        specs.append(pl.BlockSpec(memory_space=pl.ANY))
    if blocks == 2:
        target = lambda t, m: (t, 0, 0)
    else:
        target = lambda t, m: (m[MINE + 2 * chunk + t], 0, 0)
    return pl.pallas_call(
        finish_kernel,
        grid_spec=pltpu.PrefetchScalarGridSpec(
            num_scalar_prefetch=1,
            grid=(2,),
            in_specs=specs,
            out_specs=pl.BlockSpec((1, RB, width), target),
        ),
        out_shape=jax.ShapeDtypeStruct((blocks, RB, width), BF),
        input_output_aliases=aliases,
        compiler_params=pltpu.CompilerParams(vmem_limit_bytes=20 * MIB),
        cost_estimate=pl.CostEstimate(
            flops=4 * RB * depth * width, bytes_accessed=8 * MIB, transcendentals=0
        ),
    )(meta, *ins)


def place_kernel(chunk, meta, got, prior, out, sems):
    copies = [
        pltpu.make_async_copy(got.at[t], out.at[meta[THEIRS + 2 * chunk + t]], sems.at[t])
        for t in range(2)
    ]
    for copy in copies:
        copy.start()
    for copy in copies:
        copy.wait()


def place(meta, chunk, got, prior):
    in_place = pl.BlockSpec(memory_space=pl.ANY)
    return pl.pallas_call(
        functools.partial(place_kernel, chunk),
        grid_spec=pltpu.PrefetchScalarGridSpec(
            num_scalar_prefetch=1,
            grid=(1,),
            in_specs=[pl.BlockSpec(got.shape, lambda t, m: (0, 0, 0)), in_place],
            out_specs=in_place,
            scratch_shapes=[pltpu.SemaphoreType.DMA((2,))],
        ),
        out_shape=jax.ShapeDtypeStruct(prior.shape, BF),
        input_output_aliases={2: 0},
        compiler_params=pltpu.CompilerParams(vmem_limit_bytes=4 * MIB),
    )(meta, got, prior)


def after(value, *done):
    return lax.optimization_barrier((value,) + done)[0]


def body(
    section_input, last_hidden, kv_gain, query_gain, w_key, w_value, w_query, w_out, segment_ids
):
    section = lax.axis_index("section")
    c = lax.axis_index("ctx")
    core = section % 2
    y_hi = section // 8
    x0 = section_input[0]
    w_q = w_query[0]
    w_o = w_out[0]
    width = w_o.shape[1]

    x_in = send(x0, IN)
    x_out = send(x0, OUT)

    meta = jnp.array(FACTS, jnp.int32)[section, c]
    seg_row = segment_ids.reshape(8, 1, RB)

    def cache(last_hidden, w_key, w_value, w_out):
        kv_in = normalize(last_hidden, kv_gain)
        own_k = jnp.dot(kv_in, w_key, preferred_element_type=F32).astype(BF)
        own_v = jnp.dot(kv_in, w_value, preferred_element_type=F32).astype(BF)
        kv = jnp.concatenate([own_k, own_v], axis=1)
        kv2 = send(kv, CORE)
        pair = jnp.where(core == 0, jnp.stack([kv, kv2]), jnp.stack([kv2, kv]))
        far = send(pair, FAR_Y)
        far, w_mine = lax.optimization_barrier((far, reorder(meta, w_out, 0)))
        far = jnp.where(core == 0, far, send(far, CORE))
        piece = jnp.where(y_hi == 0, jnp.stack([pair, far]), jnp.stack([far, pair]))
        piece = piece.reshape(2, 2 * kv.shape[0], kv.shape[1])
        piece2 = send(piece, PARTNER)
        share = lax.dynamic_index_in_dim(piece, core, 0, keepdims=False)
        o2 = send(share, X_FAR)
        return piece, share, o2, piece2, w_mine, reorder(meta, w_out, 1)

    def nothing(last_hidden, w_key, w_value, w_out):
        two = jnp.zeros((2, 2 * last_hidden.shape[0], 2 * w_key.shape[1]), BF)
        w_none = jnp.zeros((w_out.shape[0] * w_out.shape[1], w_out.shape[2]), BF)
        return two, two[0], two[0], two, w_none, w_none

    w_o_r = w_o.reshape(8, w_q.shape[1], width)
    piece, share, o2, piece2, w_o_mine, w_o_theirs = lax.cond(
        segment_ids[0] >= 0, cache, nothing, last_hidden, w_key, w_value, w_o_r
    )
    w_q2 = send(after(w_q, piece2), PARTNER)
    o1 = send(share, X_PREV)
    o3 = send(share, X_NEXT)
    x_in, x_out, piece2, share, o1, o3 = lax.optimization_barrier(
        (x_in, x_out, piece2, share, o1, o3)
    )
    most = RB * 5 // 8
    xo_a = send(x_out[:most], IN)
    xo_b = send(x_in[most:], OUT)
    t1 = send(piece2, X_PREV)
    t3 = send(piece2, X_NEXT)
    state = project(meta, [after(x0, x_in, x_out)], query_gain, w_q, 0, width)
    state = project(meta, [x_in], query_gain, w_q, 1, width, state)
    state = project(meta, [x_out], query_gain, w_q, 3, width, state)
    xo_b, t1, t3, o1, o2, o3, piece2, *state = lax.optimization_barrier(
        (xo_b, t1, t3, o1, o2, o3, piece2, *state)
    )
    t2 = send(piece2, X_FAR)
    o1b = send(o1, CORE)
    o2b = send(o2, CORE)
    o3b = send(o3, CORE)
    xo_a, o1b, o2b, o3b = lax.optimization_barrier((xo_a, o1b, o2b, o3b))
    normed, q_own, res_own, res_other = project(
        meta, [xo_a, xo_b], query_gain, w_q, 2, width, state
    )
    t2, w_q2, w_o_theirs, normed, q_own = lax.optimization_barrier(
        (t2, w_q2, w_o_theirs, normed, q_own)
    )
    w_o2 = send(w_o_theirs, PARTNER)
    q_other = more_queries(normed, w_q2)
    pieces = (piece, o1, o1b, o2, o2b, o3, o3b, piece2, t1, t2, t3)

    result = None
    parts = []
    for chunk in range(2):
        own = attend(meta, chunk, q_own, q_other, seg_row, pieces)
        c_in = send(own, IN)
        c_out = send(own, OUT)
        co_a = send(c_out[:CUT], IN)
        co_b = send(c_in[CUT:], OUT)
        parts.append((own, c_in, co_a, co_b, c_out))
    others = [finish(meta, chunk, parts[chunk], w_o2, res_other, 2) for chunk in range(2)]
    sent = [send(other, PARTNER) for other in others]
    w_o_mine = after(w_o_mine, *others)
    result = None
    for chunk in range(2):
        result = finish(meta, chunk, parts[chunk], w_o_mine, res_own, 8, result)
    for chunk in range(2):
        result = place(meta, chunk, sent[chunk], result)
    return result.reshape(1, 8 * RB, -1)


def solution(mesh):
    return jax.shard_map(
        body,
        mesh=mesh,
        in_specs=(
            P("section", "ctx", None),
            P("section", None),
            P(),
            P("section", None),
            P(None, "ctx"),
            P(None, "ctx"),
            P("section", None, "ctx"),
            P("section", None, "ctx"),
            P(),
        ),
        out_specs=P("section", None, "ctx"),
        check_vma=False,
    )
```

```python
import functools

import jax
import jax.numpy as jnp
from jax import lax
from jax.experimental import pallas as pl
from jax.experimental.pallas import tpu as pltpu
from jax.sharding import PartitionSpec as P

HD = 128
RB = 256
CUT = 320
BF = jnp.bfloat16
F32 = jnp.float32
AXES = ("section", "ctx")
MIB = 1 << 20

PLACE = (((0, 1, 2, 3), (4, 5, 6, 7)), ((1, 0, 4, 5), (2, 3, 7, 6)))
SPOT = tuple(
    tuple(next((h, r) for h in range(2) for r in range(4) if table[h][r] == c) for c in range(8))
    for table in PLACE
)

MINE, THEIRS, SLOT, ROWS, OWN, CORE_AT, X_AT = 0, 4, 8, 12, 20, 22, 23


def facts_of(section, c):
    core = section % 2
    half, r = SPOT[core][c]
    mine, theirs = PLACE[core][half], PLACE[core][1 - half]
    ring = [r, r ^ 1, (r + 2) % 4, 3 - r]
    slots = [ring.index(p) for p in range(4)]
    rows = [place[p] for p in ring for place in (mine, theirs)]
    return [*mine, *theirs, *slots, *rows, mine[r], theirs[r], core, section // 2 % 4]


FACTS = [[facts_of(section, c) for c in range(8)] for section in range(16)]


def moves(step):
    pairs = []
    for s in range(16):
        for c in range(8):
            core = s % 2
            half, spot = SPOT[core][c]
            yh, x, k, h, r = step(s // 8, s // 2 % 4, core, half, spot)
            if k == core:
                place = PLACE[core][h][r % 4]
            else:
                place = c
            pairs.append((s * 8 + c, (yh * 8 + x % 4 * 2 + k) * 8 + place))
    return pairs


IN = moves(lambda yh, x, k, h, r: (yh, x, k, h, r ^ 1))
OUT = moves(lambda yh, x, k, h, r: (yh, x, k, h, 3 - r))
PARTNER = moves(lambda yh, x, k, h, r: (yh, x, k, 1 - h, r))
CORE = moves(lambda yh, x, k, h, r: (yh, x, 1 - k, h, r))
FAR_Y = [
    (a, b) for a, b in moves(lambda yh, x, k, h, r: (1 - yh, x, k, h, r)) if a // 8 % 2 == 0
]
X_NEXT = moves(lambda yh, x, k, h, r: (yh, x + 1, k, h, r))
X_PREV = moves(lambda yh, x, k, h, r: (yh, x - 1, k, h, r))
X_FAR = moves(lambda yh, x, k, h, r: (yh, x + 2, k, h, r))


def send(value, pairs):
    return lax.ppermute(value, AXES, pairs)


def normalize(rows, gain):
    full = rows.astype(F32)
    scaled = full * lax.rsqrt(jnp.mean(full * full, axis=-1, keepdims=True) + 1e-05) * gain
    return scaled.astype(BF)


def project_kernel(pieces, meta, *refs):
    xs = refs[:pieces]
    gain, w = refs[pieces : pieces + 2]
    normed, q, res_own, res_other = refs[-4:]
    step = 32
    base = 0
    for x in xs:
        rows = x.shape[0]

        def norm_rows(i, _, x=x, base=base):
            at = pl.multiple_of(i * step, step)
            full = x[pl.ds(at, step), :].astype(F32)
            mean = jnp.mean(full * full, axis=-1, keepdims=True)
            normed[0, pl.ds(base + at, step), :] = (
                full * lax.rsqrt(mean + 1e-05) * gain[...]
            ).astype(BF)
            return 0

        lax.fori_loop(0, rows // step, norm_rows, 0)
        width = res_own.shape[2]
        for k, out in ((0, res_own), (1, res_other)):
            first = pl.multiple_of(meta[OWN + k] * width, 128)
            out[0, base : base + rows, :] = x[:, pl.ds(first, width)]
        base += rows
    q[0] = jnp.dot(normed[0], w[...], preferred_element_type=F32).astype(BF)


def project(meta, xs, gain, w, slot, width, prior=None):
    d, n = w.shape
    shapes = [(4, RB, d), (4, RB, n), (4, RB, width), (4, RB, width)]
    whole = lambda a: pl.BlockSpec(
        a.shape, lambda i, m, nd=a.ndim: (0,) * nd, pipeline_mode=pl.Buffered(1)
    )
    ins = list(xs) + [gain, w]
    specs = [whole(a) for a in ins]
    aliases = {}
    for k, a in enumerate(prior or ()):
        aliases[1 + len(ins)] = k
        ins.append(a)
        specs.append(pl.BlockSpec(memory_space=pl.ANY))

    def kernel(meta, *refs):
        project_kernel(len(xs), meta, *refs)

    return pl.pallas_call(
        kernel,
        grid_spec=pltpu.PrefetchScalarGridSpec(
            num_scalar_prefetch=1,
            grid=(1,),
            in_specs=specs,
            out_specs=[pl.BlockSpec((1,) + s[1:], lambda i, m: (slot, 0, 0)) for s in shapes],
        ),
        out_shape=[jax.ShapeDtypeStruct(s, BF) for s in shapes],
        input_output_aliases=aliases,
        compiler_params=pltpu.CompilerParams(vmem_limit_bytes=20 * MIB),
        cost_estimate=pl.CostEstimate(
            flops=0, bytes_accessed=0, transcendentals=0
        ),
    )(meta, *ins)


def more_queries_kernel(n_ref, w_ref, q_ref):
    q_ref[...] = jnp.dot(n_ref[...], w_ref[...], preferred_element_type=F32).astype(BF)


def more_queries(normed, w):
    d, n = w.shape
    rows = 2 * RB
    return pl.pallas_call(
        more_queries_kernel,
        grid=(2,),
        in_specs=[
            pl.BlockSpec((rows, d), lambda i: (i, 0)),
            pl.BlockSpec(w.shape, lambda i: (0, 0), pipeline_mode=pl.Buffered(1)),
        ],
        out_specs=pl.BlockSpec((rows, n), lambda i: (i, 0)),
        out_shape=jax.ShapeDtypeStruct((4 * RB, n), BF),
        compiler_params=pltpu.CompilerParams(vmem_limit_bytes=20 * MIB),
        cost_estimate=pl.CostEstimate(
            flops=0, bytes_accessed=0, transcendentals=0
        ),
    )(normed.reshape(4 * RB, d), w).reshape(4, RB, n)


def attend_kernel(
    chunk, meta, q_own, q_other, seg_row, own0, o1, o1b, o2, o2b, o3, o3b,
    other0, t1, t2, t3,
    out, kv, scores, tops, sums,
):
    t = pl.program_id(0)
    core = meta[CORE_AT]

    @pl.when(t == 0)
    def _():
        kv[0, 0] = own0[...]
        kv[0, 1, core] = o1[...]
        kv[0, 1, 1 - core] = o1b[...]
        kv[0, 2, core] = o2[...]
        kv[0, 2, 1 - core] = o2b[...]
        kv[0, 3, core] = o3[...]
        kv[0, 3, 1 - core] = o3b[...]
        kv[1, 0] = other0[...]
        kv[1, 1] = t1[...]
        kv[1, 2] = t2[...]
        kv[1, 3] = t3[...]

    block = meta[MINE + 2 * chunk + t]
    earlier = (seg_row[...] < seg_row[block, :, :1]).astype(F32)
    first = jnp.maximum(jnp.sum(earlier).astype(jnp.int32) // RB, block - 4)
    count = block - first + 1
    x = meta[X_AT]
    heads = q_own.shape[2] // HD
    factor = HD ** (-0.5) * 1.4426950408889634
    pairs = [(src, i) for src in range(2) for i in range(heads)]
    qs = (q_own, q_other)

    def place(i):
        kb = first + i
        j = lax.rem(lax.rem(kb, 4) - x + 4, 4)
        return kb, j, kb // 4

    tops[...] = jnp.full(tops.shape, -1e30, F32)
    sums[...] = jnp.zeros(sums.shape, F32)
    q_doc = jnp.transpose(jnp.broadcast_to(seg_row[block], (RB, RB)))
    row_at = block * RB + lax.broadcasted_iota(jnp.int32, (RB, RB), 0)
    col_at = lax.broadcasted_iota(jnp.int32, (RB, RB), 1)

    def score(i, _):
        kb, j, y = place(i)
        visible = (q_doc == seg_row[kb]) & (kb * RB + col_at <= row_at)
        for n, (src, h) in enumerate(pairs):
            cols = slice(h * HD, (h + 1) * HD)
            s = lax.dot_general(
                qs[src][0, :, cols], kv[src, j, y, :, cols], (((1,), (1,)), ((), ())),
                preferred_element_type=F32,
            )
            s = jnp.where(visible, s, -1e30)
            scores[n, i] = s
            tops[n] = jnp.maximum(tops[n], jnp.maximum(s[:, :HD], s[:, HD:]))
        return 0

    lax.fori_loop(0, count, score, 0)
    for n in range(len(pairs)):
        tops[n] = jnp.broadcast_to(jnp.max(tops[n], axis=-1, keepdims=True), (RB, HD))

    def expo(i, _):
        for n in range(len(pairs)):
            s = scores[n, i]
            top = tops[n]
            left = jnp.exp2((s[:, :HD] - top) * factor)
            right = jnp.exp2((s[:, HD:] - top) * factor)
            scores[n, i, :, :HD] = left
            scores[n, i, :, HD:] = right
            sums[n] += left + right
        return 0

    lax.fori_loop(0, count, expo, 0)
    for n in range(len(pairs)):
        total = jnp.sum(sums[n], axis=-1, keepdims=True)
        sums[n] = jnp.broadcast_to(1.0 / total, (RB, HD))
        tops[n] = jnp.zeros((RB, HD), F32)

    def mix(i, _):
        kb, j, y = place(i)
        for n, (src, h) in enumerate(pairs):
            cols = slice((heads + h) * HD, (heads + h + 1) * HD)
            e = scores[n, i]
            inv = sums[n]
            weights = jnp.concatenate([e[:, :HD] * inv, e[:, HD:] * inv], axis=1).astype(BF)
            tops[n] += jnp.dot(weights, kv[src, j, y, :, cols], preferred_element_type=F32)
        return 0

    lax.fori_loop(0, count, mix, 0)
    for n in range(len(pairs)):
        out[:, n * HD : (n + 1) * HD] = tops[n].astype(BF)


def attend(meta, chunk, q_own, q_other, seg_row, pieces):
    n = q_own.shape[2]
    heads = n // HD
    whole = lambda a: pl.BlockSpec(a.shape, lambda t, m, nd=a.ndim: (0,) * nd)
    q_spec = pl.BlockSpec((1, RB, n), lambda t, m: (m[SLOT + 2 * chunk + t], 0, 0))
    once = lambda a: pl.BlockSpec(
        a.shape, lambda t, m, nd=a.ndim: (0,) * nd, pipeline_mode=pl.Buffered(1)
    )
    return pl.pallas_call(
        functools.partial(attend_kernel, chunk),
        grid_spec=pltpu.PrefetchScalarGridSpec(
            num_scalar_prefetch=1,
            grid=(2,),
            in_specs=[q_spec, q_spec, whole(seg_row)] + list(map(once, pieces)),
            out_specs=pl.BlockSpec((RB, 2 * n), lambda t, m: (t, 0)),
            scratch_shapes=[
                pltpu.VMEM((2, 4, 2, RB, 2 * n), BF),
                pltpu.VMEM((2 * heads, 5, RB, RB), F32),
                pltpu.VMEM((2 * heads, RB, HD), F32),
                pltpu.VMEM((2 * heads, RB, HD), F32),
            ],
        ),
        out_shape=jax.ShapeDtypeStruct((2 * RB, 2 * n), BF),
        compiler_params=pltpu.CompilerParams(vmem_limit_bytes=32 * MIB),
        cost_estimate=pl.CostEstimate(
            flops=4 * 2 * RB * 768 * 2 * n, bytes_accessed=8 * MIB, transcendentals=2 * RB * 768 * 6
        ),
    )(meta, q_own, q_other, seg_row, *pieces)


def reorder_kernel(meta, w, out):
    out[...] = w[...]


def reorder(meta, w, swap):
    k8, n, width = w.shape
    return pl.pallas_call(
        reorder_kernel,
        grid_spec=pltpu.PrefetchScalarGridSpec(
            num_scalar_prefetch=1,
            grid=(k8,),
            in_specs=[
                pl.BlockSpec((1, n, width), lambda k, m: (m[ROWS + (k + swap - 2 * swap * (k % 2))], 0, 0))
            ],
            out_specs=pl.BlockSpec((1, n, width), lambda k, m: (k, 0, 0)),
        ),
        out_shape=jax.ShapeDtypeStruct(w.shape, BF),
        compiler_params=pltpu.CompilerParams(vmem_limit_bytes=4 * MIB),
    )(meta, w).reshape(k8 * n, width)


def finish_kernel(meta, c0, c1, c2a, c2b, c3, w, res, *refs):
    out = refs[-1]
    t = pl.program_id(0)
    far = jnp.where(t == 0, c2a[:RB, :], jnp.concatenate([c2a[RB:, :], c2b[...]], axis=0))
    n = far.shape[1]
    total = res[0].astype(F32)
    for j, c in enumerate((c0[...], c1[...], far, c3[...])):
        total += jnp.dot(c, w[j * n : (j + 1) * n, :], preferred_element_type=F32)
    out[0] = total.astype(BF)


def finish(meta, chunk, parts, w, res, blocks, prior=None):
    depth, width = w.shape
    n = depth // 4
    tile = pl.BlockSpec((RB, n), lambda t, m: (t, 0))
    fixed = lambda a: pl.BlockSpec(a.shape, lambda t, m: (0, 0))
    ins = list(parts) + [w, res]
    specs = [tile, tile, fixed(parts[2]), fixed(parts[3]), tile]
    specs.append(pl.BlockSpec(w.shape, lambda t, m: (0, 0), pipeline_mode=pl.Buffered(1)))
    specs.append(pl.BlockSpec((1, RB, width), lambda t, m: (m[SLOT + 2 * chunk + t], 0, 0)))
    aliases = {}
    if prior is not None:
        aliases[1 + len(ins)] = 0
        ins.append(prior)
        specs.append(pl.BlockSpec(memory_space=pl.ANY))
    if blocks == 2:
        target = lambda t, m: (t, 0, 0)
    else:
        target = lambda t, m: (m[MINE + 2 * chunk + t], 0, 0)
    return pl.pallas_call(
        finish_kernel,
        grid_spec=pltpu.PrefetchScalarGridSpec(
            num_scalar_prefetch=1,
            grid=(2,),
            in_specs=specs,
            out_specs=pl.BlockSpec((1, RB, width), target),
        ),
        out_shape=jax.ShapeDtypeStruct((blocks, RB, width), BF),
        input_output_aliases=aliases,
        compiler_params=pltpu.CompilerParams(vmem_limit_bytes=20 * MIB),
        cost_estimate=pl.CostEstimate(
            flops=4 * RB * depth * width, bytes_accessed=8 * MIB, transcendentals=0
        ),
    )(meta, *ins)


def place_kernel(chunk, meta, got, prior, out, sems):
    copies = [
        pltpu.make_async_copy(got.at[t], out.at[meta[THEIRS + 2 * chunk + t]], sems.at[t])
        for t in range(2)
    ]
    for copy in copies:
        copy.start()
    for copy in copies:
        copy.wait()


def place(meta, chunk, got, prior):
    in_place = pl.BlockSpec(memory_space=pl.ANY)
    return pl.pallas_call(
        functools.partial(place_kernel, chunk),
        grid_spec=pltpu.PrefetchScalarGridSpec(
            num_scalar_prefetch=1,
            grid=(1,),
            in_specs=[pl.BlockSpec(got.shape, lambda t, m: (0, 0, 0)), in_place],
            out_specs=in_place,
            scratch_shapes=[pltpu.SemaphoreType.DMA((2,))],
        ),
        out_shape=jax.ShapeDtypeStruct(prior.shape, BF),
        input_output_aliases={2: 0},
        compiler_params=pltpu.CompilerParams(vmem_limit_bytes=4 * MIB),
    )(meta, got, prior)


def after(value, *done):
    return lax.optimization_barrier((value,) + done)[0]


def body(
    section_input, last_hidden, kv_gain, query_gain, w_key, w_value, w_query, w_out, segment_ids
):
    section = lax.axis_index("section")
    c = lax.axis_index("ctx")
    core = section % 2
    y_hi = section // 8
    x0 = section_input[0]
    w_q = w_query[0]
    w_o = w_out[0]
    width = w_o.shape[1]

    x_in = send(x0, IN)
    x_out = send(x0, OUT)

    meta = jnp.array(FACTS, jnp.int32)[section, c]
    seg_row = segment_ids.reshape(8, 1, RB)

    def cache(last_hidden, w_key, w_value, w_out):
        kv_in = normalize(last_hidden, kv_gain)
        own_k = jnp.dot(kv_in, w_key, preferred_element_type=F32).astype(BF)
        own_v = jnp.dot(kv_in, w_value, preferred_element_type=F32).astype(BF)
        kv = jnp.concatenate([own_k, own_v], axis=1)
        kv2 = send(kv, CORE)
        pair = jnp.where(core == 0, jnp.stack([kv, kv2]), jnp.stack([kv2, kv]))
        far = send(pair, FAR_Y)
        far, w_mine = lax.optimization_barrier((far, reorder(meta, w_out, 0)))
        far = jnp.where(core == 0, far, send(far, CORE))
        piece = jnp.where(y_hi == 0, jnp.stack([pair, far]), jnp.stack([far, pair]))
        piece = piece.reshape(2, 2 * kv.shape[0], kv.shape[1])
        piece2 = send(piece, PARTNER)
        share = lax.dynamic_index_in_dim(piece, core, 0, keepdims=False)
        o2 = send(share, X_FAR)
        return piece, share, o2, piece2, w_mine, reorder(meta, w_out, 1)

    def nothing(last_hidden, w_key, w_value, w_out):
        two = jnp.zeros((2, 2 * last_hidden.shape[0], 2 * w_key.shape[1]), BF)
        w_none = jnp.zeros((w_out.shape[0] * w_out.shape[1], w_out.shape[2]), BF)
        return two, two[0], two[0], two, w_none, w_none

    w_o_r = w_o.reshape(8, w_q.shape[1], width)
    piece, share, o2, piece2, w_o_mine, w_o_theirs = lax.cond(
        segment_ids[0] >= 0, cache, nothing, last_hidden, w_key, w_value, w_o_r
    )
    w_q2 = send(after(w_q, piece2), PARTNER)
    o1 = send(share, X_PREV)
    o3 = send(share, X_NEXT)
    x_in, x_out, piece2, share, o1, o3 = lax.optimization_barrier(
        (x_in, x_out, piece2, share, o1, o3)
    )
    most = RB * 5 // 8
    xo_a = send(x_out[:most], IN)
    xo_b = send(x_in[most:], OUT)
    t1 = send(piece2, X_PREV)
    t3 = send(piece2, X_NEXT)
    state = project(meta, [after(x0, x_in, x_out)], query_gain, w_q, 0, width)
    state = project(meta, [x_in], query_gain, w_q, 1, width, state)
    state = project(meta, [x_out], query_gain, w_q, 3, width, state)
    t1, t3, piece2, *state = lax.optimization_barrier((t1, t3, piece2, *state))
    t2 = send(piece2, X_FAR)
    o1, o2, o3, t1 = lax.optimization_barrier((o1, o2, o3, t1))
    o1b = send(o1, CORE)
    o2b = send(o2, CORE)
    o3b = send(o3, CORE)
    xo_a, xo_b, o1b, o2b, o3b = lax.optimization_barrier((xo_a, xo_b, o1b, o2b, o3b))
    normed, q_own, res_own, res_other = project(
        meta, [xo_a, xo_b], query_gain, w_q, 2, width, state
    )
    t2, w_q2, w_o_theirs, normed, q_own = lax.optimization_barrier(
        (t2, w_q2, w_o_theirs, normed, q_own)
    )
    w_o2 = send(w_o_theirs, PARTNER)
    q_other = more_queries(normed, w_q2)
    pieces = (piece, o1, o1b, o2, o2b, o3, o3b, piece2, t1, t2, t3)

    result = None
    parts = []
    for chunk in range(2):
        own = attend(meta, chunk, q_own, q_other, seg_row, pieces)
        c_in = send(own, IN)
        c_out = send(own, OUT)
        if parts:
            ours, c_in_0, co_a_0, co_b_0, c_out_0 = parts[0]
            c_in, c_out, co_b_0 = lax.optimization_barrier((c_in, c_out, co_b_0))
            parts[0] = (ours, c_in_0, co_a_0, co_b_0, c_out_0)
        else:
            c_in, c_out = lax.optimization_barrier((c_in, c_out))
        co_a = send(c_out[:CUT], IN)
        co_b = send(c_in[CUT:], OUT)
        parts.append((own, c_in, co_a, co_b, c_out))
    others = [finish(meta, chunk, parts[chunk], w_o2, res_other, 2) for chunk in range(2)]
    sent = [send(other, PARTNER) for other in others]
    w_o_mine = after(w_o_mine, *others)
    result = None
    for chunk in range(2):
        result = finish(meta, chunk, parts[chunk], w_o_mine, res_own, 8, result)
    for chunk in range(2):
        result = place(meta, chunk, sent[chunk], result)
    return result.reshape(1, 8 * RB, -1)


def solution(mesh):
    return jax.shard_map(
        body,
        mesh=mesh,
        in_specs=(
            P("section", "ctx", None),
            P("section", None),
            P(),
            P("section", None),
            P(None, "ctx"),
            P(None, "ctx"),
            P("section", None, "ctx"),
            P("section", None, "ctx"),
            P(),
        ),
        out_specs=P("section", None, "ctx"),
        check_vma=False,
    )
```

```python
import functools

import jax
import jax.numpy as jnp
from jax import lax
from jax.experimental import pallas as pl
from jax.experimental.pallas import tpu as pltpu
from jax.sharding import PartitionSpec as P

HD = 128
RB = 256
CUT = 384
BF = jnp.bfloat16
F32 = jnp.float32
AXES = ("section", "ctx")
MIB = 1 << 20

PLACE = (((0, 1, 2, 3), (4, 5, 6, 7)), ((1, 0, 4, 5), (2, 3, 7, 6)))
SPOT = tuple(
    tuple(next((h, r) for h in range(2) for r in range(4) if table[h][r] == c) for c in range(8))
    for table in PLACE
)

MINE, THEIRS, SLOT, ROWS, OWN, CORE_AT, X_AT = 0, 4, 8, 12, 20, 22, 23


def facts_of(section, c):
    core = section % 2
    half, r = SPOT[core][c]
    mine, theirs = PLACE[core][half], PLACE[core][1 - half]
    ring = [r, r ^ 1, (r + 2) % 4, 3 - r]
    slots = [ring.index(p) for p in range(4)]
    rows = [place[p] for p in ring for place in (mine, theirs)]
    return [*mine, *theirs, *slots, *rows, mine[r], theirs[r], core, section // 2 % 4]


FACTS = [[facts_of(section, c) for c in range(8)] for section in range(16)]


def moves(step):
    pairs = []
    for s in range(16):
        for c in range(8):
            core = s % 2
            half, spot = SPOT[core][c]
            yh, x, k, h, r = step(s // 8, s // 2 % 4, core, half, spot)
            if k == core:
                place = PLACE[core][h][r % 4]
            else:
                place = c
            pairs.append((s * 8 + c, (yh * 8 + x % 4 * 2 + k) * 8 + place))
    return pairs


IN = moves(lambda yh, x, k, h, r: (yh, x, k, h, r ^ 1))
OUT = moves(lambda yh, x, k, h, r: (yh, x, k, h, 3 - r))
PARTNER = moves(lambda yh, x, k, h, r: (yh, x, k, 1 - h, r))
CORE = moves(lambda yh, x, k, h, r: (yh, x, 1 - k, h, r))
FAR_Y = [
    (a, b) for a, b in moves(lambda yh, x, k, h, r: (1 - yh, x, k, h, r)) if a // 8 % 2 == 0
]
X_NEXT = moves(lambda yh, x, k, h, r: (yh, x + 1, k, h, r))
X_PREV = moves(lambda yh, x, k, h, r: (yh, x - 1, k, h, r))
X_FAR = moves(lambda yh, x, k, h, r: (yh, x + 2, k, h, r))


def send(value, pairs):
    return lax.ppermute(value, AXES, pairs)


def normalize(rows, gain):
    full = rows.astype(F32)
    scaled = full * lax.rsqrt(jnp.mean(full * full, axis=-1, keepdims=True) + 1e-05) * gain
    return scaled.astype(BF)


def project_kernel(pieces, meta, *refs):
    xs = refs[:pieces]
    gain, w = refs[pieces : pieces + 2]
    normed, q, res_own, res_other = refs[-4:]
    step = 32
    base = 0
    for x in xs:
        rows = x.shape[0]

        def norm_rows(i, _, x=x, base=base):
            at = pl.multiple_of(i * step, step)
            full = x[pl.ds(at, step), :].astype(F32)
            mean = jnp.mean(full * full, axis=-1, keepdims=True)
            normed[0, pl.ds(base + at, step), :] = (
                full * lax.rsqrt(mean + 1e-05) * gain[...]
            ).astype(BF)
            return 0

        lax.fori_loop(0, rows // step, norm_rows, 0)
        width = res_own.shape[2]
        for k, out in ((0, res_own), (1, res_other)):
            first = pl.multiple_of(meta[OWN + k] * width, 128)
            out[0, base : base + rows, :] = x[:, pl.ds(first, width)]
        base += rows
    q[0] = jnp.dot(normed[0], w[...], preferred_element_type=F32).astype(BF)


def project(meta, xs, gain, w, slot, width, prior=None):
    d, n = w.shape
    shapes = [(4, RB, d), (4, RB, n), (4, RB, width), (4, RB, width)]
    whole = lambda a: pl.BlockSpec(
        a.shape, lambda i, m, nd=a.ndim: (0,) * nd, pipeline_mode=pl.Buffered(1)
    )
    ins = list(xs) + [gain, w]
    specs = [whole(a) for a in ins]
    aliases = {}
    for k, a in enumerate(prior or ()):
        aliases[1 + len(ins)] = k
        ins.append(a)
        specs.append(pl.BlockSpec(memory_space=pl.ANY))

    def kernel(meta, *refs):
        project_kernel(len(xs), meta, *refs)

    return pl.pallas_call(
        kernel,
        grid_spec=pltpu.PrefetchScalarGridSpec(
            num_scalar_prefetch=1,
            grid=(1,),
            in_specs=specs,
            out_specs=[pl.BlockSpec((1,) + s[1:], lambda i, m: (slot, 0, 0)) for s in shapes],
        ),
        out_shape=[jax.ShapeDtypeStruct(s, BF) for s in shapes],
        input_output_aliases=aliases,
        compiler_params=pltpu.CompilerParams(vmem_limit_bytes=20 * MIB),
        cost_estimate=pl.CostEstimate(
            flops=0, bytes_accessed=0, transcendentals=0
        ),
    )(meta, *ins)


def more_queries_kernel(n_ref, w_ref, q_ref):
    q_ref[...] = jnp.dot(n_ref[...], w_ref[...], preferred_element_type=F32).astype(BF)


def more_queries(normed, w):
    d, n = w.shape
    rows = 2 * RB
    return pl.pallas_call(
        more_queries_kernel,
        grid=(2,),
        in_specs=[
            pl.BlockSpec((rows, d), lambda i: (i, 0)),
            pl.BlockSpec(w.shape, lambda i: (0, 0), pipeline_mode=pl.Buffered(1)),
        ],
        out_specs=pl.BlockSpec((rows, n), lambda i: (i, 0)),
        out_shape=jax.ShapeDtypeStruct((4 * RB, n), BF),
        compiler_params=pltpu.CompilerParams(vmem_limit_bytes=20 * MIB),
        cost_estimate=pl.CostEstimate(
            flops=0, bytes_accessed=0, transcendentals=0
        ),
    )(normed.reshape(4 * RB, d), w).reshape(4, RB, n)


def attend_kernel(
    chunk, meta, q_own, q_other, seg_row, own0, o1, o1b, o2, o2b, o3, o3b,
    other0, t1, t2, t3,
    out, kv, scores, tops, sums,
):
    t = pl.program_id(0)
    core = meta[CORE_AT]

    @pl.when(t == 0)
    def _():
        kv[0, 0] = own0[...]
        kv[0, 1, core] = o1[...]
        kv[0, 1, 1 - core] = o1b[...]
        kv[0, 2, core] = o2[...]
        kv[0, 2, 1 - core] = o2b[...]
        kv[0, 3, core] = o3[...]
        kv[0, 3, 1 - core] = o3b[...]
        kv[1, 0] = other0[...]
        kv[1, 1] = t1[...]
        kv[1, 2] = t2[...]
        kv[1, 3] = t3[...]

    block = meta[MINE + 2 * chunk + t]
    earlier = (seg_row[...] < seg_row[block, :, :1]).astype(F32)
    first = jnp.maximum(jnp.sum(earlier).astype(jnp.int32) // RB, block - 4)
    count = block - first + 1
    x = meta[X_AT]
    heads = q_own.shape[2] // HD
    factor = HD ** (-0.5) * 1.4426950408889634
    pairs = [(src, i) for src in range(2) for i in range(heads)]
    qs = (q_own, q_other)

    def place(i):
        kb = first + i
        j = lax.rem(lax.rem(kb, 4) - x + 4, 4)
        return kb, j, kb // 4

    tops[...] = jnp.full(tops.shape, -1e30, F32)
    sums[...] = jnp.zeros(sums.shape, F32)
    q_doc = jnp.transpose(jnp.broadcast_to(seg_row[block], (RB, RB)))
    row_at = block * RB + lax.broadcasted_iota(jnp.int32, (RB, RB), 0)
    col_at = lax.broadcasted_iota(jnp.int32, (RB, RB), 1)

    def score(i, _):
        kb, j, y = place(i)
        visible = (q_doc == seg_row[kb]) & (kb * RB + col_at <= row_at)
        for n, (src, h) in enumerate(pairs):
            cols = slice(h * HD, (h + 1) * HD)
            s = lax.dot_general(
                qs[src][0, :, cols], kv[src, j, y, :, cols], (((1,), (1,)), ((), ())),
                preferred_element_type=F32,
            )
            s = jnp.where(visible, s, -1e30)
            scores[n, i] = s
            tops[n] = jnp.maximum(tops[n], jnp.maximum(s[:, :HD], s[:, HD:]))
        return 0

    lax.fori_loop(0, count, score, 0)
    for n in range(len(pairs)):
        tops[n] = jnp.broadcast_to(jnp.max(tops[n], axis=-1, keepdims=True), (RB, HD))

    def expo(i, _):
        for n in range(len(pairs)):
            s = scores[n, i]
            top = tops[n]
            left = jnp.exp2((s[:, :HD] - top) * factor)
            right = jnp.exp2((s[:, HD:] - top) * factor)
            scores[n, i, :, :HD] = left
            scores[n, i, :, HD:] = right
            sums[n] += left + right
        return 0

    lax.fori_loop(0, count, expo, 0)
    for n in range(len(pairs)):
        total = jnp.sum(sums[n], axis=-1, keepdims=True)
        sums[n] = jnp.broadcast_to(1.0 / total, (RB, HD))
        tops[n] = jnp.zeros((RB, HD), F32)

    def mix(i, _):
        kb, j, y = place(i)
        for n, (src, h) in enumerate(pairs):
            cols = slice((heads + h) * HD, (heads + h + 1) * HD)
            e = scores[n, i]
            inv = sums[n]
            weights = jnp.concatenate([e[:, :HD] * inv, e[:, HD:] * inv], axis=1).astype(BF)
            tops[n] += jnp.dot(weights, kv[src, j, y, :, cols], preferred_element_type=F32)
        return 0

    lax.fori_loop(0, count, mix, 0)
    for n in range(len(pairs)):
        out[:, n * HD : (n + 1) * HD] = tops[n].astype(BF)


def attend(meta, chunk, q_own, q_other, seg_row, pieces):
    n = q_own.shape[2]
    heads = n // HD
    whole = lambda a: pl.BlockSpec(a.shape, lambda t, m, nd=a.ndim: (0,) * nd)
    q_spec = pl.BlockSpec((1, RB, n), lambda t, m: (m[SLOT + 2 * chunk + t], 0, 0))
    once = lambda a: pl.BlockSpec(
        a.shape, lambda t, m, nd=a.ndim: (0,) * nd, pipeline_mode=pl.Buffered(1)
    )
    return pl.pallas_call(
        functools.partial(attend_kernel, chunk),
        grid_spec=pltpu.PrefetchScalarGridSpec(
            num_scalar_prefetch=1,
            grid=(2,),
            in_specs=[q_spec, q_spec, whole(seg_row)] + list(map(once, pieces)),
            out_specs=pl.BlockSpec((RB, 2 * n), lambda t, m: (t, 0)),
            scratch_shapes=[
                pltpu.VMEM((2, 4, 2, RB, 2 * n), BF),
                pltpu.VMEM((2 * heads, 5, RB, RB), F32),
                pltpu.VMEM((2 * heads, RB, HD), F32),
                pltpu.VMEM((2 * heads, RB, HD), F32),
            ],
        ),
        out_shape=jax.ShapeDtypeStruct((2 * RB, 2 * n), BF),
        compiler_params=pltpu.CompilerParams(vmem_limit_bytes=32 * MIB),
        cost_estimate=pl.CostEstimate(
            flops=4 * 2 * RB * 768 * 2 * n, bytes_accessed=8 * MIB, transcendentals=2 * RB * 768 * 6
        ),
    )(meta, q_own, q_other, seg_row, *pieces)


def reorder_kernel(meta, w, out):
    out[...] = w[...]


def reorder(meta, w, swap):
    k8, n, width = w.shape
    return pl.pallas_call(
        reorder_kernel,
        grid_spec=pltpu.PrefetchScalarGridSpec(
            num_scalar_prefetch=1,
            grid=(k8,),
            in_specs=[
                pl.BlockSpec((1, n, width), lambda k, m: (m[ROWS + (k + swap - 2 * swap * (k % 2))], 0, 0))
            ],
            out_specs=pl.BlockSpec((1, n, width), lambda k, m: (k, 0, 0)),
        ),
        out_shape=jax.ShapeDtypeStruct(w.shape, BF),
        compiler_params=pltpu.CompilerParams(vmem_limit_bytes=4 * MIB),
    )(meta, w).reshape(k8 * n, width)


def finish_kernel(meta, c0, c1, c2a, c2b, c3, w, res, *refs):
    out = refs[-1]
    t = pl.program_id(0)
    far = jnp.where(t == 0, c2a[:RB, :], jnp.concatenate([c2a[RB:, :], c2b[...]], axis=0))
    n = far.shape[1]
    total = res[0].astype(F32)
    for j, c in enumerate((c0[...], c1[...], far, c3[...])):
        total += jnp.dot(c, w[j * n : (j + 1) * n, :], preferred_element_type=F32)
    out[0] = total.astype(BF)


def finish(meta, chunk, parts, w, res, blocks, prior=None):
    depth, width = w.shape
    n = depth // 4
    tile = pl.BlockSpec((RB, n), lambda t, m: (t, 0))
    fixed = lambda a: pl.BlockSpec(a.shape, lambda t, m: (0, 0))
    ins = list(parts) + [w, res]
    specs = [tile, tile, fixed(parts[2]), fixed(parts[3]), tile]
    specs.append(pl.BlockSpec(w.shape, lambda t, m: (0, 0), pipeline_mode=pl.Buffered(1)))
    specs.append(pl.BlockSpec((1, RB, width), lambda t, m: (m[SLOT + 2 * chunk + t], 0, 0)))
    aliases = {}
    if prior is not None:
        aliases[1 + len(ins)] = 0
        ins.append(prior)
        specs.append(pl.BlockSpec(memory_space=pl.ANY))
    if blocks == 2:
        target = lambda t, m: (t, 0, 0)
    else:
        target = lambda t, m: (m[MINE + 2 * chunk + t], 0, 0)
    return pl.pallas_call(
        finish_kernel,
        grid_spec=pltpu.PrefetchScalarGridSpec(
            num_scalar_prefetch=1,
            grid=(2,),
            in_specs=specs,
            out_specs=pl.BlockSpec((1, RB, width), target),
        ),
        out_shape=jax.ShapeDtypeStruct((blocks, RB, width), BF),
        input_output_aliases=aliases,
        compiler_params=pltpu.CompilerParams(vmem_limit_bytes=20 * MIB),
        cost_estimate=pl.CostEstimate(
            flops=4 * RB * depth * width, bytes_accessed=8 * MIB, transcendentals=0
        ),
    )(meta, *ins)


def place_kernel(chunk, meta, got, prior, out, sems):
    copies = [
        pltpu.make_async_copy(got.at[t], out.at[meta[THEIRS + 2 * chunk + t]], sems.at[t])
        for t in range(2)
    ]
    for copy in copies:
        copy.start()
    for copy in copies:
        copy.wait()


def place(meta, chunk, got, prior):
    in_place = pl.BlockSpec(memory_space=pl.ANY)
    return pl.pallas_call(
        functools.partial(place_kernel, chunk),
        grid_spec=pltpu.PrefetchScalarGridSpec(
            num_scalar_prefetch=1,
            grid=(1,),
            in_specs=[pl.BlockSpec(got.shape, lambda t, m: (0, 0, 0)), in_place],
            out_specs=in_place,
            scratch_shapes=[pltpu.SemaphoreType.DMA((2,))],
        ),
        out_shape=jax.ShapeDtypeStruct(prior.shape, BF),
        input_output_aliases={2: 0},
        compiler_params=pltpu.CompilerParams(vmem_limit_bytes=4 * MIB),
    )(meta, got, prior)


def after(value, *done):
    return lax.optimization_barrier((value,) + done)[0]


def body(
    section_input, last_hidden, kv_gain, query_gain, w_key, w_value, w_query, w_out, segment_ids
):
    section = lax.axis_index("section")
    c = lax.axis_index("ctx")
    core = section % 2
    y_hi = section // 8
    x0 = section_input[0]
    w_q = w_query[0]
    w_o = w_out[0]
    width = w_o.shape[1]

    x_in = send(x0, IN)
    x_out = send(x0, OUT)

    meta = jnp.array(FACTS, jnp.int32)[section, c]
    seg_row = segment_ids.reshape(8, 1, RB)

    def cache(last_hidden, w_key, w_value, w_out):
        kv_in = normalize(last_hidden, kv_gain)
        own_k = jnp.dot(kv_in, w_key, preferred_element_type=F32).astype(BF)
        own_v = jnp.dot(kv_in, w_value, preferred_element_type=F32).astype(BF)
        kv = jnp.concatenate([own_k, own_v], axis=1)
        kv2 = send(kv, CORE)
        pair = jnp.where(core == 0, jnp.stack([kv, kv2]), jnp.stack([kv2, kv]))
        far = send(pair, FAR_Y)
        far, w_mine = lax.optimization_barrier((far, reorder(meta, w_out, 0)))
        far = jnp.where(core == 0, far, send(far, CORE))
        piece = jnp.where(y_hi == 0, jnp.stack([pair, far]), jnp.stack([far, pair]))
        piece = piece.reshape(2, 2 * kv.shape[0], kv.shape[1])
        piece2 = send(piece, PARTNER)
        share = lax.dynamic_index_in_dim(piece, core, 0, keepdims=False)
        o2 = send(share, X_FAR)
        return piece, share, o2, piece2, w_mine, reorder(meta, w_out, 1)

    def nothing(last_hidden, w_key, w_value, w_out):
        two = jnp.zeros((2, 2 * last_hidden.shape[0], 2 * w_key.shape[1]), BF)
        w_none = jnp.zeros((w_out.shape[0] * w_out.shape[1], w_out.shape[2]), BF)
        return two, two[0], two[0], two, w_none, w_none

    w_o_r = w_o.reshape(8, w_q.shape[1], width)
    piece, share, o2, piece2, w_o_mine, w_o_theirs = lax.cond(
        segment_ids[0] >= 0, cache, nothing, last_hidden, w_key, w_value, w_o_r
    )
    w_q2 = send(after(w_q, piece2), PARTNER)
    o1 = send(share, X_PREV)
    o3 = send(share, X_NEXT)
    x_in, x_out, piece2, share, o1, o3 = lax.optimization_barrier(
        (x_in, x_out, piece2, share, o1, o3)
    )
    most = RB * 5 // 8
    xo_a = send(x_out[:most], IN)
    xo_b = send(x_in[most:], OUT)
    t1 = send(piece2, X_PREV)
    t3 = send(piece2, X_NEXT)
    state = project(meta, [after(x0, x_in, x_out)], query_gain, w_q, 0, width)
    state = project(meta, [x_in], query_gain, w_q, 1, width, state)
    state = project(meta, [x_out], query_gain, w_q, 3, width, state)
    t1, t3, piece2, *state = lax.optimization_barrier((t1, t3, piece2, *state))
    t2 = send(piece2, X_FAR)
    o1, o2, o3, t1 = lax.optimization_barrier((o1, o2, o3, t1))
    o1b = send(o1, CORE)
    o2b = send(o2, CORE)
    o3b = send(o3, CORE)
    xo_a, xo_b, o1b, o2b, o3b = lax.optimization_barrier((xo_a, xo_b, o1b, o2b, o3b))
    normed, q_own, res_own, res_other = project(
        meta, [xo_a, xo_b], query_gain, w_q, 2, width, state
    )
    t2, w_q2, w_o_theirs, normed, q_own = lax.optimization_barrier(
        (t2, w_q2, w_o_theirs, normed, q_own)
    )
    w_o2 = send(w_o_theirs, PARTNER)
    q_other = more_queries(normed, w_q2)
    pieces = (piece, o1, o1b, o2, o2b, o3, o3b, piece2, t1, t2, t3)

    result = None
    parts = []
    for chunk in range(2):
        own = attend(meta, chunk, q_own, q_other, seg_row, pieces)
        c_in = send(own, IN)
        c_out = send(own, OUT)
        if parts:
            ours, c_in_0, co_a_0, co_b_0, c_out_0 = parts[0]
            c_in, c_out, co_b_0 = lax.optimization_barrier((c_in, c_out, co_b_0))
            parts[0] = (ours, c_in_0, co_a_0, co_b_0, c_out_0)
        else:
            c_in, c_out = lax.optimization_barrier((c_in, c_out))
        co_a = send(c_out[:CUT], IN)
        co_b = send(c_in[CUT:], OUT)
        parts.append((own, c_in, co_a, co_b, c_out))
    others = [finish(meta, chunk, parts[chunk], w_o2, res_other, 2) for chunk in range(2)]
    sent = [send(other, PARTNER) for other in others]
    w_o_mine = after(w_o_mine, *others)
    result = None
    for chunk in range(2):
        result = finish(meta, chunk, parts[chunk], w_o_mine, res_own, 8, result)
    for chunk in range(2):
        result = place(meta, chunk, sent[chunk], result)
    return result.reshape(1, 8 * RB, -1)


def solution(mesh):
    return jax.shard_map(
        body,
        mesh=mesh,
        in_specs=(
            P("section", "ctx", None),
            P("section", None),
            P(),
            P("section", None),
            P(None, "ctx"),
            P(None, "ctx"),
            P("section", None, "ctx"),
            P("section", None, "ctx"),
            P(),
        ),
        out_specs=P("section", None, "ctx"),
        check_vma=False,
    )
```

```python
import functools

import jax
import jax.numpy as jnp
from jax import lax
from jax.experimental import pallas as pl
from jax.experimental.pallas import tpu as pltpu
from jax.sharding import PartitionSpec as P

HD = 128
RB = 256
CUT = 320
BF = jnp.bfloat16
F32 = jnp.float32
AXES = ("section", "ctx")
MIB = 1 << 20

PLACE = (((0, 1, 2, 3), (4, 5, 6, 7)), ((1, 0, 4, 5), (2, 3, 7, 6)))
SPOT = tuple(
    tuple(next((h, r) for h in range(2) for r in range(4) if table[h][r] == c) for c in range(8))
    for table in PLACE
)

MINE, THEIRS, SLOT, ROWS, OWN, CORE_AT, X_AT = 0, 4, 8, 12, 20, 22, 23


def facts_of(section, c):
    core = section % 2
    half, r = SPOT[core][c]
    mine, theirs = PLACE[core][half], PLACE[core][1 - half]
    ring = [r, r ^ 1, (r + 2) % 4, 3 - r]
    slots = [ring.index(p) for p in range(4)]
    rows = [place[p] for p in ring for place in (mine, theirs)]
    return [*mine, *theirs, *slots, *rows, mine[r], theirs[r], core, section // 2 % 4]


FACTS = [[facts_of(section, c) for c in range(8)] for section in range(16)]


def moves(step):
    pairs = []
    for s in range(16):
        for c in range(8):
            core = s % 2
            half, spot = SPOT[core][c]
            yh, x, k, h, r = step(s // 8, s // 2 % 4, core, half, spot)
            if k == core:
                place = PLACE[core][h][r % 4]
            else:
                place = c
            pairs.append((s * 8 + c, (yh * 8 + x % 4 * 2 + k) * 8 + place))
    return pairs


IN = moves(lambda yh, x, k, h, r: (yh, x, k, h, r ^ 1))
OUT = moves(lambda yh, x, k, h, r: (yh, x, k, h, 3 - r))
PARTNER = moves(lambda yh, x, k, h, r: (yh, x, k, 1 - h, r))
CORE = moves(lambda yh, x, k, h, r: (yh, x, 1 - k, h, r))
FAR_Y = [
    (a, b) for a, b in moves(lambda yh, x, k, h, r: (1 - yh, x, k, h, r)) if a // 8 % 2 == 0
]
X_NEXT = moves(lambda yh, x, k, h, r: (yh, x + 1, k, h, r))
X_PREV = moves(lambda yh, x, k, h, r: (yh, x - 1, k, h, r))
X_FAR = moves(lambda yh, x, k, h, r: (yh, x + 2, k, h, r))


def send(value, pairs):
    return lax.ppermute(value, AXES, pairs)


def normalize(rows, gain):
    full = rows.astype(F32)
    scaled = full * lax.rsqrt(jnp.mean(full * full, axis=-1, keepdims=True) + 1e-05) * gain
    return scaled.astype(BF)


def project_kernel(pieces, meta, *refs):
    xs = refs[:pieces]
    gain, w = refs[pieces : pieces + 2]
    normed, q, res_own, res_other = refs[-4:]
    step = 32
    base = 0
    for x in xs:
        rows = x.shape[0]

        def norm_rows(i, _, x=x, base=base):
            at = pl.multiple_of(i * step, step)
            full = x[pl.ds(at, step), :].astype(F32)
            mean = jnp.mean(full * full, axis=-1, keepdims=True)
            normed[0, pl.ds(base + at, step), :] = (
                full * lax.rsqrt(mean + 1e-05) * gain[...]
            ).astype(BF)
            return 0

        lax.fori_loop(0, rows // step, norm_rows, 0)
        width = res_own.shape[2]
        for k, out in ((0, res_own), (1, res_other)):
            first = pl.multiple_of(meta[OWN + k] * width, 128)
            out[0, base : base + rows, :] = x[:, pl.ds(first, width)]
        base += rows
    q[0] = jnp.dot(normed[0], w[...], preferred_element_type=F32).astype(BF)


def project(meta, xs, gain, w, slot, width, prior=None):
    d, n = w.shape
    shapes = [(4, RB, d), (4, RB, n), (4, RB, width), (4, RB, width)]
    whole = lambda a: pl.BlockSpec(
        a.shape, lambda i, m, nd=a.ndim: (0,) * nd, pipeline_mode=pl.Buffered(1)
    )
    ins = list(xs) + [gain, w]
    specs = [whole(a) for a in ins]
    aliases = {}
    for k, a in enumerate(prior or ()):
        aliases[1 + len(ins)] = k
        ins.append(a)
        specs.append(pl.BlockSpec(memory_space=pl.ANY))

    def kernel(meta, *refs):
        project_kernel(len(xs), meta, *refs)

    return pl.pallas_call(
        kernel,
        grid_spec=pltpu.PrefetchScalarGridSpec(
            num_scalar_prefetch=1,
            grid=(1,),
            in_specs=specs,
            out_specs=[pl.BlockSpec((1,) + s[1:], lambda i, m: (slot, 0, 0)) for s in shapes],
        ),
        out_shape=[jax.ShapeDtypeStruct(s, BF) for s in shapes],
        input_output_aliases=aliases,
        compiler_params=pltpu.CompilerParams(vmem_limit_bytes=20 * MIB),
        cost_estimate=pl.CostEstimate(
            flops=0, bytes_accessed=0, transcendentals=0
        ),
    )(meta, *ins)


def more_queries_kernel(n_ref, w_ref, q_ref):
    q_ref[...] = jnp.dot(n_ref[...], w_ref[...], preferred_element_type=F32).astype(BF)


def more_queries(normed, w):
    d, n = w.shape
    rows = 2 * RB
    return pl.pallas_call(
        more_queries_kernel,
        grid=(2,),
        in_specs=[
            pl.BlockSpec((rows, d), lambda i: (i, 0)),
            pl.BlockSpec(w.shape, lambda i: (0, 0), pipeline_mode=pl.Buffered(1)),
        ],
        out_specs=pl.BlockSpec((rows, n), lambda i: (i, 0)),
        out_shape=jax.ShapeDtypeStruct((4 * RB, n), BF),
        compiler_params=pltpu.CompilerParams(vmem_limit_bytes=20 * MIB),
        cost_estimate=pl.CostEstimate(
            flops=0, bytes_accessed=0, transcendentals=0
        ),
    )(normed.reshape(4 * RB, d), w).reshape(4, RB, n)


def attend_kernel(
    chunk, meta, q_own, q_other, seg_row, own0, o1, o1b, o2, o2b, o3, o3b,
    other0, t1, t2, t3,
    out, kv, scores, tops, sums,
):
    t = pl.program_id(0)
    core = meta[CORE_AT]

    @pl.when(t == 0)
    def _():
        kv[0, 0] = own0[...]
        kv[0, 1, core] = o1[...]
        kv[0, 1, 1 - core] = o1b[...]
        kv[0, 2, core] = o2[...]
        kv[0, 2, 1 - core] = o2b[...]
        kv[0, 3, core] = o3[...]
        kv[0, 3, 1 - core] = o3b[...]
        kv[1, 0] = other0[...]
        kv[1, 1] = t1[...]
        kv[1, 2] = t2[...]
        kv[1, 3] = t3[...]

    block = meta[MINE + 2 * chunk + t]
    earlier = (seg_row[...] < seg_row[block, :, :1]).astype(F32)
    first = jnp.maximum(jnp.sum(earlier).astype(jnp.int32) // RB, block - 4)
    count = block - first + 1
    x = meta[X_AT]
    heads = q_own.shape[2] // HD
    factor = HD ** (-0.5) * 1.4426950408889634
    pairs = [(src, i) for src in range(2) for i in range(heads)]
    qs = (q_own, q_other)

    def place(i):
        kb = first + i
        j = lax.rem(lax.rem(kb, 4) - x + 4, 4)
        return kb, j, kb // 4

    tops[...] = jnp.full(tops.shape, -1e30, F32)
    sums[...] = jnp.zeros(sums.shape, F32)
    q_doc = jnp.transpose(jnp.broadcast_to(seg_row[block], (RB, RB)))
    row_at = block * RB + lax.broadcasted_iota(jnp.int32, (RB, RB), 0)
    col_at = lax.broadcasted_iota(jnp.int32, (RB, RB), 1)

    def score(i, _):
        kb, j, y = place(i)
        visible = (q_doc == seg_row[kb]) & (kb * RB + col_at <= row_at)
        for n, (src, h) in enumerate(pairs):
            cols = slice(h * HD, (h + 1) * HD)
            s = lax.dot_general(
                qs[src][0, :, cols], kv[src, j, y, :, cols], (((1,), (1,)), ((), ())),
                preferred_element_type=F32,
            )
            s = jnp.where(visible, s, -1e30)
            scores[n, i] = s
            tops[n] = jnp.maximum(tops[n], jnp.maximum(s[:, :HD], s[:, HD:]))
        return 0

    lax.fori_loop(0, count, score, 0)
    for n in range(len(pairs)):
        tops[n] = jnp.broadcast_to(jnp.max(tops[n], axis=-1, keepdims=True), (RB, HD))

    def expo(i, _):
        for n in range(len(pairs)):
            s = scores[n, i]
            top = tops[n]
            left = jnp.exp2((s[:, :HD] - top) * factor)
            right = jnp.exp2((s[:, HD:] - top) * factor)
            scores[n, i, :, :HD] = left
            scores[n, i, :, HD:] = right
            sums[n] += left + right
        return 0

    lax.fori_loop(0, count, expo, 0)
    for n in range(len(pairs)):
        total = jnp.sum(sums[n], axis=-1, keepdims=True)
        sums[n] = jnp.broadcast_to(1.0 / total, (RB, HD))
        tops[n] = jnp.zeros((RB, HD), F32)

    def mix(i, _):
        kb, j, y = place(i)
        for n, (src, h) in enumerate(pairs):
            cols = slice((heads + h) * HD, (heads + h + 1) * HD)
            e = scores[n, i]
            inv = sums[n]
            weights = jnp.concatenate([e[:, :HD] * inv, e[:, HD:] * inv], axis=1).astype(BF)
            tops[n] += jnp.dot(weights, kv[src, j, y, :, cols], preferred_element_type=F32)
        return 0

    lax.fori_loop(0, count, mix, 0)
    for n in range(len(pairs)):
        out[:, n * HD : (n + 1) * HD] = tops[n].astype(BF)


def attend(meta, chunk, q_own, q_other, seg_row, pieces):
    n = q_own.shape[2]
    heads = n // HD
    whole = lambda a: pl.BlockSpec(a.shape, lambda t, m, nd=a.ndim: (0,) * nd)
    q_spec = pl.BlockSpec((1, RB, n), lambda t, m: (m[SLOT + 2 * chunk + t], 0, 0))
    once = lambda a: pl.BlockSpec(
        a.shape, lambda t, m, nd=a.ndim: (0,) * nd, pipeline_mode=pl.Buffered(1)
    )
    return pl.pallas_call(
        functools.partial(attend_kernel, chunk),
        grid_spec=pltpu.PrefetchScalarGridSpec(
            num_scalar_prefetch=1,
            grid=(2,),
            in_specs=[q_spec, q_spec, whole(seg_row)] + list(map(once, pieces)),
            out_specs=pl.BlockSpec((RB, 2 * n), lambda t, m: (t, 0)),
            scratch_shapes=[
                pltpu.VMEM((2, 4, 2, RB, 2 * n), BF),
                pltpu.VMEM((2 * heads, 5, RB, RB), F32),
                pltpu.VMEM((2 * heads, RB, HD), F32),
                pltpu.VMEM((2 * heads, RB, HD), F32),
            ],
        ),
        out_shape=jax.ShapeDtypeStruct((2 * RB, 2 * n), BF),
        compiler_params=pltpu.CompilerParams(vmem_limit_bytes=32 * MIB),
        cost_estimate=pl.CostEstimate(
            flops=4 * 2 * RB * 768 * 2 * n, bytes_accessed=8 * MIB, transcendentals=2 * RB * 768 * 6
        ),
    )(meta, q_own, q_other, seg_row, *pieces)


def reorder_kernel(meta, w, out):
    out[...] = w[...]


def reorder(meta, w, swap):
    k8, n, width = w.shape
    return pl.pallas_call(
        reorder_kernel,
        grid_spec=pltpu.PrefetchScalarGridSpec(
            num_scalar_prefetch=1,
            grid=(k8,),
            in_specs=[
                pl.BlockSpec((1, n, width), lambda k, m: (m[ROWS + (k + swap - 2 * swap * (k % 2))], 0, 0))
            ],
            out_specs=pl.BlockSpec((1, n, width), lambda k, m: (k, 0, 0)),
        ),
        out_shape=jax.ShapeDtypeStruct(w.shape, BF),
        compiler_params=pltpu.CompilerParams(vmem_limit_bytes=4 * MIB),
    )(meta, w).reshape(k8 * n, width)


def finish_kernel(meta, c0, c1, c2a, c2b, c3, w, res, *refs):
    out = refs[-1]
    t = pl.program_id(0)
    far = jnp.where(t == 0, c2a[:RB, :], jnp.concatenate([c2a[RB:, :], c2b[...]], axis=0))
    n = far.shape[1]
    total = res[0].astype(F32)
    for j, c in enumerate((c0[...], c1[...], far, c3[...])):
        total += jnp.dot(c, w[j * n : (j + 1) * n, :], preferred_element_type=F32)
    out[0] = total.astype(BF)


def finish(meta, chunk, parts, w, res, blocks, prior=None):
    depth, width = w.shape
    n = depth // 4
    tile = pl.BlockSpec((RB, n), lambda t, m: (t, 0))
    fixed = lambda a: pl.BlockSpec(a.shape, lambda t, m: (0, 0))
    ins = list(parts) + [w, res]
    specs = [tile, tile, fixed(parts[2]), fixed(parts[3]), tile]
    specs.append(pl.BlockSpec(w.shape, lambda t, m: (0, 0), pipeline_mode=pl.Buffered(1)))
    specs.append(pl.BlockSpec((1, RB, width), lambda t, m: (m[SLOT + 2 * chunk + t], 0, 0)))
    aliases = {}
    if prior is not None:
        aliases[1 + len(ins)] = 0
        ins.append(prior)
        specs.append(pl.BlockSpec(memory_space=pl.ANY))
    if blocks == 2:
        target = lambda t, m: (t, 0, 0)
    else:
        target = lambda t, m: (m[MINE + 2 * chunk + t], 0, 0)
    return pl.pallas_call(
        finish_kernel,
        grid_spec=pltpu.PrefetchScalarGridSpec(
            num_scalar_prefetch=1,
            grid=(2,),
            in_specs=specs,
            out_specs=pl.BlockSpec((1, RB, width), target),
        ),
        out_shape=jax.ShapeDtypeStruct((blocks, RB, width), BF),
        input_output_aliases=aliases,
        compiler_params=pltpu.CompilerParams(vmem_limit_bytes=20 * MIB),
        cost_estimate=pl.CostEstimate(
            flops=4 * RB * depth * width, bytes_accessed=8 * MIB, transcendentals=0
        ),
    )(meta, *ins)


def place_kernel(chunk, meta, got, prior, out, sems):
    copies = [
        pltpu.make_async_copy(got.at[t], out.at[meta[THEIRS + 2 * chunk + t]], sems.at[t])
        for t in range(2)
    ]
    for copy in copies:
        copy.start()
    for copy in copies:
        copy.wait()


def place(meta, chunk, got, prior):
    in_place = pl.BlockSpec(memory_space=pl.ANY)
    return pl.pallas_call(
        functools.partial(place_kernel, chunk),
        grid_spec=pltpu.PrefetchScalarGridSpec(
            num_scalar_prefetch=1,
            grid=(1,),
            in_specs=[pl.BlockSpec(got.shape, lambda t, m: (0, 0, 0)), in_place],
            out_specs=in_place,
            scratch_shapes=[pltpu.SemaphoreType.DMA((2,))],
        ),
        out_shape=jax.ShapeDtypeStruct(prior.shape, BF),
        input_output_aliases={2: 0},
        compiler_params=pltpu.CompilerParams(vmem_limit_bytes=4 * MIB),
    )(meta, got, prior)


def after(value, *done):
    return lax.optimization_barrier((value,) + done)[0]


def body(
    section_input, last_hidden, kv_gain, query_gain, w_key, w_value, w_query, w_out, segment_ids
):
    section = lax.axis_index("section")
    c = lax.axis_index("ctx")
    core = section % 2
    y_hi = section // 8
    x0 = section_input[0]
    w_q = w_query[0]
    w_o = w_out[0]
    width = w_o.shape[1]

    x_in = send(x0, IN)
    x_out = send(x0, OUT)

    meta = jnp.array(FACTS, jnp.int32)[section, c]
    seg_row = segment_ids.reshape(8, 1, RB)

    def cache(last_hidden, w_key, w_value, w_out):
        kv_in = normalize(last_hidden, kv_gain)
        own_k = jnp.dot(kv_in, w_key, preferred_element_type=F32).astype(BF)
        own_v = jnp.dot(kv_in, w_value, preferred_element_type=F32).astype(BF)
        kv = jnp.concatenate([own_k, own_v], axis=1)
        kv2 = send(kv, CORE)
        pair = jnp.where(core == 0, jnp.stack([kv, kv2]), jnp.stack([kv2, kv]))
        far = send(pair, FAR_Y)
        far, w_mine = lax.optimization_barrier((far, reorder(meta, w_out, 0)))
        far = jnp.where(core == 0, far, send(far, CORE))
        piece = jnp.where(y_hi == 0, jnp.stack([pair, far]), jnp.stack([far, pair]))
        piece = piece.reshape(2, 2 * kv.shape[0], kv.shape[1])
        piece2 = send(piece, PARTNER)
        share = lax.dynamic_index_in_dim(piece, core, 0, keepdims=False)
        o2 = send(share, X_FAR)
        return piece, share, o2, piece2, w_mine, reorder(meta, w_out, 1)

    def nothing(last_hidden, w_key, w_value, w_out):
        two = jnp.zeros((2, 2 * last_hidden.shape[0], 2 * w_key.shape[1]), BF)
        w_none = jnp.zeros((w_out.shape[0] * w_out.shape[1], w_out.shape[2]), BF)
        return two, two[0], two[0], two, w_none, w_none

    w_o_r = w_o.reshape(8, w_q.shape[1], width)
    piece, share, o2, piece2, w_o_mine, w_o_theirs = lax.cond(
        section >= 0, cache, nothing, last_hidden, w_key, w_value, w_o_r
    )
    w_q2 = send(after(w_q, piece2), PARTNER)
    o1 = send(share, X_PREV)
    o3 = send(share, X_NEXT)
    x_in, x_out, piece2, share, o1, o3 = lax.optimization_barrier(
        (x_in, x_out, piece2, share, o1, o3)
    )
    most = RB * 5 // 8
    xo_a = send(x_out[:most], IN)
    xo_b = send(x_in[most:], OUT)
    t1 = send(piece2, X_PREV)
    t3 = send(piece2, X_NEXT)
    state = project(meta, [after(x0, x_in, x_out)], query_gain, w_q, 0, width)
    state = project(meta, [x_in], query_gain, w_q, 1, width, state)
    state = project(meta, [x_out], query_gain, w_q, 3, width, state)
    t1, t3, piece2, *state = lax.optimization_barrier((t1, t3, piece2, *state))
    t2 = send(piece2, X_FAR)
    o1, o2, o3, t1 = lax.optimization_barrier((o1, o2, o3, t1))
    o1b = send(o1, CORE)
    o2b = send(o2, CORE)
    o3b = send(o3, CORE)
    xo_a, xo_b, o1b, o2b, o3b = lax.optimization_barrier((xo_a, xo_b, o1b, o2b, o3b))
    normed, q_own, res_own, res_other = project(
        meta, [xo_a, xo_b], query_gain, w_q, 2, width, state
    )
    t2, w_q2, w_o_theirs, normed, q_own = lax.optimization_barrier(
        (t2, w_q2, w_o_theirs, normed, q_own)
    )
    w_o2 = send(w_o_theirs, PARTNER)
    q_other = more_queries(normed, w_q2)
    pieces = (piece, o1, o1b, o2, o2b, o3, o3b, piece2, t1, t2, t3)

    result = None
    parts = []
    for chunk in range(2):
        own = attend(meta, chunk, q_own, q_other, seg_row, pieces)
        c_in = send(own, IN)
        c_out = send(own, OUT)
        if parts:
            ours, c_in_0, co_a_0, co_b_0, c_out_0 = parts[0]
            c_in, c_out, co_b_0 = lax.optimization_barrier((c_in, c_out, co_b_0))
            parts[0] = (ours, c_in_0, co_a_0, co_b_0, c_out_0)
        else:
            c_in, c_out = lax.optimization_barrier((c_in, c_out))
        co_a = send(c_out[:CUT], IN)
        co_b = send(c_in[CUT:], OUT)
        parts.append((own, c_in, co_a, co_b, c_out))
    others = [finish(meta, chunk, parts[chunk], w_o2, res_other, 2) for chunk in range(2)]
    sent = [send(other, PARTNER) for other in others]
    w_o_mine = after(w_o_mine, *others)
    result = None
    for chunk in range(2):
        result = finish(meta, chunk, parts[chunk], w_o_mine, res_own, 8, result)
    for chunk in range(2):
        result = place(meta, chunk, sent[chunk], result)
    return result.reshape(1, 8 * RB, -1)


def solution(mesh):
    return jax.shard_map(
        body,
        mesh=mesh,
        in_specs=(
            P("section", "ctx", None),
            P("section", None),
            P(),
            P("section", None),
            P(None, "ctx"),
            P(None, "ctx"),
            P("section", None, "ctx"),
            P("section", None, "ctx"),
            P(),
        ),
        out_specs=P("section", None, "ctx"),
        check_vma=False,
    )
```

```python
import functools

import jax
import jax.numpy as jnp
from jax import lax
from jax.experimental import pallas as pl
from jax.experimental.pallas import tpu as pltpu
from jax.sharding import PartitionSpec as P

HD = 128
RB = 256
CUT = 320
BF = jnp.bfloat16
F32 = jnp.float32
AXES = ("section", "ctx")
MIB = 1 << 20

PLACE = (((0, 1, 2, 3), (4, 5, 6, 7)), ((1, 0, 4, 5), (2, 3, 7, 6)))
SPOT = tuple(
    tuple(next((h, r) for h in range(2) for r in range(4) if table[h][r] == c) for c in range(8))
    for table in PLACE
)

MINE, THEIRS, SLOT, ROWS, OWN, CORE_AT, X_AT = 0, 4, 8, 12, 20, 22, 23


def facts_of(section, c):
    core = section % 2
    half, r = SPOT[core][c]
    mine, theirs = PLACE[core][half], PLACE[core][1 - half]
    ring = [r, r ^ 1, (r + 2) % 4, 3 - r]
    slots = [ring.index(p) for p in range(4)]
    rows = [place[p] for p in ring for place in (mine, theirs)]
    return [*mine, *theirs, *slots, *rows, mine[r], theirs[r], core, section // 2 % 4]


FACTS = [[facts_of(section, c) for c in range(8)] for section in range(16)]


def moves(step):
    pairs = []
    for s in range(16):
        for c in range(8):
            core = s % 2
            half, spot = SPOT[core][c]
            yh, x, k, h, r = step(s // 8, s // 2 % 4, core, half, spot)
            if k == core:
                place = PLACE[core][h][r % 4]
            else:
                place = c
            pairs.append((s * 8 + c, (yh * 8 + x % 4 * 2 + k) * 8 + place))
    return pairs


IN = moves(lambda yh, x, k, h, r: (yh, x, k, h, r ^ 1))
OUT = moves(lambda yh, x, k, h, r: (yh, x, k, h, 3 - r))
PARTNER = moves(lambda yh, x, k, h, r: (yh, x, k, 1 - h, r))
CORE = moves(lambda yh, x, k, h, r: (yh, x, 1 - k, h, r))
FAR_Y = [
    (a, b) for a, b in moves(lambda yh, x, k, h, r: (1 - yh, x, k, h, r)) if a // 8 % 2 == 0
]
X_NEXT = moves(lambda yh, x, k, h, r: (yh, x + 1, k, h, r))
X_PREV = moves(lambda yh, x, k, h, r: (yh, x - 1, k, h, r))
X_FAR = moves(lambda yh, x, k, h, r: (yh, x + 2, k, h, r))


def send(value, pairs):
    return lax.ppermute(value, AXES, pairs)


def normalize(rows, gain):
    full = rows.astype(F32)
    scaled = full * lax.rsqrt(jnp.mean(full * full, axis=-1, keepdims=True) + 1e-05) * gain
    return scaled.astype(BF)


def project_kernel(pieces, meta, *refs):
    xs = refs[:pieces]
    gain, w = refs[pieces : pieces + 2]
    normed, q, res_own, res_other = refs[-4:]
    step = 32
    base = 0
    for x in xs:
        rows = x.shape[0]

        def norm_rows(i, _, x=x, base=base):
            at = pl.multiple_of(i * step, step)
            full = x[pl.ds(at, step), :].astype(F32)
            mean = jnp.mean(full * full, axis=-1, keepdims=True)
            normed[0, pl.ds(base + at, step), :] = (
                full * lax.rsqrt(mean + 1e-05) * gain[...]
            ).astype(BF)
            return 0

        lax.fori_loop(0, rows // step, norm_rows, 0)
        width = res_own.shape[2]
        for k, out in ((0, res_own), (1, res_other)):
            first = pl.multiple_of(meta[OWN + k] * width, 128)
            out[0, base : base + rows, :] = x[:, pl.ds(first, width)]
        base += rows
    q[0] = jnp.dot(normed[0], w[...], preferred_element_type=F32).astype(BF)


def project(meta, xs, gain, w, slot, width, prior=None):
    d, n = w.shape
    shapes = [(4, RB, d), (4, RB, n), (4, RB, width), (4, RB, width)]
    whole = lambda a: pl.BlockSpec(
        a.shape, lambda i, m, nd=a.ndim: (0,) * nd, pipeline_mode=pl.Buffered(1)
    )
    ins = list(xs) + [gain, w]
    specs = [whole(a) for a in ins]
    aliases = {}
    for k, a in enumerate(prior or ()):
        aliases[1 + len(ins)] = k
        ins.append(a)
        specs.append(pl.BlockSpec(memory_space=pl.ANY))

    def kernel(meta, *refs):
        project_kernel(len(xs), meta, *refs)

    return pl.pallas_call(
        kernel,
        grid_spec=pltpu.PrefetchScalarGridSpec(
            num_scalar_prefetch=1,
            grid=(1,),
            in_specs=specs,
            out_specs=[pl.BlockSpec((1,) + s[1:], lambda i, m: (slot, 0, 0)) for s in shapes],
        ),
        out_shape=[jax.ShapeDtypeStruct(s, BF) for s in shapes],
        input_output_aliases=aliases,
        compiler_params=pltpu.CompilerParams(vmem_limit_bytes=20 * MIB),
        cost_estimate=pl.CostEstimate(
            flops=0, bytes_accessed=0, transcendentals=0
        ),
    )(meta, *ins)


def more_queries_kernel(n_ref, w_ref, q_ref):
    q_ref[...] = jnp.dot(n_ref[...], w_ref[...], preferred_element_type=F32).astype(BF)


def more_queries(normed, w):
    d, n = w.shape
    rows = 2 * RB
    return pl.pallas_call(
        more_queries_kernel,
        grid=(2,),
        in_specs=[
            pl.BlockSpec((rows, d), lambda i: (i, 0)),
            pl.BlockSpec(w.shape, lambda i: (0, 0), pipeline_mode=pl.Buffered(1)),
        ],
        out_specs=pl.BlockSpec((rows, n), lambda i: (i, 0)),
        out_shape=jax.ShapeDtypeStruct((4 * RB, n), BF),
        compiler_params=pltpu.CompilerParams(vmem_limit_bytes=20 * MIB),
        cost_estimate=pl.CostEstimate(
            flops=0, bytes_accessed=0, transcendentals=0
        ),
    )(normed.reshape(4 * RB, d), w).reshape(4, RB, n)


def attend_kernel(
    chunk, meta, q_own, q_other, seg_row, own0, o1, o1b, o2, o2b, o3, o3b,
    other0, t1, t2, t3,
    out, kv, scores, tops, sums,
):
    t = pl.program_id(0)
    core = meta[CORE_AT]

    @pl.when(t == 0)
    def _():
        kv[0, 0] = own0[...]
        kv[0, 1, core] = o1[...]
        kv[0, 1, 1 - core] = o1b[...]
        kv[0, 2, core] = o2[...]
        kv[0, 2, 1 - core] = o2b[...]
        kv[0, 3, core] = o3[...]
        kv[0, 3, 1 - core] = o3b[...]
        kv[1, 0] = other0[...]
        kv[1, 1] = t1[...]
        kv[1, 2] = t2[...]
        kv[1, 3] = t3[...]

    block = meta[MINE + 2 * chunk + t]
    earlier = (seg_row[...] < seg_row[block, :, :1]).astype(F32)
    first = jnp.maximum(jnp.sum(earlier).astype(jnp.int32) // RB, block - 4)
    count = block - first + 1
    x = meta[X_AT]
    heads = q_own.shape[2] // HD
    factor = HD ** (-0.5) * 1.4426950408889634
    pairs = [(src, i) for src in range(2) for i in range(heads)]
    qs = (q_own, q_other)

    def place(i):
        kb = first + i
        j = lax.rem(lax.rem(kb, 4) - x + 4, 4)
        return kb, j, kb // 4

    tops[...] = jnp.full(tops.shape, -1e30, F32)
    sums[...] = jnp.zeros(sums.shape, F32)
    q_doc = jnp.transpose(jnp.broadcast_to(seg_row[block], (RB, RB)))
    row_at = block * RB + lax.broadcasted_iota(jnp.int32, (RB, RB), 0)
    col_at = lax.broadcasted_iota(jnp.int32, (RB, RB), 1)

    def score(i, _):
        kb, j, y = place(i)
        visible = (q_doc == seg_row[kb]) & (kb * RB + col_at <= row_at)
        for n, (src, h) in enumerate(pairs):
            cols = slice(h * HD, (h + 1) * HD)
            s = lax.dot_general(
                qs[src][0, :, cols], kv[src, j, y, :, cols], (((1,), (1,)), ((), ())),
                preferred_element_type=F32,
            )
            s = jnp.where(visible, s, -1e30)
            scores[n, i] = s
            tops[n] = jnp.maximum(tops[n], jnp.maximum(s[:, :HD], s[:, HD:]))
        return 0

    lax.fori_loop(0, count, score, 0)
    for n in range(len(pairs)):
        tops[n] = jnp.broadcast_to(jnp.max(tops[n], axis=-1, keepdims=True), (RB, HD))

    def expo(i, _):
        for n in range(len(pairs)):
            s = scores[n, i]
            top = tops[n]
            left = jnp.exp2((s[:, :HD] - top) * factor)
            right = jnp.exp2((s[:, HD:] - top) * factor)
            scores[n, i, :, :HD] = left
            scores[n, i, :, HD:] = right
            sums[n] += left + right
        return 0

    lax.fori_loop(0, count, expo, 0)
    for n in range(len(pairs)):
        total = jnp.sum(sums[n], axis=-1, keepdims=True)
        sums[n] = jnp.broadcast_to(1.0 / total, (RB, HD))
        tops[n] = jnp.zeros((RB, HD), F32)

    def mix(i, _):
        kb, j, y = place(i)
        for n, (src, h) in enumerate(pairs):
            cols = slice((heads + h) * HD, (heads + h + 1) * HD)
            e = scores[n, i]
            inv = sums[n]
            weights = jnp.concatenate([e[:, :HD] * inv, e[:, HD:] * inv], axis=1).astype(BF)
            tops[n] += jnp.dot(weights, kv[src, j, y, :, cols], preferred_element_type=F32)
        return 0

    lax.fori_loop(0, count, mix, 0)
    for n in range(len(pairs)):
        out[:, n * HD : (n + 1) * HD] = tops[n].astype(BF)


def attend(meta, chunk, q_own, q_other, seg_row, pieces):
    n = q_own.shape[2]
    heads = n // HD
    whole = lambda a: pl.BlockSpec(a.shape, lambda t, m, nd=a.ndim: (0,) * nd)
    q_spec = pl.BlockSpec((1, RB, n), lambda t, m: (m[SLOT + 2 * chunk + t], 0, 0))
    once = lambda a: pl.BlockSpec(
        a.shape, lambda t, m, nd=a.ndim: (0,) * nd, pipeline_mode=pl.Buffered(1)
    )
    return pl.pallas_call(
        functools.partial(attend_kernel, chunk),
        grid_spec=pltpu.PrefetchScalarGridSpec(
            num_scalar_prefetch=1,
            grid=(2,),
            in_specs=[q_spec, q_spec, whole(seg_row)] + list(map(once, pieces)),
            out_specs=pl.BlockSpec((RB, 2 * n), lambda t, m: (t, 0)),
            scratch_shapes=[
                pltpu.VMEM((2, 4, 2, RB, 2 * n), BF),
                pltpu.VMEM((2 * heads, 5, RB, RB), F32),
                pltpu.VMEM((2 * heads, RB, HD), F32),
                pltpu.VMEM((2 * heads, RB, HD), F32),
            ],
        ),
        out_shape=jax.ShapeDtypeStruct((2 * RB, 2 * n), BF),
        compiler_params=pltpu.CompilerParams(vmem_limit_bytes=32 * MIB),
        cost_estimate=pl.CostEstimate(
            flops=4 * 2 * RB * 768 * 2 * n, bytes_accessed=8 * MIB, transcendentals=2 * RB * 768 * 6
        ),
    )(meta, q_own, q_other, seg_row, *pieces)


def reorder_kernel(meta, w, out):
    out[...] = w[...]


def reorder(meta, w, swap):
    k8, n, width = w.shape
    return pl.pallas_call(
        reorder_kernel,
        grid_spec=pltpu.PrefetchScalarGridSpec(
            num_scalar_prefetch=1,
            grid=(k8,),
            in_specs=[
                pl.BlockSpec((1, n, width), lambda k, m: (m[ROWS + (k + swap - 2 * swap * (k % 2))], 0, 0))
            ],
            out_specs=pl.BlockSpec((1, n, width), lambda k, m: (k, 0, 0)),
        ),
        out_shape=jax.ShapeDtypeStruct(w.shape, BF),
        compiler_params=pltpu.CompilerParams(vmem_limit_bytes=4 * MIB),
    )(meta, w).reshape(k8 * n, width)


def finish_kernel(meta, c0, c1, c2a, c2b, c3, w, res, *refs):
    out = refs[-1]
    t = pl.program_id(0)
    far = jnp.where(t == 0, c2a[:RB, :], jnp.concatenate([c2a[RB:, :], c2b[...]], axis=0))
    n = far.shape[1]
    total = res[0].astype(F32)
    for j, c in enumerate((c0[...], c1[...], far, c3[...])):
        total += jnp.dot(c, w[j * n : (j + 1) * n, :], preferred_element_type=F32)
    out[0] = total.astype(BF)


def finish(meta, chunk, parts, w, res, blocks, prior=None):
    depth, width = w.shape
    n = depth // 4
    tile = pl.BlockSpec((RB, n), lambda t, m: (t, 0))
    fixed = lambda a: pl.BlockSpec(a.shape, lambda t, m: (0, 0))
    ins = list(parts) + [w, res]
    specs = [tile, tile, fixed(parts[2]), fixed(parts[3]), tile]
    specs.append(pl.BlockSpec(w.shape, lambda t, m: (0, 0), pipeline_mode=pl.Buffered(1)))
    specs.append(pl.BlockSpec((1, RB, width), lambda t, m: (m[SLOT + 2 * chunk + t], 0, 0)))
    aliases = {}
    if prior is not None:
        aliases[1 + len(ins)] = 0
        ins.append(prior)
        specs.append(pl.BlockSpec(memory_space=pl.ANY))
    if blocks == 2:
        target = lambda t, m: (t, 0, 0)
    else:
        target = lambda t, m: (m[MINE + 2 * chunk + t], 0, 0)
    return pl.pallas_call(
        finish_kernel,
        grid_spec=pltpu.PrefetchScalarGridSpec(
            num_scalar_prefetch=1,
            grid=(2,),
            in_specs=specs,
            out_specs=pl.BlockSpec((1, RB, width), target),
        ),
        out_shape=jax.ShapeDtypeStruct((blocks, RB, width), BF),
        input_output_aliases=aliases,
        compiler_params=pltpu.CompilerParams(vmem_limit_bytes=20 * MIB),
        cost_estimate=pl.CostEstimate(
            flops=4 * RB * depth * width, bytes_accessed=8 * MIB, transcendentals=0
        ),
    )(meta, *ins)


def place_kernel(chunk, meta, got, prior, out, sems):
    copies = [
        pltpu.make_async_copy(got.at[t], out.at[meta[THEIRS + 2 * chunk + t]], sems.at[t])
        for t in range(2)
    ]
    for copy in copies:
        copy.start()
    for copy in copies:
        copy.wait()


def place(meta, chunk, got, prior):
    in_place = pl.BlockSpec(memory_space=pl.ANY)
    return pl.pallas_call(
        functools.partial(place_kernel, chunk),
        grid_spec=pltpu.PrefetchScalarGridSpec(
            num_scalar_prefetch=1,
            grid=(1,),
            in_specs=[pl.BlockSpec(got.shape, lambda t, m: (0, 0, 0)), in_place],
            out_specs=in_place,
            scratch_shapes=[pltpu.SemaphoreType.DMA((2,))],
        ),
        out_shape=jax.ShapeDtypeStruct(prior.shape, BF),
        input_output_aliases={2: 0},
        compiler_params=pltpu.CompilerParams(vmem_limit_bytes=4 * MIB),
    )(meta, got, prior)


def after(value, *done):
    return lax.optimization_barrier((value,) + done)[0]


def body(
    section_input, last_hidden, kv_gain, query_gain, w_key, w_value, w_query, w_out, segment_ids
):
    section = lax.axis_index("section")
    c = lax.axis_index("ctx")
    core = section % 2
    y_hi = section // 8
    x0 = section_input[0]
    w_q = w_query[0]
    w_o = w_out[0]
    width = w_o.shape[1]

    x_in = send(x0, IN)
    x_out = send(x0, OUT)

    meta = jnp.array(FACTS, jnp.int32)[section, c]
    seg_row = segment_ids.reshape(8, 1, RB)

    def cache(last_hidden, w_key, w_value, w_out):
        kv_in = normalize(last_hidden, kv_gain)
        own_k = jnp.dot(kv_in, w_key, preferred_element_type=F32).astype(BF)
        own_v = jnp.dot(kv_in, w_value, preferred_element_type=F32).astype(BF)
        kv = jnp.concatenate([own_k, own_v], axis=1)
        kv2 = send(kv, CORE)
        pair = jnp.where(core == 0, jnp.stack([kv, kv2]), jnp.stack([kv2, kv]))
        far = send(pair, FAR_Y)
        far, w_mine = lax.optimization_barrier((far, reorder(meta, w_out, 0)))
        far = jnp.where(core == 0, far, send(far, CORE))
        piece = jnp.where(y_hi == 0, jnp.stack([pair, far]), jnp.stack([far, pair]))
        piece = piece.reshape(2, 2 * kv.shape[0], kv.shape[1])
        piece2 = send(piece, PARTNER)
        share = lax.dynamic_index_in_dim(piece, core, 0, keepdims=False)
        o2 = send(share, X_FAR)
        return piece, share, o2, piece2, w_mine, reorder(meta, w_out, 1)

    def nothing(last_hidden, w_key, w_value, w_out):
        two = jnp.zeros((2, 2 * last_hidden.shape[0], 2 * w_key.shape[1]), BF)
        w_none = jnp.zeros((w_out.shape[0] * w_out.shape[1], w_out.shape[2]), BF)
        return two, two[0], two[0], two, w_none, w_none

    w_o_r = w_o.reshape(8, w_q.shape[1], width)
    piece, share, o2, piece2, w_o_mine, w_o_theirs = lax.cond(
        section >= 0, cache, nothing, last_hidden, w_key, w_value, w_o_r
    )
    w_q2 = send(after(w_q, piece2), PARTNER)
    o1 = send(share, X_PREV)
    o3 = send(share, X_NEXT)
    x_in, x_out, piece2, share, o1, o3 = lax.optimization_barrier(
        (x_in, x_out, piece2, share, o1, o3)
    )
    most = RB * 5 // 8
    xo_a = send(x_out[:most], IN)
    xo_b = send(x_in[most:], OUT)
    t1 = send(piece2, X_PREV)
    t3 = send(piece2, X_NEXT)
    state = project(meta, [after(x0, x_in, x_out)], query_gain, w_q, 0, width)
    state = project(meta, [x_in], query_gain, w_q, 1, width, state)
    t1, t3, piece2, *state = lax.optimization_barrier((t1, t3, piece2, *state))
    t2 = send(piece2, X_FAR)
    state = project(meta, [x_out], query_gain, w_q, 3, width, state)
    o1, o2, o3, t1 = lax.optimization_barrier((o1, o2, o3, t1))
    o1b = send(o1, CORE)
    o2b = send(o2, CORE)
    o3b = send(o3, CORE)
    xo_a, xo_b, o1b, o2b, o3b = lax.optimization_barrier((xo_a, xo_b, o1b, o2b, o3b))
    normed, q_own, res_own, res_other = project(
        meta, [xo_a, xo_b], query_gain, w_q, 2, width, state
    )
    t2, w_q2, w_o_theirs, normed, q_own = lax.optimization_barrier(
        (t2, w_q2, w_o_theirs, normed, q_own)
    )
    w_o2 = send(w_o_theirs, PARTNER)
    q_other = more_queries(normed, w_q2)
    pieces = (piece, o1, o1b, o2, o2b, o3, o3b, piece2, t1, t2, t3)

    result = None
    parts = []
    for chunk in range(2):
        own = attend(meta, chunk, q_own, q_other, seg_row, pieces)
        c_in = send(own, IN)
        c_out = send(own, OUT)
        if parts:
            ours, c_in_0, co_a_0, co_b_0, c_out_0 = parts[0]
            c_in, c_out, co_b_0 = lax.optimization_barrier((c_in, c_out, co_b_0))
            parts[0] = (ours, c_in_0, co_a_0, co_b_0, c_out_0)
        else:
            c_in, c_out = lax.optimization_barrier((c_in, c_out))
        co_a = send(c_out[:CUT], IN)
        co_b = send(c_in[CUT:], OUT)
        parts.append((own, c_in, co_a, co_b, c_out))
    others = [finish(meta, chunk, parts[chunk], w_o2, res_other, 2) for chunk in range(2)]
    sent = [send(other, PARTNER) for other in others]
    w_o_mine = after(w_o_mine, *others)
    result = None
    for chunk in range(2):
        result = finish(meta, chunk, parts[chunk], w_o_mine, res_own, 8, result)
    for chunk in range(2):
        result = place(meta, chunk, sent[chunk], result)
    return result.reshape(1, 8 * RB, -1)


def solution(mesh):
    return jax.shard_map(
        body,
        mesh=mesh,
        in_specs=(
            P("section", "ctx", None),
            P("section", None),
            P(),
            P("section", None),
            P(None, "ctx"),
            P(None, "ctx"),
            P("section", None, "ctx"),
            P("section", None, "ctx"),
            P(),
        ),
        out_specs=P("section", None, "ctx"),
        check_vma=False,
    )
```
